256 devices in a mesh: ctx: 32 (over x, z_lo, core), tp: 8 (over z_hi, y).
Axes of the slice: x: 4, y: 4, z: 8 (z_hi: 2, z_lo: 4; z = z_hi * 4 + z_lo), core: 2. Of those that a mesh axis runs over, the one named last changes fastest.
Arguments:
- queries: bfloat16 [4096, 4096], P('ctx', 'tp'), may hold values from -256 to 256
- keys: bfloat16 [4096, 1024], P('ctx', 'tp'), may hold values from -4 to 4
- values: bfloat16 [4096, 1024], P('ctx', 'tp'), may hold values from -6 to 6
- stretch_of: int32 [64], replicated, may hold values from 0 to 63, as said below
- out_weight: bfloat16 [4096, 8192], P('tp'), may hold values from -0.09375 to 0.09375
- grad_heads: bfloat16 [4096, 4096], P('ctx', 'tp'), may hold values from -6 to 6
Outputs:
- mixed: bfloat16 [4096, 8192], P(('ctx', 'tp'))
- q_grad: bfloat16 [4096, 4096], P('ctx', 'tp')
- k_grad: bfloat16 [4096, 1024], P('ctx', 'tp')
- v_grad: bfloat16 [4096, 1024], P('ctx', 'tp')
The draws below stay inside these ranges and needn't reach their ends.
Inputs may be any that keep to these rules, and one draw needn't show every extreme that they name: `stretch_of`: a permutation of the 64 stretch numbers; the two slots of index i of ctx, slots 2 * i and 2 * i + 1, hold stretches j and 63 - j in either order.
All inputs are finite; a program needn't handle non-finite values.
Results may differ from the reference program's by a relative error of at most 0.039.
Values may be sent and summed in bfloat16 or wider, within the bound.
No kernel may reach another device: no remote copies, remote signals or barrier semaphores. Data moves between devices by JAX's collectives and lax.ppermute only.
A program may use at most 64 MiB of HBM per device.

```python
import jax
import jax.numpy as jnp
from jax import lax

D = 8192
HD = 128
KV = 8
QPG = 4
TOK_DEV = 128
TOKENS = 4096
HEADS = 32
N_CTX = 32
N_TP = 8


def base_keys(key):
    raw = jax.random.normal(key, (TOK_DEV * N_CTX, KV * HD), jnp.float32)
    return jnp.clip(raw, -4.0, 4.0)


def draw_keys(key, part):
    base = base_keys(key)
    return base.astype(jnp.bfloat16)


def draw_queries(key, part):
    base = base_keys(key)
    key = jax.random.fold_in(key, 3)
    count = base.shape[0]
    return jax.random.normal(key, (count, KV * QPG * HD), jnp.float32).astype(jnp.bfloat16)


def draw_stretch_of(key, part):
    key = jax.random.fold_in(key, 5)
    first_key, second_key = jax.random.split(key)
    pairs = jax.random.permutation(first_key, N_CTX).astype(jnp.int32)
    flips = jax.random.randint(second_key, (N_CTX,), 0, 2)
    lower = jnp.where(flips == 1, 2 * N_CTX - 1 - pairs, pairs)
    upper = 2 * N_CTX - 1 - lower
    return jnp.stack([lower, upper], axis=1).reshape(2 * N_CTX).astype(jnp.int32)


def level_of(own_key, extent, cuts, least, top_value):
    loudness, own = 1.0, jax.random.fold_in(own_key, 6)
    for dim, blocks in cuts:
        heights = jnp.exp(jax.random.uniform(jax.random.fold_in(own, dim), (blocks,), jnp.float32, least / len(cuts), top_value / len(cuts)))
        loudness = loudness * jnp.repeat(heights, extent[dim] // blocks).reshape([-1 if axis == dim else 1 for axis in range(len(extent))])
    return loudness


def bell_draw(key, shape, scale, reach, cuts=(), kind=jnp.bfloat16):
    values = jax.random.normal(key, shape, jnp.float32) * scale
    if len(cuts) > 0:
        values = level_of(key, shape, cuts, -0.22, 0.18) * values
    return jnp.clip(values, min=-reach, max=reach).astype(kind)


def setup_inputs(seed: int = 0) -> dict:
    key_of = jax.random.split(jax.random.key(seed), 7)
    return {
        "queries": draw_queries(jax.random.fold_in(key_of[6], 71), 0),
        "keys": draw_keys(jax.random.fold_in(key_of[6], 71), 0),
        "values": bell_draw(key_of[2], (TOKENS, KV * HD), 1.0, 6.0, ((0, 32), (1, 8))),
        "stretch_of": draw_stretch_of(jax.random.fold_in(key_of[6], 71), 0),
        "out_weight": bell_draw(key_of[4], (HEADS * HD, D), (HEADS * HD) ** -0.5, 0.09375, ((0, 8),)),
        "grad_heads": bell_draw(key_of[5], (TOKENS, HEADS * HD), 1.0, 6.0, ((0, 32), (1, 8))),
    }


def reference(queries, keys, values, stretch_of, out_weight, grad_heads):
    stretch = TOK_DEV // 2
    total = TOK_DEV * N_CTX
    rows = jnp.arange(total, dtype=jnp.int32)
    position = jnp.take(stretch_of.astype(jnp.int32), rows // stretch) * stretch + rows % stretch
    scale = HD ** -0.5

    def per_head(head):
        group = head // QPG
        q_cols = lax.dynamic_slice_in_dim(queries, (head * HD).astype(jnp.int32), HD, 1)
        do_cols = lax.dynamic_slice_in_dim(grad_heads, (head * HD).astype(jnp.int32), HD, 1)
        k_cols = lax.dynamic_slice_in_dim(keys, (group * HD).astype(jnp.int32), HD, 1)
        v_cols = lax.dynamic_slice_in_dim(values, (group * HD).astype(jnp.int32), HD, 1)
        visible = position[None, :] <= position[:, None]
        scores = jnp.dot(q_cols, k_cols.T, preferred_element_type=jnp.float32) * scale
        scores = jnp.where(visible, scores, -1e30)
        top = jnp.max(scores, axis=1)
        lse = top + jnp.log(jnp.sum(jnp.exp(scores - top[:, None]), axis=1))
        probs = jnp.exp(scores - lse[:, None])
        weights = probs.astype(jnp.bfloat16)
        attn = jnp.dot(weights, v_cols, preferred_element_type=jnp.float32).astype(jnp.bfloat16)
        delta = jnp.sum(do_cols.astype(jnp.float32) * attn.astype(jnp.float32), axis=1)
        dprobs = jnp.dot(do_cols, v_cols.T, preferred_element_type=jnp.float32)
        dscores = (probs * (dprobs - delta[:, None])).astype(jnp.bfloat16)
        q_grad = (jnp.dot(dscores, k_cols, preferred_element_type=jnp.float32) * scale).astype(jnp.bfloat16)
        k_part = jnp.dot(dscores.T, q_cols, preferred_element_type=jnp.float32) * scale
        v_part = jnp.dot(weights.T, do_cols, preferred_element_type=jnp.float32)
        return attn, q_grad, k_part, v_part

    attn, q_grad, k_part, v_part = lax.map(per_head, jnp.arange(HEADS, dtype=jnp.int32))
    attn = attn.transpose(1, 0, 2).reshape(total, HEADS * HD)
    q_grad = q_grad.transpose(1, 0, 2).reshape(total, HEADS * HD)
    k_grad = k_part.reshape(KV, QPG, total, HD).sum(axis=1).transpose(1, 0, 2).reshape(total, KV * HD)
    v_grad = v_part.reshape(KV, QPG, total, HD).sum(axis=1).transpose(1, 0, 2).reshape(total, KV * HD)
    width = HEADS * HD // N_TP
    attn_blocks = attn.reshape(total, N_TP, width).transpose(1, 0, 2)
    weight_blocks = out_weight.reshape(N_TP, width, D)

    def add_block(carry, pair):
        block, weight = pair
        product = jnp.dot(block, weight, preferred_element_type=jnp.float32).astype(jnp.bfloat16)
        product = lax.optimization_barrier(product)
        return carry + product.astype(jnp.float32), None

    mixed, unused = lax.scan(add_block, jnp.zeros((total, D), jnp.float32), (attn_blocks, weight_blocks))
    return mixed.astype(jnp.bfloat16), q_grad, k_grad.astype(jnp.bfloat16), v_grad.astype(jnp.bfloat16)
```

```python
import functools
import jax
import jax.numpy as jnp
from jax import lax
from jax.experimental import pallas as pl
from jax.experimental.pallas import tpu as pltpu

HD = 128
QPG = 4
NEG = -1e30
SCALE = HD ** (-0.5)
NT = (((1,), (1,)), ((), ()))
NN = (((1,), (0,)), ((), ()))
TN = (((0,), (0,)), ((), ()))


def dot(a, b, dims):
    return lax.dot_general(a, b, dims, preferred_element_type=jnp.float32)


def fwd_kernel(stretch, span, ids_ref, own_ref, q_ref, kv_ref, do_ref,
               attn_ref, p_ref, ks_ref, vs_ref, qs_ref, ds_ref, delta_ref,
               s_buf, top_ref, sum_ref, acc_ref, diff_ref):
    slots = ids_ref.shape[0]
    steps = p_ref.shape[0]
    cols = QPG * stretch
    for slot in range(slots):
        start = pl.multiple_of(ids_ref[slot] * stretch, stretch)
        ks_ref[pl.ds(start, stretch), :] = kv_ref[slot * stretch:(slot + 1) * stretch, :HD]
        vs_ref[pl.ds(start, stretch), :] = kv_ref[slot * stretch:(slot + 1) * stretch, HD:]
    for part in range(2):
        for head in range(QPG):
            rows = slice(part * stretch, (part + 1) * stretch)
            to = slice(head * stretch, (head + 1) * stretch)
            qs_ref[part, to, :] = q_ref[rows, head * HD:(head + 1) * HD]
            ds_ref[part, to, :] = do_ref[rows, head * HD:(head + 1) * HD]
    k_at = lax.broadcasted_iota(jnp.int32, (span, cols), 0)
    q_at = lax.broadcasted_iota(jnp.int32, (span, cols), 1) % stretch
    diff_ref[...] = k_at - q_at
    top_ref[...] = jnp.full_like(top_ref, NEG)
    sum_ref[...] = jnp.zeros_like(sum_ref)
    acc_ref[...] = jnp.zeros_like(acc_ref)
    first = (own_ref[0] * stretch + stretch - 1) // span + 1

    def place(step):
        part = jnp.where(step >= first, 1, 0)
        chunk = step - part * first
        return part, chunk

    def score_step(step, carry):
        part, chunk = place(step)
        start = pl.multiple_of(chunk * span, span)
        scores = dot(ks_ref[pl.ds(start, span), :], qs_ref[part], NT) * SCALE
        limit = own_ref[part] * stretch - start
        scores = jnp.where(diff_ref[...] <= limit, scores, NEG)
        s_buf[step] = scores
        top_ref[part] = jnp.maximum(top_ref[part], jnp.max(scores.reshape(span // 8, 8, cols), axis=0))
        return carry

    lax.fori_loop(0, steps, score_step, 0, unroll=UNROLL)
    for part in range(2):
        top_ref[part] = jnp.broadcast_to(jnp.max(top_ref[part], axis=0, keepdims=True), (8, cols))

    def sum_step(step, carry):
        part, chunk = place(step)
        shifted = jnp.exp(s_buf[step].reshape(span // 8, 8, cols) - top_ref[part][None])
        s_buf[step] = shifted.reshape(span, cols)
        sum_ref[part] += jnp.sum(shifted, axis=0)
        return carry

    lax.fori_loop(0, steps, sum_step, 0, unroll=UNROLL)
    for part in range(2):
        total = jnp.sum(sum_ref[part], axis=0, keepdims=True)
        sum_ref[part] = jnp.broadcast_to(1.0 / total, (8, cols))

    def value_step(step, carry):
        part, chunk = place(step)
        start = pl.multiple_of(chunk * span, span)
        weights = (s_buf[step].reshape(span // 8, 8, cols) * sum_ref[part][None]).reshape(span, cols)
        weights = weights.astype(jnp.bfloat16)
        p_ref[step] = weights
        acc_ref[part] += dot(vs_ref[pl.ds(start, span), :], weights, TN)
        return carry

    lax.fori_loop(0, steps, value_step, 0, unroll=UNROLL)
    for part in range(2):
        out = acc_ref[part].T.astype(jnp.bfloat16)
        prod = ds_ref[part].astype(jnp.float32) * out.astype(jnp.float32)
        delta_ref[part] = jnp.broadcast_to(jnp.sum(prod.T, axis=0, keepdims=True), (8, cols))
        for head in range(QPG):
            attn_ref[part * stretch:(part + 1) * stretch, head * HD:(head + 1) * HD] = (
                out[head * stretch:(head + 1) * stretch])


def bwd_kernel(stretch, span, ids_ref, own_ref, p_ref, ks_ref, vs_ref, qs_ref, ds_ref, delta_ref,
               dq_ref, dkv_ref, acc_ref, dk_ref, dv_ref):
    slots = ids_ref.shape[0]
    steps = p_ref.shape[0]
    cols = QPG * stretch
    acc_ref[...] = jnp.zeros_like(acc_ref)
    dk_ref[...] = jnp.zeros_like(dk_ref)
    dv_ref[...] = jnp.zeros_like(dv_ref)
    first = (own_ref[0] * stretch + stretch - 1) // span + 1

    def grad_step(step, carry):
        part = jnp.where(step >= first, 1, 0)
        start = pl.multiple_of((step - part * first) * span, span)
        here = pl.ds(start, span)
        weights = p_ref[step]
        grad_probs = dot(vs_ref[here, :], ds_ref[part], NT)
        moved = (grad_probs.reshape(span // 8, 8, cols) - delta_ref[part][None]).reshape(span, cols)
        grad_scores = (weights.astype(jnp.float32) * moved).astype(jnp.bfloat16)
        dv_ref[here, :] += dot(weights, ds_ref[part], NN)
        dk_ref[here, :] += dot(grad_scores, qs_ref[part], NN)
        acc_ref[part] += dot(ks_ref[here, :], grad_scores, TN)
        return carry

    lax.fori_loop(0, steps, grad_step, 0, unroll=UNROLL)
    for part in range(2):
        out = (acc_ref[part].T * SCALE).astype(jnp.bfloat16)
        for head in range(QPG):
            dq_ref[part * stretch:(part + 1) * stretch, head * HD:(head + 1) * HD] = (
                out[head * stretch:(head + 1) * stretch])
    for slot in range(slots):
        start = pl.multiple_of(ids_ref[slot] * stretch, stretch)
        to = slice(slot * stretch, (slot + 1) * stretch)
        dkv_ref[to, :HD] = (dk_ref[pl.ds(start, stretch), :] * SCALE).astype(jnp.bfloat16)
        dkv_ref[to, HD:] = dv_ref[pl.ds(start, stretch), :].astype(jnp.bfloat16)


UNROLL = 1
MIB = 1024 * 1024


def forward(ids, own, queries, kv, grad_heads):
    tokens = queries.shape[0]
    stretch = tokens // 2
    total = kv.shape[0]
    span = 4 * stretch
    cols = QPG * stretch
    steps = total // span + 1
    smem = pl.BlockSpec(memory_space=pltpu.SMEM)
    vmem = pl.BlockSpec(memory_space=pltpu.VMEM)
    b16, f32 = jnp.bfloat16, jnp.float32
    shape = jax.ShapeDtypeStruct
    return pl.pallas_call(
        functools.partial(fwd_kernel, stretch, span),
        out_shape=(
            shape((tokens, QPG * HD), b16),
            shape((steps, span, cols), b16),
            shape((total, HD), b16),
            shape((total, HD), b16),
            shape((2, cols, HD), b16),
            shape((2, cols, HD), b16),
            shape((2, 8, cols), f32),
        ),
        in_specs=[smem, smem, vmem, vmem, vmem],
        out_specs=[vmem] * 7,
        scratch_shapes=[
            pltpu.VMEM((steps, span, cols), f32),
            pltpu.VMEM((2, 8, cols), f32),
            pltpu.VMEM((2, 8, cols), f32),
            pltpu.VMEM((2, HD, cols), f32),
            pltpu.VMEM((span, cols), jnp.int32),
        ],
        compiler_params=pltpu.CompilerParams(vmem_limit_bytes=32 * MIB),
        name="attention_forward",
    )(ids, own, queries, kv, grad_heads)


def backward(ids, own, saved):
    probs, ks, vs, qs, ds, delta = saved
    total = ks.shape[0]
    steps, span, cols = probs.shape
    stretch = cols // QPG
    smem = pl.BlockSpec(memory_space=pltpu.SMEM)
    vmem = pl.BlockSpec(memory_space=pltpu.VMEM)
    b16, f32 = jnp.bfloat16, jnp.float32
    shape = jax.ShapeDtypeStruct
    return pl.pallas_call(
        functools.partial(bwd_kernel, stretch, span),
        out_shape=(shape((2 * stretch, QPG * HD), b16), shape((total, 2 * HD), b16)),
        in_specs=[smem, smem] + [vmem] * 6,
        out_specs=[vmem] * 2,
        scratch_shapes=[
            pltpu.VMEM((2, HD, cols), f32),
            pltpu.VMEM((total, HD), f32),
            pltpu.VMEM((total, HD), f32),
        ],
        compiler_params=pltpu.CompilerParams(vmem_limit_bytes=32 * MIB),
        name="attention_backward",
    )(ids, own, probs, ks, vs, qs, ds, delta)


def on_device(queries, keys, values, stretch_of, out_weight, grad_heads):
    own = lax.dynamic_slice_in_dim(stretch_of, 2 * lax.axis_index("ctx"), 2, 0)
    kv = lax.all_gather(jnp.concatenate([keys, values], axis=1), "ctx", axis=0, tiled=True)
    attn, *saved = forward(stretch_of, own, queries, kv, grad_heads)
    mixed = lax.psum_scatter(
        jnp.dot(attn, out_weight, preferred_element_type=jnp.float32).astype(jnp.bfloat16),
        "tp", scatter_dimension=0, tiled=True)
    q_grad, term = backward(stretch_of, own, saved)
    reduced = lax.psum_scatter(term, "ctx", scatter_dimension=0, tiled=True)
    return mixed, q_grad, reduced[:, :HD], reduced[:, HD:]


def solution(mesh):
    from jax.sharding import PartitionSpec as P
    placed = (P("ctx", "tp"), P("ctx", "tp"), P("ctx", "tp"), P(), P("tp", None), P("ctx", "tp"))
    return jax.shard_map(
        on_device,
        mesh=mesh,
        in_specs=placed,
        out_specs=(P(("ctx", "tp"), None), P("ctx", "tp"), P("ctx", "tp"), P("ctx", "tp")),
        check_vma=False,
    )
```

```python
import functools
import jax
import jax.numpy as jnp
from jax import lax
from jax.experimental import pallas as pl
from jax.experimental.pallas import tpu as pltpu
from jax.sharding import Mesh, PartitionSpec as P

HD = 128
QPG = 4
NEG = -1e30
SCALE = HD ** (-0.5)
NT = (((1,), (1,)), ((), ()))
NN = (((1,), (0,)), ((), ()))
TN = (((0,), (0,)), ((), ()))
MIB = 1024 * 1024
NX, NZ, NC, NH, NY = 4, 4, 2, 2, 4
CTX = ("x", "zl", "core")
TP = ("zh", "y")
MIX_SPAN = 1024
UNROLL_F = 1
UNROLL_B = 1


def dot(a, b, dims):
    return lax.dot_general(a, b, dims, preferred_element_type=jnp.float32)


def slot_of(x, zl, core, half):
    return ((x * NZ + zl) * NC + core) * 2 + half


def own_slot():
    return slot_of(lax.axis_index("x"), lax.axis_index("zl"), lax.axis_index("core"), 0)


def fwd_kernel(stretch, span, ids_ref, q_hbm, kv_hbm, do_hbm, w_hbm,
               mix0, mix1, mix2, mix3, p_ref, kv_ref, qs_ref, ds_ref, delta_ref,
               q_ref, do_ref, w_ref, s_buf, top_ref, sum_ref, acc_ref, diff_ref, attn_ref, turned_ref,
               mixed_ref, kv_sem, q_sem, do_sem, w_sem, out_sem):
    steps = p_ref.shape[0]
    cols = QPG * stretch
    copies = [pltpu.make_async_copy(q_hbm, q_ref, q_sem), pltpu.make_async_copy(do_hbm, do_ref, do_sem)]
    for copy in copies:
        copy.start()
    zl = lax.axis_index("zl")
    place_of = 0
    for core in range(NC):
        for x in range(NX):
            for step in range(NZ):
                first_slot = slot_of(x, jnp.bitwise_xor(zl, step), core, 0)
                for half in range(2):
                    start = pl.multiple_of(ids_ref[first_slot + half] * stretch, stretch)
                    pltpu.make_async_copy(
                        kv_hbm.at[pl.ds(place_of * stretch, stretch), :],
                        kv_ref.at[pl.ds(start, stretch), :], kv_sem).start()
                    place_of += 1
    weight_copy = pltpu.make_async_copy(w_hbm, w_ref, w_sem)
    weight_copy.start()
    k_at = lax.broadcasted_iota(jnp.int32, (span, cols), 0)
    q_at = lax.broadcasted_iota(jnp.int32, (span, cols), 1) % stretch
    diff_ref[...] = k_at - q_at
    top_ref[...] = jnp.full_like(top_ref, NEG)
    sum_ref[...] = jnp.zeros_like(sum_ref)
    acc_ref[...] = jnp.zeros_like(acc_ref)
    for copy in copies:
        copy.wait()
    for part in range(2):
        for head in range(QPG):
            rows = slice(part * stretch, (part + 1) * stretch)
            to = slice(head * stretch, (head + 1) * stretch)
            qs_ref[part, to, :] = q_ref[rows, head * HD:(head + 1) * HD]
            ds_ref[part, to, :] = do_ref[rows, head * HD:(head + 1) * HD]
    mine = own_slot()
    own = [ids_ref[mine], ids_ref[mine + 1]]
    first = (own[0] * stretch + stretch - 1) // span + 1
    pltpu.make_async_copy(kv_hbm, kv_ref, kv_sem).wait()

    def place(step):
        late = step >= first
        part = jnp.where(late, 1, 0)
        chunk = step - part * first
        return part, pl.multiple_of(chunk * span, span), jnp.where(late, own[1], own[0]) * stretch

    def score_step(step, carry):
        part, start, at = place(step)
        scores = dot(kv_ref[pl.ds(start, span), :HD], qs_ref[part], NT) * SCALE
        scores = jnp.where(diff_ref[...] <= at - start, scores, NEG)
        s_buf[step] = scores
        top_ref[part] = jnp.maximum(top_ref[part], jnp.max(scores.reshape(span // 8, 8, cols), axis=0))
        return carry

    lax.fori_loop(0, steps, score_step, 0, unroll=UNROLL_F)
    for part in range(2):
        top_ref[part] = jnp.broadcast_to(jnp.max(top_ref[part], axis=0, keepdims=True), (8, cols))

    def sum_step(step, carry):
        part, start, at = place(step)
        shifted = jnp.exp(s_buf[step].reshape(span // 8, 8, cols) - top_ref[part][None])
        s_buf[step] = shifted.reshape(span, cols)
        sum_ref[part] += jnp.sum(shifted, axis=0)
        return carry

    lax.fori_loop(0, steps, sum_step, 0, unroll=UNROLL_F)
    for part in range(2):
        total = jnp.sum(sum_ref[part], axis=0, keepdims=True)
        sum_ref[part] = jnp.broadcast_to(1.0 / total, (8, cols))

    def value_step(step, carry):
        part, start, at = place(step)
        weights = (s_buf[step].reshape(span // 8, 8, cols) * sum_ref[part][None]).reshape(span, cols)
        weights = weights.astype(jnp.bfloat16)
        p_ref[step] = weights
        acc_ref[part] += dot(kv_ref[pl.ds(start, span), HD:], weights, TN)
        return carry

    lax.fori_loop(0, steps, value_step, 0, unroll=UNROLL_F)
    for part in range(2):
        out = acc_ref[part].T.astype(jnp.bfloat16)
        prod = ds_ref[part].astype(jnp.float32) * out.astype(jnp.float32)
        delta_ref[part] = jnp.broadcast_to(jnp.sum(prod.T, axis=0, keepdims=True), (8, cols))
        for head in range(QPG):
            attn_ref[part * stretch:(part + 1) * stretch, head * HD:(head + 1) * HD] = (
                out[head * stretch:(head + 1) * stretch])
    rows = attn_ref.shape[0] // (NH * NY)
    zh, y = lax.axis_index("zh"), lax.axis_index("y")
    for y_step in range(NY):
        for h_step in range(NH):
            block = jnp.bitwise_xor(zh, h_step) * NY + lax.rem(y + y_step, NY)
            to = (y_step * NH + h_step) * rows
            turned_ref[to:to + rows, :] = attn_ref[pl.ds(pl.multiple_of(block * rows, rows), rows), :]
    weight_copy.wait()
    mixes = (mix0, mix1, mix2, mix3)
    piece = NH * rows
    spans = w_ref.shape[1] // MIX_SPAN
    outs = []
    for index in range(spans):
        at = slice(index * MIX_SPAN, (index + 1) * MIX_SPAN)
        mixed_ref[:, at] = dot(turned_ref[...], w_ref[:, at], NN).astype(jnp.bfloat16)
        for number, mix in enumerate(mixes):
            copy = pltpu.make_async_copy(
                mixed_ref.at[number * piece:(number + 1) * piece, at], mix.at[:, at], out_sem.at[index, number])
            copy.start()
            outs.append(copy)
    for copy in outs:
        copy.wait()


def bwd_kernel(stretch, span, ids_ref, p_ref, kv_ref, qs_ref, ds_ref, delta_ref,
               dq_ref, keep_ref, give_ref, acc_ref, dk_ref, dv_ref):
    steps = p_ref.shape[0]
    cols = QPG * stretch
    acc_ref[...] = jnp.zeros_like(acc_ref)
    dk_ref[...] = jnp.zeros_like(dk_ref)
    dv_ref[...] = jnp.zeros_like(dv_ref)
    mine = own_slot()
    first = (ids_ref[mine] * stretch + stretch - 1) // span + 1

    def grad_step(step, carry):
        part = jnp.where(step >= first, 1, 0)
        start = pl.multiple_of((step - part * first) * span, span)
        here = pl.ds(start, span)
        weights = p_ref[step]
        grad_probs = dot(kv_ref[here, HD:], ds_ref[part], NT)
        moved = (grad_probs.reshape(span // 8, 8, cols) - delta_ref[part][None]).reshape(span, cols)
        grad_scores = (weights.astype(jnp.float32) * moved).astype(jnp.bfloat16)
        dv_ref[here, :] += dot(weights, ds_ref[part], NN)
        dk_ref[here, :] += dot(grad_scores, qs_ref[part], NN)
        acc_ref[part] += dot(kv_ref[here, :HD], grad_scores, TN)
        return carry

    lax.fori_loop(0, steps, grad_step, 0, unroll=UNROLL_B)
    x, zl, core = (lax.axis_index(name) for name in CTX)
    for c_step, out in ((1, give_ref), (0, keep_ref)):
        to = 0
        for x_step in range(NX):
            for z_step in range(NZ):
                slot = slot_of(lax.rem(x + x_step, NX), jnp.bitwise_xor(zl, z_step),
                               jnp.bitwise_xor(core, c_step), 0)
                for half in range(2):
                    start = pl.multiple_of(ids_ref[slot + half] * stretch, stretch)
                    here = pl.ds(start, stretch)
                    out[to:to + stretch, :HD] = (dk_ref[here, :] * SCALE).astype(jnp.bfloat16)
                    out[to:to + stretch, HD:] = dv_ref[here, :].astype(jnp.bfloat16)
                    to += stretch
    for part in range(2):
        out = (acc_ref[part].T * SCALE).astype(jnp.bfloat16)
        for head in range(QPG):
            dq_ref[part * stretch:(part + 1) * stretch, head * HD:(head + 1) * HD] = (
                out[head * stretch:(head + 1) * stretch])


def forward(ids, queries, kv, grad_heads, out_weight):
    tokens = queries.shape[0]
    stretch = tokens // 2
    total = kv.shape[0]
    span = 4 * stretch
    cols = QPG * stretch
    steps = total // span + 1
    depth, width = out_weight.shape
    smem = pl.BlockSpec(memory_space=pltpu.SMEM)
    vmem = pl.BlockSpec(memory_space=pltpu.VMEM)
    hbm = pl.BlockSpec(memory_space=pltpu.HBM)
    b16, f32 = jnp.bfloat16, jnp.float32
    shape = jax.ShapeDtypeStruct
    return pl.pallas_call(
        functools.partial(fwd_kernel, stretch, span),
        out_shape=(shape((tokens // NY, width), b16),) * NY + (
            shape((steps, span, cols), b16),
            shape((total, 2 * HD), b16),
            shape((2, cols, HD), b16),
            shape((2, cols, HD), b16),
            shape((2, 8, cols), f32),
        ),
        in_specs=[smem, hbm, hbm, hbm, hbm],
        out_specs=[hbm] * NY + [vmem] * 5,
        scratch_shapes=[
            pltpu.VMEM((tokens, QPG * HD), b16),
            pltpu.VMEM((tokens, QPG * HD), b16),
            pltpu.VMEM((depth, width), b16),
            pltpu.VMEM((steps, span, cols), f32),
            pltpu.VMEM((2, 8, cols), f32),
            pltpu.VMEM((2, 8, cols), f32),
            pltpu.VMEM((2, HD, cols), f32),
            pltpu.VMEM((span, cols), jnp.int32),
            pltpu.VMEM((tokens, QPG * HD), b16),
            pltpu.VMEM((tokens, QPG * HD), b16),
            pltpu.VMEM((tokens, width), b16),
            pltpu.SemaphoreType.DMA,
            pltpu.SemaphoreType.DMA,
            pltpu.SemaphoreType.DMA,
            pltpu.SemaphoreType.DMA,
            pltpu.SemaphoreType.DMA((width // MIX_SPAN, NY)),
        ],
        compiler_params=pltpu.CompilerParams(vmem_limit_bytes=40 * MIB),
        cost_estimate=pl.CostEstimate(flops=4 * 10**9, bytes_accessed=12 * 10**6, transcendentals=10**6),
        name="attention_forward",
    )(ids, queries, kv, grad_heads, out_weight)


def backward(ids, saved):
    probs, kv, qs, ds, delta = saved
    total = kv.shape[0]
    steps, span, cols = probs.shape
    stretch = cols // QPG
    smem = pl.BlockSpec(memory_space=pltpu.SMEM)
    vmem = pl.BlockSpec(memory_space=pltpu.VMEM)
    b16, f32 = jnp.bfloat16, jnp.float32
    shape = jax.ShapeDtypeStruct
    return pl.pallas_call(
        functools.partial(bwd_kernel, stretch, span),
        out_shape=(shape((2 * stretch, QPG * HD), b16), shape((total // 2, 2 * HD), b16),
                   shape((total // 2, 2 * HD), b16)),
        in_specs=[smem] + [vmem] * 5,
        out_specs=[vmem] * 3,
        scratch_shapes=[
            pltpu.VMEM((2, HD, cols), f32),
            pltpu.VMEM((total, HD), f32),
            pltpu.VMEM((total, HD), f32),
        ],
        compiler_params=pltpu.CompilerParams(vmem_limit_bytes=32 * MIB),
        cost_estimate=pl.CostEstimate(flops=4 * 10**9, bytes_accessed=12 * 10**6, transcendentals=0),
        name="attention_backward",
    )(ids, probs, kv, qs, ds, delta)


def ahead(block, axis, step):
    count = lax.axis_size(axis)
    return lax.ppermute(block, axis, [(i, (i + step) % count) for i in range(count)])


def across(block, axis, step):
    count = lax.axis_size(axis)
    return lax.ppermute(block, axis, [(i, i ^ step) for i in range(count)])


def total_of(parts):
    total = parts[0].astype(jnp.float32)
    for part in parts[1:]:
        total = total + part.astype(jnp.float32)
    return total.astype(jnp.bfloat16)


def on_device(queries, keys, values, stretch_of, out_weight, grad_heads):
    kv = jnp.concatenate([keys, values], axis=1)
    kv = jnp.concatenate([kv] + [across(kv, "zl", step) for step in range(1, NZ)], axis=0)
    kv = lax.all_gather(kv, "x", axis=0, tiled=True)
    kv = lax.all_gather(kv, "core", axis=0, tiled=True)
    *mixes, probs, kv, qs, ds, delta = forward(stretch_of, queries, kv, grad_heads, out_weight)
    mixed = total_of([mixes[0]] + [ahead(mixes[step], "y", step) for step in range(1, NY)])
    rows = mixed.shape[0] // NH
    mixed = total_of([mixed[:rows], across(mixed[rows:], "zh", 1)])
    q_grad, keep, give = backward(stretch_of, (probs, kv, qs, ds, delta))
    term = total_of([keep, across(give, "core", 1)])
    part = term.shape[0] // NX
    term = total_of([term[:part]] + [
        ahead(term[step * part:(step + 1) * part], "x", step) for step in range(1, NX)])
    part = term.shape[0] // NZ
    term = total_of([term[:part]] + [
        across(term[step * part:(step + 1) * part], "zl", step) for step in range(1, NZ)])
    return mixed, q_grad, term[:, :HD], term[:, HD:]


def solution(mesh):
    fine = Mesh(mesh.devices.reshape(NX, NZ, NC, NH, NY), CTX + TP)
    return jax.shard_map(
        on_device,
        mesh=fine,
        in_specs=(P(CTX, TP), P(CTX, TP), P(CTX, TP), P(), P(TP, None), P(CTX, TP)),
        out_specs=(P(CTX + TP, None), P(CTX, TP), P(CTX, TP), P(CTX, TP)),
        check_vma=False,
    )
```

```python
import functools
import jax
import jax.numpy as jnp
from jax import lax
from jax.experimental import pallas as pl
from jax.experimental.pallas import tpu as pltpu
from jax.sharding import Mesh, PartitionSpec as P

HD = 128
QPG = 4
NEG = -1e30
SCALE = HD ** (-0.5)
NT = (((1,), (1,)), ((), ()))
NN = (((1,), (0,)), ((), ()))
TN = (((0,), (0,)), ((), ()))
MIB = 1024 * 1024
NX, NZ, NC, NH, NY = 4, 4, 2, 2, 4
CTX = ("x", "zl", "core")
TP = ("zh", "y")
MIX_SPAN = 1024
UNROLL_S = 17
UNROLL_V = 17
UNROLL_B = 17
SMEM = pl.BlockSpec(memory_space=pltpu.SMEM)
VMEM = pl.BlockSpec(memory_space=pltpu.VMEM)
HBM = pl.BlockSpec(memory_space=pltpu.HBM)


def dot(a, b, dims):
    return lax.dot_general(a, b, dims, preferred_element_type=jnp.float32)


def slot_of(x, zl, core, half):
    return ((x * NZ + zl) * NC + core) * 2 + half


def place_of(c_step, x_step, z_step):
    x, zl, core = (lax.axis_index(name) for name in CTX)
    return slot_of(lax.rem(x + x_step, NX), jnp.bitwise_xor(zl, z_step), jnp.bitwise_xor(core, c_step), 0)


def pair_kernel(k_hbm, v_hbm, kv_ref, sem):
    copies = [pltpu.make_async_copy(k_hbm, kv_ref.at[:, :HD], sem.at[0]),
              pltpu.make_async_copy(v_hbm, kv_ref.at[:, HD:], sem.at[1])]
    for copy in copies:
        copy.start()
    for copy in copies:
        copy.wait()


def heads_kernel(ids_ref, q_hbm, do_hbm, same_ref, qs_ref, ds_ref, sem):
    stretch = q_hbm.shape[0] // 2
    for slot in range(ids_ref.shape[0]):
        same_ref[slot] = ids_ref[slot]
    copies = []
    for which, (source, target) in enumerate(((q_hbm, qs_ref), (do_hbm, ds_ref))):
        for part in range(2):
            for head in range(QPG):
                copies.append(pltpu.make_async_copy(
                    source.at[part * stretch:(part + 1) * stretch, head * HD:(head + 1) * HD],
                    target.at[part, head * stretch:(head + 1) * stretch, :],
                    sem.at[which, part, head]))
    for copy in copies:
        copy.start()
    for copy in copies:
        copy.wait()


def fwd_kernel(stretch, span, ids_ref, qs_ref, ds_ref, *rest):
    pieces, rest = rest[:NC * NX], rest[NC * NX:]
    w_hbm, rest = rest[0], rest[1:]
    mixes, rest = rest[:NY], rest[NY:]
    (p_ref, kv_ref, delta_ref, inv_ref,
     w_ref, s_buf, top_ref, sum_ref, acc_ref, diff_ref, attn_ref, turned_ref, w_sem) = rest
    steps = p_ref.shape[0]
    cols = QPG * stretch
    weight_copy = pltpu.make_async_copy(w_hbm, w_ref, w_sem)
    weight_copy.start()
    for c_step in range(NC):
        for x_step in range(NX):
            piece = pieces[c_step * NX + x_step]
            for z_step in range(NZ):
                slot = place_of(c_step, x_step, z_step)
                for half in range(2):
                    start = pl.multiple_of(ids_ref[slot + half] * stretch, stretch)
                    at = (z_step * 2 + half) * stretch
                    kv_ref[pl.ds(start, stretch), :] = piece[at:at + stretch, :]
    k_at = lax.broadcasted_iota(jnp.int32, (span, cols), 0)
    q_at = lax.broadcasted_iota(jnp.int32, (span, cols), 1) % stretch
    diff_ref[...] = k_at - q_at
    top_ref[...] = jnp.full_like(top_ref, NEG)
    sum_ref[...] = jnp.zeros_like(sum_ref)
    acc_ref[...] = jnp.zeros_like(acc_ref)
    mine = place_of(0, 0, 0)
    own = [ids_ref[mine], ids_ref[mine + 1]]
    first = (own[0] * stretch + stretch - 1) // span + 1

    def place(step):
        late = step >= first
        part = jnp.where(late, 1, 0)
        chunk = step - part * first
        return part, pl.multiple_of(chunk * span, span), jnp.where(late, own[1], own[0]) * stretch

    def score_step(step, carry):
        part, start, at = place(step)
        scores = dot(kv_ref[pl.ds(start, span), :HD], qs_ref[part], NT)
        scores = jnp.where(diff_ref[...] <= at - start, scores, NEG)
        s_buf[step] = scores
        top_ref[part] = jnp.maximum(top_ref[part], jnp.max(scores.reshape(span // 8, 8, cols), axis=0))
        return carry

    lax.fori_loop(0, steps, score_step, 0, unroll=UNROLL_S)
    for part in range(2):
        top_ref[part] = jnp.broadcast_to(jnp.max(top_ref[part], axis=0, keepdims=True), (8, cols))

    def value_step(step, carry):
        part, start, at = place(step)
        shifted = jnp.exp((s_buf[step].reshape(span // 8, 8, cols) - top_ref[part][None]) * SCALE)
        sum_ref[part] += jnp.sum(shifted, axis=0)
        weights = shifted.reshape(span, cols).astype(jnp.bfloat16)
        p_ref[step] = weights
        acc_ref[part] += dot(kv_ref[pl.ds(start, span), HD:], weights, TN)
        return carry

    lax.fori_loop(0, steps, value_step, 0, unroll=UNROLL_V)
    for part in range(2):
        inverse = 1.0 / jnp.sum(sum_ref[part], axis=0, keepdims=True)
        inv_ref[part] = jnp.broadcast_to(inverse, (8, cols))
        out = (acc_ref[part] * inverse).T.astype(jnp.bfloat16)
        prod = ds_ref[part].astype(jnp.float32) * out.astype(jnp.float32)
        delta_ref[part] = jnp.broadcast_to(jnp.sum(prod.T, axis=0, keepdims=True), (8, cols))
        for head in range(QPG):
            attn_ref[part * stretch:(part + 1) * stretch, head * HD:(head + 1) * HD] = (
                out[head * stretch:(head + 1) * stretch])
    rows = attn_ref.shape[0] // (NH * NY)
    zh, y = lax.axis_index("zh"), lax.axis_index("y")
    for y_step in range(NY):
        for h_step in range(NH):
            block = jnp.bitwise_xor(zh, h_step) * NY + lax.rem(y + y_step, NY)
            to = (y_step * NH + h_step) * rows
            turned_ref[to:to + rows, :] = attn_ref[pl.ds(pl.multiple_of(block * rows, rows), rows), :]
    weight_copy.wait()
    piece = NH * rows

    for index in range(w_ref.shape[1] // MIX_SPAN):
        at = slice(index * MIX_SPAN, (index + 1) * MIX_SPAN)
        mixed = dot(turned_ref[...], w_ref[:, at], NN).astype(jnp.bfloat16)
        for number, mix in enumerate(mixes):
            mix[:, at] = mixed[number * piece:(number + 1) * piece]


def bwd_kernel(stretch, span, ids_ref, p_ref, kv_ref, qs_ref, ds_ref, delta_ref, inv_ref,
               dq_ref, keep_ref, give_ref, acc_ref, dk_ref, dv_ref, dn_ref):
    steps = p_ref.shape[0]
    cols = QPG * stretch
    acc_ref[...] = jnp.zeros_like(acc_ref)
    dk_ref[...] = jnp.zeros_like(dk_ref)
    dv_ref[...] = jnp.zeros_like(dv_ref)
    for part in range(2):
        column = jnp.broadcast_to(inv_ref[part][:1], (HD, cols)).T
        dn_ref[part] = (ds_ref[part].astype(jnp.float32) * column).astype(jnp.bfloat16)
    first = (ids_ref[place_of(0, 0, 0)] * stretch + stretch - 1) // span + 1

    def grad_step(step, carry):
        part = jnp.where(step >= first, 1, 0)
        start = pl.multiple_of((step - part * first) * span, span)
        here = pl.ds(start, span)
        weights = p_ref[step]
        grad_probs = dot(kv_ref[here, HD:], ds_ref[part], NT)
        moved = (grad_probs.reshape(span // 8, 8, cols) - delta_ref[part][None]) * inv_ref[part][None]
        grad_scores = (weights.astype(jnp.float32) * moved.reshape(span, cols)).astype(jnp.bfloat16)
        dv_ref[here, :] += dot(weights, dn_ref[part], NN)
        dk_ref[here, :] += dot(grad_scores, qs_ref[part], NN)
        acc_ref[part] += dot(kv_ref[here, :HD], grad_scores, TN)
        return carry

    lax.fori_loop(0, steps, grad_step, 0, unroll=UNROLL_B)
    for c_step, out in ((1, give_ref), (0, keep_ref)):
        to = 0
        for x_step in range(NX):
            for z_step in range(NZ):
                slot = place_of(c_step, x_step, z_step)
                for half in range(2):
                    here = pl.ds(pl.multiple_of(ids_ref[slot + half] * stretch, stretch), stretch)
                    out[to:to + stretch, :HD] = (dk_ref[here, :] * SCALE).astype(jnp.bfloat16)
                    out[to:to + stretch, HD:] = dv_ref[here, :].astype(jnp.bfloat16)
                    to += stretch
    for part in range(2):
        out = (acc_ref[part].T * SCALE).astype(jnp.bfloat16)
        for head in range(QPG):
            dq_ref[part * stretch:(part + 1) * stretch, head * HD:(head + 1) * HD] = (
                out[head * stretch:(head + 1) * stretch])


def pair(keys, values):
    return pl.pallas_call(
        pair_kernel,
        out_shape=jax.ShapeDtypeStruct((keys.shape[0], 2 * HD), jnp.bfloat16),
        in_specs=[HBM] * 2,
        out_specs=VMEM,
        scratch_shapes=[pltpu.SemaphoreType.DMA((2,))],
        compiler_params=pltpu.CompilerParams(vmem_limit_bytes=60 * MIB),
        name="pair",
    )(keys, values)


def by_heads(ids, queries, grad_heads):
    shape = jax.ShapeDtypeStruct((2, QPG * queries.shape[0] // 2, HD), jnp.bfloat16)
    return pl.pallas_call(
        heads_kernel,
        out_shape=(jax.ShapeDtypeStruct(ids.shape, ids.dtype), shape, shape),
        in_specs=[SMEM] + [HBM] * 2,
        out_specs=[SMEM] + [VMEM] * 2,
        scratch_shapes=[pltpu.SemaphoreType.DMA((2, 2, QPG))],
        compiler_params=pltpu.CompilerParams(vmem_limit_bytes=4 * MIB),
        name="by_heads",
    )(ids, queries, grad_heads)


def forward(ids, qs, ds, pieces, out_weight):
    cols = qs.shape[1]
    stretch = cols // QPG
    tokens = 2 * stretch
    total = sum(piece.shape[0] for piece in pieces)
    span = 4 * stretch
    steps = total // span + 1
    depth, width = out_weight.shape
    b16, f32 = jnp.bfloat16, jnp.float32
    shape = jax.ShapeDtypeStruct
    return pl.pallas_call(
        functools.partial(fwd_kernel, stretch, span),
        out_shape=(shape((tokens // NY, width), b16),) * NY + (
            shape((steps, span, cols), b16),
            shape((total, 2 * HD), b16),
            shape((2, 8, cols), f32),
            shape((2, 8, cols), f32),
        ),
        in_specs=[SMEM] + [VMEM] * (2 + len(pieces)) + [HBM],
        out_specs=[VMEM] * (NY + 4),
        scratch_shapes=[
            pltpu.VMEM((depth, width), b16),
            pltpu.VMEM((steps, span, cols), f32),
            pltpu.VMEM((2, 8, cols), f32),
            pltpu.VMEM((2, 8, cols), f32),
            pltpu.VMEM((2, HD, cols), f32),
            pltpu.VMEM((span, cols), jnp.int32),
            pltpu.VMEM((tokens, QPG * HD), b16),
            pltpu.VMEM((tokens, QPG * HD), b16),
            pltpu.SemaphoreType.DMA,
        ],
        compiler_params=pltpu.CompilerParams(vmem_limit_bytes=40 * MIB),
        cost_estimate=pl.CostEstimate(flops=4 * 10**9, bytes_accessed=12 * 10**6, transcendentals=10**6),
        name="attention_forward",
    )(ids, qs, ds, *pieces, out_weight)


def backward(ids, probs, kv, qs, ds, delta, inverse):
    total = kv.shape[0]
    steps, span, cols = probs.shape
    stretch = cols // QPG
    b16, f32 = jnp.bfloat16, jnp.float32
    shape = jax.ShapeDtypeStruct
    return pl.pallas_call(
        functools.partial(bwd_kernel, stretch, span),
        out_shape=(shape((2 * stretch, QPG * HD), b16), shape((total // 2, 2 * HD), b16),
                   shape((total // 2, 2 * HD), b16)),
        in_specs=[SMEM] + [VMEM] * 6,
        out_specs=[VMEM] * 3,
        scratch_shapes=[
            pltpu.VMEM((2, HD, cols), f32),
            pltpu.VMEM((total, HD), f32),
            pltpu.VMEM((total, HD), f32),
            pltpu.VMEM((2, cols, HD), b16),
        ],
        compiler_params=pltpu.CompilerParams(vmem_limit_bytes=32 * MIB),
        cost_estimate=pl.CostEstimate(flops=5 * 10**10, bytes_accessed=12 * 10**6, transcendentals=0),
        name="attention_backward",
    )(ids, probs, kv, qs, ds, delta, inverse)


def ahead(block, axis, step):
    count = lax.axis_size(axis)
    return lax.ppermute(block, axis, [(i, (i + step) % count) for i in range(count)])


def behind(block, axis, step):
    count = lax.axis_size(axis)
    return lax.ppermute(block, axis, [((i + step) % count, i) for i in range(count)])


def across(block, axis, step):
    count = lax.axis_size(axis)
    return lax.ppermute(block, axis, [(i, i ^ step) for i in range(count)])


def total_of(parts):
    total = parts[0].astype(jnp.float32)
    for part in parts[1:]:
        total = total + part.astype(jnp.float32)
    return total.astype(jnp.bfloat16)


def on_device(queries, keys, values, stretch_of, out_weight, grad_heads):
    kv = pair(keys, values)
    stretch_of, qs, ds = by_heads(stretch_of, queries, grad_heads)
    kv = jnp.concatenate([kv] + [across(kv, "zl", step) for step in range(1, NZ)], axis=0)
    pieces = [kv] + [behind(kv, "x", step) for step in range(1, NX)]
    pieces = pieces + [across(piece, "core", 1) for piece in pieces]
    *mixes, probs, kv, delta, inverse = forward(stretch_of, qs, ds, pieces, out_weight)
    mixed = total_of([mixes[0]] + [ahead(mixes[step], "y", step) for step in range(1, NY)])
    rows = mixed.shape[0] // NH
    mixed = total_of([mixed[:rows], across(mixed[rows:], "zh", 1)])
    q_grad, keep, give = backward(stretch_of, probs, kv, qs, ds, delta, inverse)
    term = total_of([keep, across(give, "core", 1)])
    part = term.shape[0] // NX
    term = total_of([term[:part]] + [
        ahead(term[step * part:(step + 1) * part], "x", step) for step in range(1, NX)])
    part = term.shape[0] // NZ
    term = total_of([term[:part]] + [
        across(term[step * part:(step + 1) * part], "zl", step) for step in range(1, NZ)])
    return mixed, q_grad, term[:, :HD], term[:, HD:]


def solution(mesh):
    fine = Mesh(mesh.devices.reshape(NX, NZ, NC, NH, NY), CTX + TP)
    return jax.shard_map(
        on_device,
        mesh=fine,
        in_specs=(P(CTX, TP), P(CTX, TP), P(CTX, TP), P(), P(TP, None), P(CTX, TP)),
        out_specs=(P(CTX + TP, None), P(CTX, TP), P(CTX, TP), P(CTX, TP)),
        check_vma=False,
    )
```

```python
import functools
import jax
import jax.numpy as jnp
from jax import lax
from jax.experimental import pallas as pl
from jax.experimental.pallas import tpu as pltpu
from jax.sharding import Mesh, PartitionSpec as P

HD = 128
QPG = 4
NEG = -1e30
SCALE = HD ** (-0.5)
NT = (((1,), (1,)), ((), ()))
NN = (((1,), (0,)), ((), ()))
TN = (((0,), (0,)), ((), ()))
MIB = 1024 * 1024
NX, NZ, NC, NH, NY = 4, 4, 2, 2, 4
CTX = ("x", "zl", "core")
TP = ("zh", "y")
MIX_SPAN = 1024
CHUNK = 4
BWD_FLOPS = 2 * 10**10
SMEM = pl.BlockSpec(memory_space=pltpu.SMEM)
VMEM = pl.BlockSpec(memory_space=pltpu.VMEM)
HBM = pl.BlockSpec(memory_space=pltpu.HBM)
ANY = pl.BlockSpec(memory_space=pl.ANY)


def dot(a, b, dims):
    return lax.dot_general(a, b, dims, preferred_element_type=jnp.float32)


def slot_of(x, zl, core, half):
    return ((x * NZ + zl) * NC + core) * 2 + half


def place_of(c_step, x_step, z_step):
    x, zl, core = (lax.axis_index(name) for name in CTX)
    return slot_of(lax.rem(x + x_step, NX), jnp.bitwise_xor(zl, z_step), jnp.bitwise_xor(core, c_step), 0)


def pair_kernel(k_hbm, v_hbm, kv_ref, sem):
    copies = [pltpu.make_async_copy(k_hbm, kv_ref.at[:, :HD], sem.at[0]),
              pltpu.make_async_copy(v_hbm, kv_ref.at[:, HD:], sem.at[1])]
    for copy in copies:
        copy.start()
    for copy in copies:
        copy.wait()


def heads_kernel(q_hbm, do_hbm, kv_ref, qs_ref, ds_ref, same_ref, sem):
    stretch = q_hbm.shape[0] // 2
    copies = []
    for which, (source, target) in enumerate(((q_hbm, qs_ref), (do_hbm, ds_ref))):
        for part in range(2):
            for head in range(QPG):
                copies.append(pltpu.make_async_copy(
                    source.at[part * stretch:(part + 1) * stretch, head * HD:(head + 1) * HD],
                    target.at[part, head * stretch:(head + 1) * stretch, :],
                    sem.at[which, part, head]))
    for copy in copies:
        copy.start()
    same_ref[...] = kv_ref[...]
    for copy in copies:
        copy.wait()


def plan_kernel(ids_ref, plan_ref, slot_ref):
    slots = ids_ref.shape[0]
    core = lax.axis_index("core")
    mine = place_of(0, 0, 0)
    own = [ids_ref[mine], ids_ref[mine + 1]]
    for slot in range(slots):
        slot_ref[ids_ref[slot]] = jnp.int32(slot)
    near, far, *seen = (jnp.int32(0),) * 6
    for value in range(slots):
        slot = slot_ref[value]
        away = jnp.bitwise_xor(lax.rem(slot // 2, NC), core)
        at = jnp.where(away == 0, near, slots // 2 + far)
        plan_ref[slot] = at
        plan_ref[slots + at] = jnp.int32(value)
        near, far = near + (1 - away), far + away
        seen = [before + jnp.where((own[part] >= value) & (away == side), 1, 0)
                for before, (side, part) in zip(seen, ((0, 0), (0, 1), (1, 0), (1, 1)))]
    for index in range(4):
        plan_ref[2 * slots + index] = (seen[index] + CHUNK - 1) // CHUNK
    for part in range(2):
        plan_ref[2 * slots + 4 + part] = own[part]


class Plan:
    def __init__(self, ref, slots, stretch):
        self.ref, self.slots, self.stretch = ref, slots, stretch
        self.span = CHUNK * stretch

    def row(self, slot):
        return pl.multiple_of(self.ref[slot] * self.stretch, self.stretch)

    def step(self, side, index):
        first = self.ref[2 * self.slots + 2 * side]
        count = first + self.ref[2 * self.slots + 2 * side + 1]
        late = index >= first
        part = jnp.where(late, 1, 0)
        last = self.slots // 2 // CHUNK - 1
        chunk = jnp.minimum(index - part * first, last)
        row = pl.multiple_of(chunk * self.span, self.span)
        return part, row, chunk, index < count

    def limits(self, side, part, chunk, valid):
        own = self.ref[2 * self.slots + 4 + part]
        at = self.slots + side * (self.slots // 2) + chunk * CHUNK
        return [jnp.where(valid, (own - self.ref[at + group]) * self.stretch, -2 * self.stretch)
                for group in range(CHUNK)]


def fwd_kernel(stretch, plan_ref, qs_ref, ds_ref, *rest):
    pieces, rest = rest[:NC * NX], rest[NC * NX:]
    (w_hbm, own_ref, front_ref, back_ref, far_a, far_b, p_ref, kv_ref, delta_ref, inv_ref,
     w_ref, s_buf, top_ref, sum_ref, acc_ref, diff_ref, attn_ref, turned_ref, w_sem) = rest
    steps, span, cols = p_ref.shape
    total = kv_ref.shape[0]
    plan = Plan(plan_ref, total // stretch, stretch)
    weight_copies = []
    for index in range(w_ref.shape[1] // MIX_SPAN):
        at = slice(index * MIX_SPAN, (index + 1) * MIX_SPAN)
        weight_copies.append(pltpu.make_async_copy(w_hbm.at[:, at], w_ref.at[:, at], w_sem.at[index]))
    for copy in weight_copies:
        copy.start()
    for c_step in range(NC):
        for x_step in range(NX):
            piece = pieces[c_step * NX + x_step]
            for z_step in range(NZ):
                slot = place_of(c_step, x_step, z_step)
                for half in range(2):
                    at = (z_step * 2 + half) * stretch
                    kv_ref[pl.ds(plan.row(slot + half), stretch), :] = piece[at:at + stretch, :]
    k_at = lax.broadcasted_iota(jnp.int32, (stretch, cols), 0)
    q_at = lax.broadcasted_iota(jnp.int32, (stretch, cols), 1) % stretch
    diff_ref[...] = k_at - q_at
    top_ref[...] = jnp.full_like(top_ref, NEG)
    sum_ref[...] = jnp.zeros_like(sum_ref)
    acc_ref[...] = jnp.zeros_like(acc_ref)

    for step in range(steps):
        side, index = divmod(step, steps // 2)
        part, row, chunk, valid = plan.step(side, index)
        scores = dot(kv_ref[pl.ds(side * (total // 2) + row, span), :HD], qs_ref[part], NT)
        limits = plan.limits(side, part, chunk, valid)
        top = top_ref[part]
        for group, limit in enumerate(limits):
            rows = slice(group * stretch, (group + 1) * stretch)
            block = jnp.where(diff_ref[...] <= limit, scores[rows], NEG)
            s_buf[step, rows] = block
            top = jnp.maximum(top, jnp.max(block.reshape(stretch // 8, 8, cols), axis=0))
        top_ref[part] = top
    for part in range(2):
        top_ref[part] = jnp.broadcast_to(jnp.max(top_ref[part], axis=0, keepdims=True), (8, cols))

    for step in range(steps):
        side, index = divmod(step, steps // 2)
        part, row, chunk, valid = plan.step(side, index)
        shifted = jnp.exp((s_buf[step].reshape(span // 8, 8, cols) - top_ref[part][None]) * SCALE)
        sum_ref[part] += jnp.sum(shifted, axis=0)
        weights = shifted.reshape(span, cols).astype(jnp.bfloat16)
        p_ref[step] = weights
        acc_ref[part] += dot(kv_ref[pl.ds(side * (total // 2) + row, span), HD:], weights, TN)

    for part in range(2):
        inverse = 1.0 / jnp.sum(sum_ref[part], axis=0, keepdims=True)
        inv_ref[part] = jnp.broadcast_to(inverse, (8, cols))
        out = (acc_ref[part] * inverse).T.astype(jnp.bfloat16)
        prod = ds_ref[part].astype(jnp.float32) * out.astype(jnp.float32)
        delta_ref[part] = jnp.broadcast_to(jnp.sum(prod.T, axis=0, keepdims=True), (8, cols))
        for head in range(QPG):
            attn_ref[part * stretch:(part + 1) * stretch, head * HD:(head + 1) * HD] = (
                out[head * stretch:(head + 1) * stretch])
    rows = attn_ref.shape[0] // (NH * NY)
    zh, y = lax.axis_index("zh"), lax.axis_index("y")
    for y_step in range(NY):
        for h_step in range(NH):
            block = jnp.bitwise_xor(zh, h_step) * NY + lax.rem(y + y_step, NY)
            to = (y_step * NH + h_step) * rows
            turned_ref[to:to + rows, :] = attn_ref[pl.ds(pl.multiple_of(block * rows, rows), rows), :]
    piece = NH * rows
    for index in range(w_ref.shape[1] // MIX_SPAN):
        at = slice(index * MIX_SPAN, (index + 1) * MIX_SPAN)
        weight_copies[index].wait()
        mixed = dot(turned_ref[...], w_ref[:, at], NN).astype(jnp.bfloat16)
        own_ref[:, at] = mixed[:piece]
        front_ref[:, at] = mixed[piece:2 * piece]
        back_ref[:, at] = mixed[3 * piece:]
        half = w_ref.shape[1] // 2
        if at.start < half:
            far_a[:, at] = mixed[2 * piece:3 * piece]
        else:
            far_b[:, at.start - half:at.stop - half] = mixed[2 * piece:3 * piece]


def bwd_kernel(stretch, side, plan_ref, p_ref, kv_ref, qs_ref, ds_ref, delta_ref, inv_ref, *rest):
    steps, span, cols = p_ref.shape
    total = kv_ref.shape[0]
    plan = Plan(plan_ref, total // stretch, stretch)
    if side == 0:
        acc_in, token_ref, dq_ref, out_ref, acc_ref, dk_ref, dv_ref, dn_ref = rest
        acc_ref[...] = acc_in[...]
    else:
        acc_ref, out_ref, dk_ref, dv_ref, dn_ref = rest
        acc_ref[...] = jnp.zeros_like(acc_ref)
    dk_ref[...] = jnp.zeros_like(dk_ref)
    dv_ref[...] = jnp.zeros_like(dv_ref)
    for part in range(2):
        column = jnp.broadcast_to(inv_ref[part][:1], (HD, cols)).T
        dn_ref[part] = (ds_ref[part].astype(jnp.float32) * column).astype(jnp.bfloat16)

    for index in range(steps // 2):
        part, row, chunk, valid = plan.step(side, index)
        here = pl.ds(row, span)
        there = pl.ds(side * (total // 2) + row, span)
        weights = p_ref[side * (steps // 2) + index]
        grad_probs = dot(kv_ref[there, HD:], ds_ref[part], NT)
        moved = (grad_probs.reshape(span // 8, 8, cols) - delta_ref[part][None]) * inv_ref[part][None]
        grad_scores = (weights.astype(jnp.float32) * moved.reshape(span, cols)).astype(jnp.bfloat16)
        dv_ref[here, :] += dot(weights, dn_ref[part], NN)
        dk_ref[here, :] += dot(grad_scores, qs_ref[part], NN)
        acc_ref[part] += dot(kv_ref[there, :HD], grad_scores, TN)

    to = 0
    for x_step in range(NX):
        for z_step in range(NZ):
            slot = place_of(side, x_step, z_step)
            for half in range(2):
                here = pl.ds(plan.row(slot + half) - side * (total // 2), stretch)
                out_ref[to:to + stretch, :HD] = (dk_ref[here, :] * SCALE).astype(jnp.bfloat16)
                out_ref[to:to + stretch, HD:] = dv_ref[here, :].astype(jnp.bfloat16)
                to += stretch
    if side == 0:
        for part in range(2):
            out = (acc_ref[part].T * SCALE).astype(jnp.bfloat16)
            for head in range(QPG):
                dq_ref[part * stretch:(part + 1) * stretch, head * HD:(head + 1) * HD] = (
                    out[head * stretch:(head + 1) * stretch])


def pair(keys, values):
    return pl.pallas_call(
        pair_kernel,
        out_shape=jax.ShapeDtypeStruct((keys.shape[0], 2 * HD), jnp.bfloat16),
        in_specs=[HBM] * 2,
        out_specs=VMEM,
        scratch_shapes=[pltpu.SemaphoreType.DMA((2,))],
        compiler_params=pltpu.CompilerParams(vmem_limit_bytes=60 * MIB),
        name="pair",
    )(keys, values)


def by_heads(queries, grad_heads, kv):
    shape = jax.ShapeDtypeStruct((2, QPG * queries.shape[0] // 2, HD), jnp.bfloat16)
    return pl.pallas_call(
        heads_kernel,
        out_shape=(shape, shape, jax.ShapeDtypeStruct(kv.shape, kv.dtype)),
        in_specs=[HBM] * 2 + [VMEM],
        out_specs=[VMEM] * 3,
        scratch_shapes=[pltpu.SemaphoreType.DMA((2, 2, QPG))],
        compiler_params=pltpu.CompilerParams(vmem_limit_bytes=4 * MIB),
        name="by_heads",
    )(queries, grad_heads, kv)


def plan_of(ids):
    slots = ids.shape[0]
    return pl.pallas_call(
        plan_kernel,
        out_shape=jax.ShapeDtypeStruct((2 * slots + 8,), jnp.int32),
        in_specs=[SMEM],
        out_specs=SMEM,
        scratch_shapes=[pltpu.SMEM((slots,), jnp.int32)],
        compiler_params=pltpu.CompilerParams(vmem_limit_bytes=4 * MIB),
        name="plan",
    )(ids)


def relay_kernel(front_in, back_in, front_add, back_add, front_ref, back_ref):
    half = front_add.shape[1]
    for index in range(2):
        at = slice(index * half // 2, (index + 1) * half // 2)
        front_ref[:, at] = (front_in[:, at].astype(jnp.float32) + front_add[:, at].astype(jnp.float32)
                            ).astype(jnp.bfloat16)
        to = slice(half + index * half // 2, half + (index + 1) * half // 2)
        back_ref[:, to] = (back_in[:, to].astype(jnp.float32) + back_add[:, at].astype(jnp.float32)
                           ).astype(jnp.bfloat16)


def relay(front, back, front_add, back_add):
    shape = jax.ShapeDtypeStruct(front.shape, front.dtype)
    return pl.pallas_call(
        relay_kernel,
        out_shape=(shape, shape),
        in_specs=[VMEM] * 4,
        out_specs=[VMEM] * 2,
        input_output_aliases={0: 0, 1: 1},
        compiler_params=pltpu.CompilerParams(vmem_limit_bytes=8 * MIB),
        name="relay",
    )(front, back, front_add, back_add)


def stack_kernel(token_ref, *refs):
    *parts, out_ref = refs
    rows = parts[0].shape[0]
    for index, part in enumerate(parts):
        out_ref[index * rows:(index + 1) * rows, :] = part[...]


def stack(token, *parts):
    rows, width = parts[0].shape
    return pl.pallas_call(
        stack_kernel,
        out_shape=jax.ShapeDtypeStruct((len(parts) * rows, width), parts[0].dtype),
        in_specs=[ANY] + [VMEM] * len(parts),
        out_specs=VMEM,
        compiler_params=pltpu.CompilerParams(vmem_limit_bytes=4 * MIB),
        name="stack",
    )(token, *parts)


def forward(plan, qs, ds, pieces, out_weight):
    cols = qs.shape[1]
    stretch = cols // QPG
    tokens = 2 * stretch
    total = sum(piece.shape[0] for piece in pieces)
    span = CHUNK * stretch
    steps = total // span + 2
    depth, width = out_weight.shape
    b16, f32 = jnp.bfloat16, jnp.float32
    shape = jax.ShapeDtypeStruct
    return pl.pallas_call(
        functools.partial(fwd_kernel, stretch),
        out_shape=(shape((tokens // NY, width), b16),) * 3 + (shape((tokens // NY, width // 2), b16),) * 2 + (
            shape((steps, span, cols), b16),
            shape((total, 2 * HD), b16),
            shape((2, 8, cols), f32),
            shape((2, 8, cols), f32),
        ),
        in_specs=[SMEM] + [VMEM] * (2 + len(pieces)) + [HBM],
        out_specs=[VMEM] * 9,
        scratch_shapes=[
            pltpu.VMEM((depth, width), b16),
            pltpu.VMEM((steps, span, cols), f32),
            pltpu.VMEM((2, 8, cols), f32),
            pltpu.VMEM((2, 8, cols), f32),
            pltpu.VMEM((2, HD, cols), f32),
            pltpu.VMEM((stretch, cols), jnp.int32),
            pltpu.VMEM((tokens, QPG * HD), b16),
            pltpu.VMEM((tokens, QPG * HD), b16),
            pltpu.SemaphoreType.DMA((width // MIX_SPAN,)),
        ],
        compiler_params=pltpu.CompilerParams(vmem_limit_bytes=40 * MIB),
        cost_estimate=pl.CostEstimate(flops=4 * 10**9, bytes_accessed=12 * 10**6, transcendentals=10**6),
        name="attention_forward",
    )(plan, qs, ds, *pieces, out_weight)


def backward(side, plan, probs, kv, qs, ds, delta, inverse, *partial):
    total = kv.shape[0]
    steps, span, cols = probs.shape
    stretch = cols // QPG
    b16, f32 = jnp.bfloat16, jnp.float32
    shape = jax.ShapeDtypeStruct
    terms = shape((total // 2, 2 * HD), b16)
    sums = (2, HD, cols)
    scratch = [
        pltpu.VMEM((total // 2, HD), f32),
        pltpu.VMEM((total // 2, HD), f32),
        pltpu.VMEM((2, cols, HD), b16),
    ]
    return pl.pallas_call(
        functools.partial(bwd_kernel, stretch, side),
        out_shape=(shape(sums, f32) if side else shape((2 * stretch, QPG * HD), b16), terms),
        in_specs=[SMEM] + [VMEM] * 6 + [VMEM, ANY][:len(partial)],
        out_specs=[VMEM] * 2,
        scratch_shapes=scratch if side else [pltpu.VMEM(sums, f32)] + scratch,
        compiler_params=pltpu.CompilerParams(vmem_limit_bytes=32 * MIB),
        cost_estimate=pl.CostEstimate(flops=BWD_FLOPS, bytes_accessed=8 * 10**6, transcendentals=0),
        name="attention_backward_%d" % side,
    )(plan, probs, kv, qs, ds, delta, inverse, *partial)


def ahead(block, axis, step):
    count = lax.axis_size(axis)
    return lax.ppermute(block, axis, [(i, (i + step) % count) for i in range(count)])


def behind(block, axis, step):
    count = lax.axis_size(axis)
    return lax.ppermute(block, axis, [((i + step) % count, i) for i in range(count)])


def across(block, axis, step):
    count = lax.axis_size(axis)
    return lax.ppermute(block, axis, [(i, i ^ step) for i in range(count)])


def total_of(parts):
    total = parts[0].astype(jnp.float32)
    for part in parts[1:]:
        total = total + part.astype(jnp.float32)
    return total.astype(jnp.bfloat16)


def on_device(queries, keys, values, stretch_of, out_weight, grad_heads):
    kv = pair(keys, values)
    qs, ds, same = by_heads(queries, grad_heads, kv)
    plan = plan_of(stretch_of)
    kv = stack(qs, same, *[across(kv, "zl", step) for step in range(1, NZ)])
    pieces = [kv] + [behind(kv, "x", step) for step in range(1, NX)]
    pieces = pieces + [across(piece, "core", 1) for piece in pieces]
    own, front, back, far_a, far_b, probs, kv, delta, inverse = forward(plan, qs, ds, pieces, out_weight)
    saved = (plan, probs, kv, qs, ds, delta, inverse)
    far_a, far_b = ahead(far_a, "y", 1), ahead(far_b, "y", NY - 1)
    partial, give = backward(1, *saved)
    front, back = relay(front, back, far_a, far_b)
    mixed = total_of([own, ahead(front, "y", 1), ahead(back, "y", NY - 1)])
    rows = mixed.shape[0] // NH
    mixed = total_of([mixed[:rows], across(mixed[rows:], "zh", 1)])
    q_grad, keep = backward(0, *saved, partial, front)
    term = total_of([keep, across(give, "core", 1)])
    part = term.shape[0] // NX
    term = total_of([term[:part]] + [
        ahead(term[step * part:(step + 1) * part], "x", step) for step in range(1, NX)])
    part = term.shape[0] // NZ
    term = total_of([term[:part]] + [
        across(term[step * part:(step + 1) * part], "zl", step) for step in range(1, NZ)])
    return mixed, q_grad, term[:, :HD], term[:, HD:]


def solution(mesh):
    fine = Mesh(mesh.devices.reshape(NX, NZ, NC, NH, NY), CTX + TP)
    return jax.shard_map(
        on_device,
        mesh=fine,
        in_specs=(P(CTX, TP), P(CTX, TP), P(CTX, TP), P(), P(TP, None), P(CTX, TP)),
        out_specs=(P(CTX + TP, None), P(CTX, TP), P(CTX, TP), P(CTX, TP)),
        check_vma=False,
    )
```

```python
import functools
import jax
import jax.numpy as jnp
from jax import lax
from jax.experimental import pallas as pl
from jax.experimental.pallas import tpu as pltpu
from jax.sharding import Mesh, PartitionSpec as P

HD = 128
QPG = 4
NEG = -1e30
SCALE = HD ** (-0.5)
NT = (((1,), (1,)), ((), ()))
NN = (((1,), (0,)), ((), ()))
TN = (((0,), (0,)), ((), ()))
MIB = 1024 * 1024
NX, NZ, NC, NH, NY = 4, 4, 2, 2, 4
CTX = ("x", "zl", "core")
TP = ("zh", "y")
MIX_SPAN = 1024
CHUNK = 4
FWD_MIB = 32
BWD_FLOPS = 2 * 10**10
SMEM = pl.BlockSpec(memory_space=pltpu.SMEM)
VMEM = pl.BlockSpec(memory_space=pltpu.VMEM)
HBM = pl.BlockSpec(memory_space=pltpu.HBM)
ANY = pl.BlockSpec(memory_space=pl.ANY)


def dot(a, b, dims):
    return lax.dot_general(a, b, dims, preferred_element_type=jnp.float32)


def slot_of(x, zl, core, half):
    return ((x * NZ + zl) * NC + core) * 2 + half


def place_of(c_step, x_step, z_step):
    x, zl, core = (lax.axis_index(name) for name in CTX)
    return slot_of(lax.rem(x + x_step, NX), jnp.bitwise_xor(zl, z_step), jnp.bitwise_xor(core, c_step), 0)


def pair_kernel(k_hbm, v_hbm, kv_ref, sem):
    copies = [pltpu.make_async_copy(k_hbm, kv_ref.at[:, :HD], sem.at[0]),
              pltpu.make_async_copy(v_hbm, kv_ref.at[:, HD:], sem.at[1])]
    for copy in copies:
        copy.start()
    for copy in copies:
        copy.wait()


def heads_kernel(q_hbm, do_hbm, kv_ref, qs_ref, ds_ref, same_ref, sem):
    stretch = q_hbm.shape[0] // 2
    copies = []
    for which, (source, target) in enumerate(((q_hbm, qs_ref), (do_hbm, ds_ref))):
        for part in range(2):
            for head in range(QPG):
                copies.append(pltpu.make_async_copy(
                    source.at[part * stretch:(part + 1) * stretch, head * HD:(head + 1) * HD],
                    target.at[part, head * stretch:(head + 1) * stretch, :],
                    sem.at[which, part, head]))
    for copy in copies:
        copy.start()
    same_ref[...] = kv_ref[...]
    for copy in copies:
        copy.wait()


def stage_kernel(ids_ref, piece_ref, plan_ref, same_ref, slot_ref):
    same_ref[...] = piece_ref[...]
    slots = ids_ref.shape[0]
    core = lax.axis_index("core")
    mine = place_of(0, 0, 0)
    own = [ids_ref[mine], ids_ref[mine + 1]]
    for slot in range(slots):
        slot_ref[ids_ref[slot]] = jnp.int32(slot)
    near, far, *seen = (jnp.int32(0),) * 6
    for value in range(slots):
        slot = slot_ref[value]
        away = jnp.bitwise_xor(lax.rem(slot // 2, NC), core)
        at = jnp.where(away == 0, near, slots // 2 + far)
        plan_ref[slot] = at
        plan_ref[slots + at] = jnp.int32(value)
        near, far = near + (1 - away), far + away
        seen = [before + jnp.where((own[part] >= value) & (away == side), 1, 0)
                for before, (side, part) in zip(seen, ((0, 0), (0, 1), (1, 0), (1, 1)))]
    for index in range(4):
        plan_ref[2 * slots + index] = (seen[index] + CHUNK - 1) // CHUNK
    for part in range(2):
        plan_ref[2 * slots + 4 + part] = own[part]


class Plan:
    def __init__(self, ref, slots, stretch):
        self.ref, self.slots, self.stretch = ref, slots, stretch
        self.span = CHUNK * stretch

    def row(self, slot):
        return pl.multiple_of(self.ref[slot] * self.stretch, self.stretch)

    def step(self, side, index):
        first = self.ref[2 * self.slots + 2 * side]
        count = first + self.ref[2 * self.slots + 2 * side + 1]
        late = index >= first
        part = jnp.where(late, 1, 0)
        last = self.slots // 2 // CHUNK - 1
        chunk = jnp.minimum(index - part * first, last)
        row = pl.multiple_of(chunk * self.span, self.span)
        return part, row, chunk, index < count

    def limits(self, side, part, chunk, valid):
        own = self.ref[2 * self.slots + 4 + part]
        at = self.slots + side * (self.slots // 2) + chunk * CHUNK
        return [jnp.where(valid, (own - self.ref[at + group]) * self.stretch, -2 * self.stretch)
                for group in range(CHUNK)]


def attend(stretch, side, plan_ref, qs_ref, pieces, p_ref, kv_ref, top_ref, sum_ref, acc_ref, s_buf, diff_ref):
    steps, span, cols = p_ref.shape
    rows = kv_ref.shape[0]
    plan = Plan(plan_ref, 2 * rows // stretch, stretch)
    for x_step in range(NX):
        for z_step in range(NZ):
            slot = place_of(side, x_step, z_step)
            for half in range(2):
                at = (z_step * 2 + half) * stretch
                kv_ref[pl.ds(plan.row(slot + half) - side * rows, stretch), :] = pieces[x_step][at:at + stretch, :]
    k_at = lax.broadcasted_iota(jnp.int32, (stretch, cols), 0)
    q_at = lax.broadcasted_iota(jnp.int32, (stretch, cols), 1) % stretch
    diff_ref[...] = k_at - q_at
    top_ref[...] = jnp.full_like(top_ref, NEG)
    sum_ref[...] = jnp.zeros_like(sum_ref)
    acc_ref[...] = jnp.zeros_like(acc_ref)

    for index in range(steps):
        part, row, chunk, valid = plan.step(side, index)
        scores = dot(kv_ref[pl.ds(row, span), :HD], qs_ref[part], NT)
        top = top_ref[part]
        for group, limit in enumerate(plan.limits(side, part, chunk, valid)):
            at = slice(group * stretch, (group + 1) * stretch)
            block = jnp.where(diff_ref[...] <= limit, scores[at], NEG)
            s_buf[index, at] = block
            top = jnp.maximum(top, jnp.max(block.reshape(stretch // 8, 8, cols), axis=0))
        top_ref[part] = top
    for part in range(2):
        top_ref[part] = jnp.broadcast_to(jnp.max(top_ref[part], axis=0, keepdims=True), (8, cols))

    for index in range(steps):
        part, row, chunk, valid = plan.step(side, index)
        shifted = jnp.exp((s_buf[index].reshape(span // 8, 8, cols) - top_ref[part][None]) * SCALE)
        sum_ref[part] += jnp.sum(shifted, axis=0)
        weights = shifted.reshape(span, cols).astype(jnp.bfloat16)
        p_ref[index] = weights
        acc_ref[part] += dot(kv_ref[pl.ds(row, span), HD:], weights, TN)


def near_kernel(stretch, plan_ref, qs_ref, *rest):
    attend(stretch, 0, plan_ref, qs_ref, rest[:NX], *rest[NX:])


def far_kernel(stretch, plan_ref, qs_ref, *rest):
    pieces, rest = rest[:NX], rest[NX:]
    (ds_ref, w_ref, near_top, near_sum, near_acc,
     own_ref, front_ref, back_ref, far_a, far_b, p_ref, kv_ref, delta_ref, near_inv, far_inv,
     top_ref, sum_ref, acc_ref, s_buf, diff_ref, attn_ref, turned_ref) = rest
    attend(stretch, 1, plan_ref, qs_ref, pieces, p_ref, kv_ref, top_ref, sum_ref, acc_ref, s_buf, diff_ref)
    cols = qs_ref.shape[1]
    for part in range(2):
        top = jnp.maximum(near_top[part][:1], top_ref[part][:1])
        near = jnp.exp((near_top[part][:1] - top) * SCALE)
        far = jnp.exp((top_ref[part][:1] - top) * SCALE)
        total = (jnp.sum(near_sum[part], axis=0, keepdims=True) * near
                 + jnp.sum(sum_ref[part], axis=0, keepdims=True) * far)
        near, far = near / total, far / total
        near_inv[part] = jnp.broadcast_to(near, (8, cols))
        far_inv[part] = jnp.broadcast_to(far, (8, cols))
        out = (near_acc[part] * near + acc_ref[part] * far).T.astype(jnp.bfloat16)
        prod = ds_ref[part].astype(jnp.float32) * out.astype(jnp.float32)
        delta_ref[part] = jnp.broadcast_to(jnp.sum(prod.T, axis=0, keepdims=True), (8, cols))
        for head in range(QPG):
            attn_ref[part * stretch:(part + 1) * stretch, head * HD:(head + 1) * HD] = (
                out[head * stretch:(head + 1) * stretch])
    rows = attn_ref.shape[0] // (NH * NY)
    zh, y = lax.axis_index("zh"), lax.axis_index("y")
    for y_step in range(NY):
        for h_step in range(NH):
            block = jnp.bitwise_xor(zh, h_step) * NY + lax.rem(y + y_step, NY)
            to = (y_step * NH + h_step) * rows
            turned_ref[to:to + rows, :] = attn_ref[pl.ds(pl.multiple_of(block * rows, rows), rows), :]
    piece = NH * rows
    half = w_ref.shape[1] // 2
    for index in range(w_ref.shape[1] // MIX_SPAN):
        at = slice(index * MIX_SPAN, (index + 1) * MIX_SPAN)
        mixed = dot(turned_ref[...], w_ref[:, at], NN).astype(jnp.bfloat16)
        own_ref[:, at] = mixed[:piece]
        front_ref[:, at] = mixed[piece:2 * piece]
        back_ref[:, at] = mixed[3 * piece:]
        if at.start < half:
            far_a[:, at] = mixed[2 * piece:3 * piece]
        else:
            far_b[:, at.start - half:at.stop - half] = mixed[2 * piece:3 * piece]


def bwd_kernel(stretch, side, plan_ref, p_ref, kv_ref, qs_ref, ds_ref, delta_ref, inv_ref, *rest):
    steps, span, cols = p_ref.shape
    total = 2 * kv_ref.shape[0]
    plan = Plan(plan_ref, total // stretch, stretch)
    if side == 0:
        acc_in, dq_ref, out_ref, acc_ref, dk_ref, dv_ref, dn_ref = rest
        acc_ref[...] = acc_in[...]
    else:
        acc_ref, out_ref, dk_ref, dv_ref, dn_ref = rest
        acc_ref[...] = jnp.zeros_like(acc_ref)
    dk_ref[...] = jnp.zeros_like(dk_ref)
    dv_ref[...] = jnp.zeros_like(dv_ref)
    for part in range(2):
        column = jnp.broadcast_to(inv_ref[part][:1], (HD, cols)).T
        dn_ref[part] = (ds_ref[part].astype(jnp.float32) * column).astype(jnp.bfloat16)

    for index in range(steps):
        part, row, chunk, valid = plan.step(side, index)
        here = pl.ds(row, span)
        weights = p_ref[index]
        grad_probs = dot(kv_ref[here, HD:], ds_ref[part], NT)
        moved = (grad_probs.reshape(span // 8, 8, cols) - delta_ref[part][None]) * inv_ref[part][None]
        grad_scores = (weights.astype(jnp.float32) * moved.reshape(span, cols)).astype(jnp.bfloat16)
        dv_ref[here, :] += dot(weights, dn_ref[part], NN)
        dk_ref[here, :] += dot(grad_scores, qs_ref[part], NN)
        acc_ref[part] += dot(kv_ref[here, :HD], grad_scores, TN)

    to = 0
    for x_step in range(NX):
        for z_step in range(NZ):
            slot = place_of(side, x_step, z_step)
            for half in range(2):
                here = pl.ds(plan.row(slot + half) - side * (total // 2), stretch)
                out_ref[to:to + stretch, :HD] = (dk_ref[here, :] * SCALE).astype(jnp.bfloat16)
                out_ref[to:to + stretch, HD:] = dv_ref[here, :].astype(jnp.bfloat16)
                to += stretch
    if side == 0:
        for part in range(2):
            out = (acc_ref[part].T * SCALE).astype(jnp.bfloat16)
            for head in range(QPG):
                dq_ref[part * stretch:(part + 1) * stretch, head * HD:(head + 1) * HD] = (
                    out[head * stretch:(head + 1) * stretch])


def pair(keys, values):
    return pl.pallas_call(
        pair_kernel,
        out_shape=jax.ShapeDtypeStruct((keys.shape[0], 2 * HD), jnp.bfloat16),
        in_specs=[HBM] * 2,
        out_specs=VMEM,
        scratch_shapes=[pltpu.SemaphoreType.DMA((2,))],
        compiler_params=pltpu.CompilerParams(vmem_limit_bytes=60 * MIB),
        name="pair",
    )(keys, values)


def by_heads(queries, grad_heads, kv):
    shape = jax.ShapeDtypeStruct((2, QPG * queries.shape[0] // 2, HD), jnp.bfloat16)
    return pl.pallas_call(
        heads_kernel,
        out_shape=(shape, shape, jax.ShapeDtypeStruct(kv.shape, kv.dtype)),
        in_specs=[HBM] * 2 + [VMEM],
        out_specs=[VMEM] * 3,
        scratch_shapes=[pltpu.SemaphoreType.DMA((2, 2, QPG))],
        compiler_params=pltpu.CompilerParams(vmem_limit_bytes=4 * MIB),
        name="by_heads",
    )(queries, grad_heads, kv)


def stage(ids, piece):
    slots = ids.shape[0]
    shape = jax.ShapeDtypeStruct
    return pl.pallas_call(
        stage_kernel,
        out_shape=(shape((2 * slots + 8,), jnp.int32), shape(piece.shape, piece.dtype)),
        in_specs=[SMEM, VMEM],
        out_specs=[SMEM, VMEM],
        scratch_shapes=[pltpu.SMEM((slots,), jnp.int32)],
        compiler_params=pltpu.CompilerParams(vmem_limit_bytes=4 * MIB),
        name="stage",
    )(ids, piece)


def relay_kernel(front_in, back_in, front_add, back_add, front_ref, back_ref):
    half = front_add.shape[1]
    for index in range(2):
        at = slice(index * half // 2, (index + 1) * half // 2)
        front_ref[:, at] = (front_in[:, at].astype(jnp.float32) + front_add[:, at].astype(jnp.float32)
                            ).astype(jnp.bfloat16)
        to = slice(half + index * half // 2, half + (index + 1) * half // 2)
        back_ref[:, to] = (back_in[:, to].astype(jnp.float32) + back_add[:, at].astype(jnp.float32)
                           ).astype(jnp.bfloat16)


def relay(front, back, front_add, back_add):
    shape = jax.ShapeDtypeStruct(front.shape, front.dtype)
    return pl.pallas_call(
        relay_kernel,
        out_shape=(shape, shape),
        in_specs=[VMEM] * 4,
        out_specs=[VMEM] * 2,
        input_output_aliases={0: 0, 1: 1},
        compiler_params=pltpu.CompilerParams(vmem_limit_bytes=8 * MIB),
        name="relay",
    )(front, back, front_add, back_add)


def stack_kernel(token_ref, *refs):
    *parts, out_ref = refs
    rows = parts[0].shape[0]
    for index, part in enumerate(parts):
        out_ref[index * rows:(index + 1) * rows, :] = part[...]


def stack(token, *parts):
    rows, width = parts[0].shape
    return pl.pallas_call(
        stack_kernel,
        out_shape=jax.ShapeDtypeStruct((len(parts) * rows, width), parts[0].dtype),
        in_specs=[ANY] + [VMEM] * len(parts),
        out_specs=VMEM,
        compiler_params=pltpu.CompilerParams(vmem_limit_bytes=4 * MIB),
        name="stack",
    )(token, *parts)


def forward(side, plan, qs, pieces, *more):
    cols = qs.shape[1]
    stretch = cols // QPG
    tokens = 2 * stretch
    total = sum(piece.shape[0] for piece in pieces)
    span = CHUNK * stretch
    steps = total // span + 1
    b16, f32 = jnp.bfloat16, jnp.float32
    shape = jax.ShapeDtypeStruct
    weights, keys = shape((steps, span, cols), b16), shape((total, 2 * HD), b16)
    row, sums = (2, 8, cols), (2, HD, cols)
    scratch = [pltpu.VMEM((steps, span, cols), f32), pltpu.VMEM((stretch, cols), jnp.int32)]
    if side:
        width = more[1].shape[1]
        outs = (shape((tokens // NY, width), b16),) * 3 + (shape((tokens // NY, width // 2), b16),) * 2 + (
            weights, keys, shape(row, f32), shape(row, f32), shape(row, f32))
        scratch = [pltpu.VMEM(row, f32), pltpu.VMEM(row, f32), pltpu.VMEM(sums, f32)] + scratch + [
            pltpu.VMEM((tokens, QPG * HD), b16), pltpu.VMEM((tokens, QPG * HD), b16)]
    else:
        outs = (weights, keys, shape(row, f32), shape(row, f32), shape(sums, f32))
    return pl.pallas_call(
        functools.partial(far_kernel if side else near_kernel, stretch),
        out_shape=outs,
        in_specs=[SMEM] + [VMEM] * (1 + len(pieces) + len(more)),
        out_specs=[VMEM] * len(outs),
        scratch_shapes=scratch,
        compiler_params=pltpu.CompilerParams(vmem_limit_bytes=FWD_MIB * MIB),
        cost_estimate=pl.CostEstimate(flops=3 * 10**9, bytes_accessed=8 * 10**6, transcendentals=10**6),
        name="attention_forward_%d" % side,
    )(plan, qs, *pieces, *more)


def backward(side, plan, probs, kv, qs, ds, delta, inverse, *partial):
    total = 2 * kv.shape[0]
    steps, span, cols = probs.shape
    stretch = cols // QPG
    b16, f32 = jnp.bfloat16, jnp.float32
    shape = jax.ShapeDtypeStruct
    terms = shape((total // 2, 2 * HD), b16)
    sums = (2, HD, cols)
    scratch = [
        pltpu.VMEM((total // 2, HD), f32),
        pltpu.VMEM((total // 2, HD), f32),
        pltpu.VMEM((2, cols, HD), b16),
    ]
    return pl.pallas_call(
        functools.partial(bwd_kernel, stretch, side),
        out_shape=(shape(sums, f32) if side else shape((2 * stretch, QPG * HD), b16), terms),
        in_specs=[SMEM] + [VMEM] * (6 + len(partial)),
        out_specs=[VMEM] * 2,
        scratch_shapes=scratch if side else [pltpu.VMEM(sums, f32)] + scratch,
        compiler_params=pltpu.CompilerParams(vmem_limit_bytes=32 * MIB),
        cost_estimate=pl.CostEstimate(flops=BWD_FLOPS, bytes_accessed=8 * 10**6, transcendentals=0),
        name="attention_backward_%d" % side,
    )(plan, probs, kv, qs, ds, delta, inverse, *partial)


def ahead(block, axis, step):
    count = lax.axis_size(axis)
    return lax.ppermute(block, axis, [(i, (i + step) % count) for i in range(count)])


def behind(block, axis, step):
    count = lax.axis_size(axis)
    return lax.ppermute(block, axis, [((i + step) % count, i) for i in range(count)])


def across(block, axis, step):
    count = lax.axis_size(axis)
    return lax.ppermute(block, axis, [(i, i ^ step) for i in range(count)])


def total_of(parts):
    total = parts[0].astype(jnp.float32)
    for part in parts[1:]:
        total = total + part.astype(jnp.float32)
    return total.astype(jnp.bfloat16)


def on_device(queries, keys, values, stretch_of, out_weight, grad_heads):
    kv = pair(keys, values)
    qs, ds, same = by_heads(queries, grad_heads, kv)
    kv = stack(qs, same, *[across(kv, "zl", step) for step in range(1, NZ)])
    plan, same = stage(stretch_of, kv)
    near = [kv] + [behind(kv, "x", step) for step in range(1, NX)]
    far = [across(piece, "core", 1) for piece in [same] + near[1:]]
    near_probs, near_kv, *partial = forward(0, plan, qs, near)
    own, front, back, far_a, far_b, far_probs, far_kv, delta, near_inv, far_inv = forward(
        1, plan, qs, far, ds, out_weight, *partial)
    far_a, far_b = ahead(far_a, "y", 1), ahead(far_b, "y", NY - 1)
    partial, give = backward(1, plan, far_probs, far_kv, qs, ds, delta, far_inv)
    front, back = relay(front, back, far_a, far_b)
    mixed = total_of([own, ahead(front, "y", 1), ahead(back, "y", NY - 1)])
    rows = mixed.shape[0] // NH
    mixed = total_of([mixed[:rows], across(mixed[rows:], "zh", 1)])
    q_grad, keep = backward(0, plan, near_probs, near_kv, qs, ds, delta, near_inv, partial)
    term = total_of([keep, across(give, "core", 1)])
    part = term.shape[0] // NX
    term = total_of([term[:part]] + [
        ahead(term[step * part:(step + 1) * part], "x", step) for step in range(1, NX)])
    part = term.shape[0] // NZ
    term = total_of([term[:part]] + [
        across(term[step * part:(step + 1) * part], "zl", step) for step in range(1, NZ)])
    return mixed, q_grad, term[:, :HD], term[:, HD:]


def solution(mesh):
    fine = Mesh(mesh.devices.reshape(NX, NZ, NC, NH, NY), CTX + TP)
    return jax.shard_map(
        on_device,
        mesh=fine,
        in_specs=(P(CTX, TP), P(CTX, TP), P(CTX, TP), P(), P(TP, None), P(CTX, TP)),
        out_specs=(P(CTX + TP, None), P(CTX, TP), P(CTX, TP), P(CTX, TP)),
        check_vma=False,
    )
```

```python
import functools
import jax
import jax.numpy as jnp
from jax import lax
from jax.experimental import pallas as pl
from jax.experimental.pallas import tpu as pltpu
from jax.sharding import Mesh, PartitionSpec as P

HD = 128
QPG = 4
NEG = -1e30
SCALE = HD ** (-0.5)
NT = (((1,), (1,)), ((), ()))
NN = (((1,), (0,)), ((), ()))
TN = (((0,), (0,)), ((), ()))
MIB = 1024 * 1024
NX, NZ, NC, NH, NY = 4, 4, 2, 2, 4
CTX = ("x", "zl", "core")
TP = ("zh", "y")
MIX_SPAN = 1024
CHUNK = 4
FWD_MIB = 32
BWD_FLOPS = 2 * 10**10
SMEM = pl.BlockSpec(memory_space=pltpu.SMEM)
VMEM = pl.BlockSpec(memory_space=pltpu.VMEM)
HBM = pl.BlockSpec(memory_space=pltpu.HBM)
ANY = pl.BlockSpec(memory_space=pl.ANY)


def dot(a, b, dims):
    return lax.dot_general(a, b, dims, preferred_element_type=jnp.float32)


def slot_of(x, zl, core, half):
    return ((x * NZ + zl) * NC + core) * 2 + half


def place_of(c_step, x_step, z_step):
    x, zl, core = (lax.axis_index(name) for name in CTX)
    return slot_of(lax.rem(x + x_step, NX), jnp.bitwise_xor(zl, z_step), jnp.bitwise_xor(core, c_step), 0)


def pair_kernel(k_hbm, v_hbm, kv_ref, sem):
    copies = [pltpu.make_async_copy(k_hbm, kv_ref.at[:, :HD], sem.at[0]),
              pltpu.make_async_copy(v_hbm, kv_ref.at[:, HD:], sem.at[1])]
    for copy in copies:
        copy.start()
    for copy in copies:
        copy.wait()


def heads_kernel(q_hbm, do_hbm, kv_ref, qs_ref, ds_ref, same_ref, sem):
    stretch = q_hbm.shape[0] // 2
    copies = []
    for which, (source, target) in enumerate(((q_hbm, qs_ref), (do_hbm, ds_ref))):
        for part in range(2):
            for head in range(QPG):
                copies.append(pltpu.make_async_copy(
                    source.at[part * stretch:(part + 1) * stretch, head * HD:(head + 1) * HD],
                    target.at[part, head * stretch:(head + 1) * stretch, :],
                    sem.at[which, part, head]))
    for copy in copies:
        copy.start()
    same_ref[...] = kv_ref[...]
    for copy in copies:
        copy.wait()


def stage_kernel(ids_ref, piece_ref, plan_ref, same_ref, slot_ref):
    same_ref[...] = piece_ref[...]
    slots = ids_ref.shape[0]
    core = lax.axis_index("core")
    mine = place_of(0, 0, 0)
    own = [ids_ref[mine], ids_ref[mine + 1]]
    for slot in range(slots):
        slot_ref[ids_ref[slot]] = jnp.int32(slot)
    near, far, *seen = (jnp.int32(0),) * 6
    for value in range(slots):
        slot = slot_ref[value]
        away = jnp.bitwise_xor(lax.rem(slot // 2, NC), core)
        at = jnp.where(away == 0, near, slots // 2 + far)
        plan_ref[slot] = at
        plan_ref[slots + at] = jnp.int32(value)
        near, far = near + (1 - away), far + away
        seen = [before + jnp.where((own[part] >= value) & (away == side), 1, 0)
                for before, (side, part) in zip(seen, ((0, 0), (0, 1), (1, 0), (1, 1)))]
    for index in range(4):
        plan_ref[2 * slots + index] = (seen[index] + CHUNK - 1) // CHUNK
    for part in range(2):
        plan_ref[2 * slots + 4 + part] = own[part]


class Plan:
    def __init__(self, ref, slots, stretch):
        self.ref, self.slots, self.stretch = ref, slots, stretch
        self.span = CHUNK * stretch

    def row(self, slot):
        return pl.multiple_of(self.ref[slot] * self.stretch, self.stretch)

    def step(self, side, index):
        first = self.ref[2 * self.slots + 2 * side]
        count = first + self.ref[2 * self.slots + 2 * side + 1]
        late = index >= first
        part = jnp.where(late, 1, 0)
        last = self.slots // 2 // CHUNK - 1
        chunk = jnp.minimum(index - part * first, last)
        row = pl.multiple_of(chunk * self.span, self.span)
        return part, row, chunk, index < count

    def limits(self, side, part, chunk, valid):
        own = self.ref[2 * self.slots + 4 + part]
        at = self.slots + side * (self.slots // 2) + chunk * CHUNK
        return [jnp.where(valid, (own - self.ref[at + group]) * self.stretch, -2 * self.stretch)
                for group in range(CHUNK)]


def attend(stretch, side, plan_ref, qs_ref, pieces, p_ref, kv_ref, top_ref, sum_ref, acc_ref, s_buf, diff_ref):
    steps, span, cols = p_ref.shape
    rows = kv_ref.shape[0]
    plan = Plan(plan_ref, 2 * rows // stretch, stretch)
    for x_step in range(NX):
        for z_step in range(NZ):
            slot = place_of(side, x_step, z_step)
            for half in range(2):
                at = (z_step * 2 + half) * stretch
                kv_ref[pl.ds(plan.row(slot + half) - side * rows, stretch), :] = pieces[x_step][at:at + stretch, :]
    k_at = lax.broadcasted_iota(jnp.int32, (stretch, cols), 0)
    q_at = lax.broadcasted_iota(jnp.int32, (stretch, cols), 1) % stretch
    diff_ref[...] = k_at - q_at
    top_ref[...] = jnp.full_like(top_ref, NEG)
    sum_ref[...] = jnp.zeros_like(sum_ref)
    acc_ref[...] = jnp.zeros_like(acc_ref)

    for index in range(steps):
        part, row, chunk, valid = plan.step(side, index)
        scores = dot(kv_ref[pl.ds(row, span), :HD], qs_ref[part], NT)
        top = top_ref[part]
        for group, limit in enumerate(plan.limits(side, part, chunk, valid)):
            at = slice(group * stretch, (group + 1) * stretch)
            block = jnp.where(diff_ref[...] <= limit, scores[at], NEG)
            s_buf[index, at] = block
            top = jnp.maximum(top, jnp.max(block.reshape(stretch // 8, 8, cols), axis=0))
        top_ref[part] = top
    for part in range(2):
        top_ref[part] = jnp.broadcast_to(jnp.max(top_ref[part], axis=0, keepdims=True), (8, cols))

    for index in range(steps):
        part, row, chunk, valid = plan.step(side, index)
        shifted = jnp.exp((s_buf[index].reshape(span // 8, 8, cols) - top_ref[part][None]) * SCALE)
        sum_ref[part] += jnp.sum(shifted, axis=0)
        weights = shifted.reshape(span, cols).astype(jnp.bfloat16)
        p_ref[index] = weights
        acc_ref[part] += dot(kv_ref[pl.ds(row, span), HD:], weights, TN)


def near_kernel(stretch, plan_ref, qs_ref, *rest):
    attend(stretch, 0, plan_ref, qs_ref, rest[:NX], *rest[NX:])


def far_kernel(stretch, plan_ref, qs_ref, *rest):
    pieces, rest = rest[:NX], rest[NX:]
    (ds_ref, w_ref, near_top, near_sum, near_acc,
     own_ref, front_ref, back_ref, ahead_ref, behind_ref, p_ref, kv_ref, delta_ref, near_inv, far_inv,
     top_ref, sum_ref, acc_ref, s_buf, diff_ref, attn_ref, turned_ref) = rest
    attend(stretch, 1, plan_ref, qs_ref, pieces, p_ref, kv_ref, top_ref, sum_ref, acc_ref, s_buf, diff_ref)
    cols = qs_ref.shape[1]
    for part in range(2):
        top = jnp.maximum(near_top[part][:1], top_ref[part][:1])
        near = jnp.exp((near_top[part][:1] - top) * SCALE)
        far = jnp.exp((top_ref[part][:1] - top) * SCALE)
        total = (jnp.sum(near_sum[part], axis=0, keepdims=True) * near
                 + jnp.sum(sum_ref[part], axis=0, keepdims=True) * far)
        near, far = near / total, far / total
        near_inv[part] = jnp.broadcast_to(near, (8, cols))
        far_inv[part] = jnp.broadcast_to(far, (8, cols))
        out = (near_acc[part] * near + acc_ref[part] * far).T.astype(jnp.bfloat16)
        prod = ds_ref[part].astype(jnp.float32) * out.astype(jnp.float32)
        delta_ref[part] = jnp.broadcast_to(jnp.sum(prod.T, axis=0, keepdims=True), (8, cols))
        for head in range(QPG):
            attn_ref[part * stretch:(part + 1) * stretch, head * HD:(head + 1) * HD] = (
                out[head * stretch:(head + 1) * stretch])
    rows = attn_ref.shape[0] // (NH * NY)
    zh, y = lax.axis_index("zh"), lax.axis_index("y")
    for y_step in range(NY):
        for h_step in range(NH):
            block = jnp.bitwise_xor(zh, h_step) * NY + lax.rem(y + y_step, NY)
            to = (y_step * NH + h_step) * rows
            turned_ref[to:to + rows, :] = attn_ref[pl.ds(pl.multiple_of(block * rows, rows), rows), :]
    piece = NH * rows
    half = w_ref.shape[1] // 2
    for index in range(w_ref.shape[1] // MIX_SPAN):
        at = slice(index * MIX_SPAN, (index + 1) * MIX_SPAN)
        mixed = dot(turned_ref[...], w_ref[:, at], NN).astype(jnp.bfloat16)
        own_ref[:, at] = mixed[:piece]
        if at.start < half:
            ahead_ref[:, at] = mixed[2 * piece:3 * piece]
            behind_ref[:, at] = mixed[3 * piece:]
            front_ref[:, at] = mixed[piece:2 * piece]
        else:
            ahead_ref[:, at] = mixed[piece:2 * piece]
            behind_ref[:, at] = mixed[2 * piece:3 * piece]
            back_ref[:, at.start - half:at.stop - half] = mixed[3 * piece:]


def bwd_kernel(stretch, side, plan_ref, p_ref, kv_ref, qs_ref, ds_ref, delta_ref, inv_ref, *rest):
    steps, span, cols = p_ref.shape
    total = 2 * kv_ref.shape[0]
    plan = Plan(plan_ref, total // stretch, stretch)
    if side == 0:
        acc_in, dq_ref, out_ref, acc_ref, dk_ref, dv_ref, dn_ref = rest
        acc_ref[...] = acc_in[...]
    else:
        acc_ref, out_ref, dk_ref, dv_ref, dn_ref = rest
        acc_ref[...] = jnp.zeros_like(acc_ref)
    dk_ref[...] = jnp.zeros_like(dk_ref)
    dv_ref[...] = jnp.zeros_like(dv_ref)
    for part in range(2):
        column = jnp.broadcast_to(inv_ref[part][:1], (HD, cols)).T
        dn_ref[part] = (ds_ref[part].astype(jnp.float32) * column).astype(jnp.bfloat16)

    for index in range(steps):
        part, row, chunk, valid = plan.step(side, index)
        here = pl.ds(row, span)
        weights = p_ref[index]
        grad_probs = dot(kv_ref[here, HD:], ds_ref[part], NT)
        moved = (grad_probs.reshape(span // 8, 8, cols) - delta_ref[part][None]) * inv_ref[part][None]
        grad_scores = (weights.astype(jnp.float32) * moved.reshape(span, cols)).astype(jnp.bfloat16)
        dv_ref[here, :] += dot(weights, dn_ref[part], NN)
        dk_ref[here, :] += dot(grad_scores, qs_ref[part], NN)
        acc_ref[part] += dot(kv_ref[here, :HD], grad_scores, TN)

    to = 0
    for x_step in range(NX):
        for z_step in range(NZ):
            slot = place_of(side, x_step, z_step)
            for half in range(2):
                here = pl.ds(plan.row(slot + half) - side * (total // 2), stretch)
                out_ref[to:to + stretch, :HD] = (dk_ref[here, :] * SCALE).astype(jnp.bfloat16)
                out_ref[to:to + stretch, HD:] = dv_ref[here, :].astype(jnp.bfloat16)
                to += stretch
    if side == 0:
        for part in range(2):
            out = (acc_ref[part].T * SCALE).astype(jnp.bfloat16)
            for head in range(QPG):
                dq_ref[part * stretch:(part + 1) * stretch, head * HD:(head + 1) * HD] = (
                    out[head * stretch:(head + 1) * stretch])


def pair(keys, values):
    return pl.pallas_call(
        pair_kernel,
        out_shape=jax.ShapeDtypeStruct((keys.shape[0], 2 * HD), jnp.bfloat16),
        in_specs=[HBM] * 2,
        out_specs=VMEM,
        scratch_shapes=[pltpu.SemaphoreType.DMA((2,))],
        compiler_params=pltpu.CompilerParams(vmem_limit_bytes=60 * MIB),
        name="pair",
    )(keys, values)


def by_heads(queries, grad_heads, kv):
    shape = jax.ShapeDtypeStruct((2, QPG * queries.shape[0] // 2, HD), jnp.bfloat16)
    return pl.pallas_call(
        heads_kernel,
        out_shape=(shape, shape, jax.ShapeDtypeStruct(kv.shape, kv.dtype)),
        in_specs=[HBM] * 2 + [VMEM],
        out_specs=[VMEM] * 3,
        scratch_shapes=[pltpu.SemaphoreType.DMA((2, 2, QPG))],
        compiler_params=pltpu.CompilerParams(vmem_limit_bytes=4 * MIB),
        name="by_heads",
    )(queries, grad_heads, kv)


def stage(ids, piece):
    slots = ids.shape[0]
    shape = jax.ShapeDtypeStruct
    return pl.pallas_call(
        stage_kernel,
        out_shape=(shape((2 * slots + 8,), jnp.int32), shape(piece.shape, piece.dtype)),
        in_specs=[SMEM, VMEM],
        out_specs=[SMEM, VMEM],
        scratch_shapes=[pltpu.SMEM((slots,), jnp.int32)],
        compiler_params=pltpu.CompilerParams(vmem_limit_bytes=4 * MIB),
        name="stage",
    )(ids, piece)


def added(*parts):
    total = parts[0].astype(jnp.float32)
    for part in parts[1:]:
        total = total + part.astype(jnp.float32)
    return total.astype(jnp.bfloat16)


def relay_kernel(front_in, back_in, ahead_in, behind_in, token_ref, front_ref, back_ref):
    half = front_in.shape[1]
    for index in range(half // MIX_SPAN):
        at = slice(index * MIX_SPAN, (index + 1) * MIX_SPAN)
        front_ref[:, at] = added(front_in[:, at], ahead_in[:, at])
        back_ref[:, at] = added(back_in[:, at], behind_in[:, half + at.start:half + at.stop])


def relay(front, back, from_behind, from_ahead, token):
    shape = jax.ShapeDtypeStruct(front.shape, front.dtype)
    return pl.pallas_call(
        relay_kernel,
        out_shape=(shape, shape),
        in_specs=[VMEM] * 4 + [ANY],
        out_specs=[VMEM] * 2,
        compiler_params=pltpu.CompilerParams(vmem_limit_bytes=8 * MIB),
        name="relay",
    )(front, back, from_behind, from_ahead, token)


def settle_kernel(own, from_behind, from_ahead, front, back, keep_ref, give_ref):
    half = front.shape[1]
    rows = keep_ref.shape[0]
    for index in range(half // MIX_SPAN):
        at = slice(index * MIX_SPAN, (index + 1) * MIX_SPAN)
        to = slice(half + at.start, half + at.stop)
        for where, total in ((at, added(own[:, at], front[:, at], from_ahead[:, at])),
                             (to, added(own[:, to], back[:, at], from_behind[:, to]))):
            keep_ref[:, where] = total[:rows]
            give_ref[:, where] = total[rows:]


def settle(own, from_behind, from_ahead, front, back):
    shape = jax.ShapeDtypeStruct((own.shape[0] // NH, own.shape[1]), own.dtype)
    return pl.pallas_call(
        settle_kernel,
        out_shape=(shape, shape),
        in_specs=[VMEM] * 5,
        out_specs=[VMEM] * 2,
        compiler_params=pltpu.CompilerParams(vmem_limit_bytes=8 * MIB),
        name="settle",
    )(own, from_behind, from_ahead, front, back)


def stack_kernel(token_ref, *refs):
    *parts, out_ref = refs
    rows = parts[0].shape[0]
    for index, part in enumerate(parts):
        out_ref[index * rows:(index + 1) * rows, :] = part[...]


def stack(token, *parts):
    rows, width = parts[0].shape
    return pl.pallas_call(
        stack_kernel,
        out_shape=jax.ShapeDtypeStruct((len(parts) * rows, width), parts[0].dtype),
        in_specs=[ANY] + [VMEM] * len(parts),
        out_specs=VMEM,
        compiler_params=pltpu.CompilerParams(vmem_limit_bytes=4 * MIB),
        name="stack",
    )(token, *parts)


def forward(side, plan, qs, pieces, *more):
    cols = qs.shape[1]
    stretch = cols // QPG
    tokens = 2 * stretch
    total = sum(piece.shape[0] for piece in pieces)
    span = CHUNK * stretch
    steps = total // span + 1
    b16, f32 = jnp.bfloat16, jnp.float32
    shape = jax.ShapeDtypeStruct
    weights, keys = shape((steps, span, cols), b16), shape((total, 2 * HD), b16)
    row, sums = (2, 8, cols), (2, HD, cols)
    scratch = [pltpu.VMEM((steps, span, cols), f32), pltpu.VMEM((stretch, cols), jnp.int32)]
    if side:
        width = more[1].shape[1]
        outs = (shape((tokens // NY, width), b16),) + (shape((tokens // NY, width // 2), b16),) * 2 + (
            shape((tokens // NY, width), b16),) * 2 + (
            weights, keys, shape(row, f32), shape(row, f32), shape(row, f32))
        scratch = [pltpu.VMEM(row, f32), pltpu.VMEM(row, f32), pltpu.VMEM(sums, f32)] + scratch + [
            pltpu.VMEM((tokens, QPG * HD), b16), pltpu.VMEM((tokens, QPG * HD), b16)]
    else:
        outs = (weights, keys, shape(row, f32), shape(row, f32), shape(sums, f32))
    return pl.pallas_call(
        functools.partial(far_kernel if side else near_kernel, stretch),
        out_shape=outs,
        in_specs=[SMEM] + [VMEM] * (1 + len(pieces) + len(more)),
        out_specs=[VMEM] * len(outs),
        scratch_shapes=scratch,
        compiler_params=pltpu.CompilerParams(vmem_limit_bytes=FWD_MIB * MIB),
        cost_estimate=pl.CostEstimate(flops=3 * 10**9, bytes_accessed=8 * 10**6, transcendentals=10**6),
        name="attention_forward_%d" % side,
    )(plan, qs, *pieces, *more)


def backward(side, plan, probs, kv, qs, ds, delta, inverse, *partial):
    total = 2 * kv.shape[0]
    steps, span, cols = probs.shape
    stretch = cols // QPG
    b16, f32 = jnp.bfloat16, jnp.float32
    shape = jax.ShapeDtypeStruct
    terms = shape((total // 2, 2 * HD), b16)
    sums = (2, HD, cols)
    scratch = [
        pltpu.VMEM((total // 2, HD), f32),
        pltpu.VMEM((total // 2, HD), f32),
        pltpu.VMEM((2, cols, HD), b16),
    ]
    return pl.pallas_call(
        functools.partial(bwd_kernel, stretch, side),
        out_shape=(shape(sums, f32) if side else shape((2 * stretch, QPG * HD), b16), terms),
        in_specs=[SMEM] + [VMEM] * (6 + len(partial)),
        out_specs=[VMEM] * 2,
        scratch_shapes=scratch if side else [pltpu.VMEM(sums, f32)] + scratch,
        compiler_params=pltpu.CompilerParams(vmem_limit_bytes=32 * MIB),
        cost_estimate=pl.CostEstimate(flops=BWD_FLOPS, bytes_accessed=8 * 10**6, transcendentals=0),
        name="attention_backward_%d" % side,
    )(plan, probs, kv, qs, ds, delta, inverse, *partial)


def ahead(block, axis, step):
    count = lax.axis_size(axis)
    return lax.ppermute(block, axis, [(i, (i + step) % count) for i in range(count)])


def behind(block, axis, step):
    count = lax.axis_size(axis)
    return lax.ppermute(block, axis, [((i + step) % count, i) for i in range(count)])


def across(block, axis, step):
    count = lax.axis_size(axis)
    return lax.ppermute(block, axis, [(i, i ^ step) for i in range(count)])


def total_of(parts):
    total = parts[0].astype(jnp.float32)
    for part in parts[1:]:
        total = total + part.astype(jnp.float32)
    return total.astype(jnp.bfloat16)


def on_device(queries, keys, values, stretch_of, out_weight, grad_heads):
    kv = pair(keys, values)
    qs, ds, same = by_heads(queries, grad_heads, kv)
    kv = stack(qs, same, *[across(kv, "zl", step) for step in range(1, NZ)])
    plan, same = stage(stretch_of, kv)
    near = [kv] + [behind(kv, "x", step) for step in range(1, NX)]
    far = [across(piece, "core", 1) for piece in [same] + near[1:]]
    near_probs, near_kv, *partial = forward(0, plan, qs, near)
    own, front, back, to_ahead, to_behind, far_probs, far_kv, delta, near_inv, far_inv = forward(
        1, plan, qs, far, ds, out_weight, *partial)
    from_behind, from_ahead = ahead(to_ahead, "y", 1), ahead(to_behind, "y", NY - 1)
    partial, give = backward(1, plan, far_probs, far_kv, qs, ds, delta, far_inv)
    q_grad, keep = backward(0, plan, near_probs, near_kv, qs, ds, delta, near_inv, partial)
    term = total_of([keep, across(give, "core", 1)])
    front, back = relay(front, back, from_behind, from_ahead, term)
    mixed, give = settle(own, from_behind, from_ahead, ahead(front, "y", 1), ahead(back, "y", NY - 1))
    mixed = total_of([mixed, across(give, "zh", 1)])
    part = term.shape[0] // NX
    term = total_of([term[:part]] + [
        ahead(term[step * part:(step + 1) * part], "x", step) for step in range(1, NX)])
    part = term.shape[0] // NZ
    term = total_of([term[:part]] + [
        across(term[step * part:(step + 1) * part], "zl", step) for step in range(1, NZ)])
    return mixed, q_grad, term[:, :HD], term[:, HD:]


def solution(mesh):
    fine = Mesh(mesh.devices.reshape(NX, NZ, NC, NH, NY), CTX + TP)
    return jax.shard_map(
        on_device,
        mesh=fine,
        in_specs=(P(CTX, TP), P(CTX, TP), P(CTX, TP), P(), P(TP, None), P(CTX, TP)),
        out_specs=(P(CTX + TP, None), P(CTX, TP), P(CTX, TP), P(CTX, TP)),
        check_vma=False,
    )
```

```python
import functools
import jax
import jax.numpy as jnp
from jax import lax
from jax.experimental import pallas as pl
from jax.experimental.pallas import tpu as pltpu
from jax.sharding import Mesh, PartitionSpec as P

HD = 128
QPG = 4
NEG = -1e30
SCALE = HD ** (-0.5)
NT = (((1,), (1,)), ((), ()))
NN = (((1,), (0,)), ((), ()))
TN = (((0,), (0,)), ((), ()))
MIB = 1024 * 1024
NX, NZ, NC, NH, NY = 4, 4, 2, 2, 4
CTX = ("x", "zl", "core")
TP = ("zh", "y")
MIX_SPAN = 1024
CHUNK = 4
FWD_MIB = 32
BWD_FLOPS = 2 * 10**10
SMEM = pl.BlockSpec(memory_space=pltpu.SMEM)
VMEM = pl.BlockSpec(memory_space=pltpu.VMEM)
HBM = pl.BlockSpec(memory_space=pltpu.HBM)
ANY = pl.BlockSpec(memory_space=pl.ANY)


def dot(a, b, dims):
    return lax.dot_general(a, b, dims, preferred_element_type=jnp.float32)


def slot_of(x, zl, core, half):
    return ((x * NZ + zl) * NC + core) * 2 + half


def place_of(c_step, x_step, z_step):
    x, zl, core = (lax.axis_index(name) for name in CTX)
    return slot_of(lax.rem(x + x_step, NX), jnp.bitwise_xor(zl, z_step), jnp.bitwise_xor(core, c_step), 0)


def pair_kernel(k_hbm, v_hbm, kv_ref, sem):
    copies = [pltpu.make_async_copy(k_hbm, kv_ref.at[:, :HD], sem.at[0]),
              pltpu.make_async_copy(v_hbm, kv_ref.at[:, HD:], sem.at[1])]
    for copy in copies:
        copy.start()
    for copy in copies:
        copy.wait()


def heads_kernel(q_hbm, do_hbm, kv_ref, qs_ref, ds_ref, same_ref, sem):
    stretch = q_hbm.shape[0] // 2
    copies = []
    for which, (source, target) in enumerate(((q_hbm, qs_ref), (do_hbm, ds_ref))):
        for part in range(2):
            for head in range(QPG):
                copies.append(pltpu.make_async_copy(
                    source.at[part * stretch:(part + 1) * stretch, head * HD:(head + 1) * HD],
                    target.at[part, head * stretch:(head + 1) * stretch, :],
                    sem.at[which, part, head]))
    for copy in copies:
        copy.start()
    same_ref[...] = kv_ref[...]
    for copy in copies:
        copy.wait()


def stage_kernel(ids_ref, piece_ref, plan_ref, same_ref, slot_ref):
    same_ref[...] = piece_ref[...]
    slots = ids_ref.shape[0]
    core = lax.axis_index("core")
    mine = place_of(0, 0, 0)
    own = [ids_ref[mine], ids_ref[mine + 1]]
    for slot in range(slots):
        slot_ref[ids_ref[slot]] = jnp.int32(slot)
    near, far, *seen = (jnp.int32(0),) * 6
    for value in range(slots):
        slot = slot_ref[value]
        away = jnp.bitwise_xor(lax.rem(slot // 2, NC), core)
        at = jnp.where(away == 0, near, slots // 2 + far)
        plan_ref[slot] = at
        plan_ref[slots + at] = jnp.int32(value)
        near, far = near + (1 - away), far + away
        seen = [before + jnp.where((own[part] >= value) & (away == side), 1, 0)
                for before, (side, part) in zip(seen, ((0, 0), (0, 1), (1, 0), (1, 1)))]
    for index in range(4):
        plan_ref[2 * slots + index] = (seen[index] + CHUNK - 1) // CHUNK
    for part in range(2):
        plan_ref[2 * slots + 4 + part] = own[part]


class Plan:
    def __init__(self, ref, slots, stretch):
        self.ref, self.slots, self.stretch = ref, slots, stretch
        self.span = CHUNK * stretch

    def row(self, slot):
        return pl.multiple_of(self.ref[slot] * self.stretch, self.stretch)

    def step(self, side, index):
        first = self.ref[2 * self.slots + 2 * side]
        count = first + self.ref[2 * self.slots + 2 * side + 1]
        late = index >= first
        part = jnp.where(late, 1, 0)
        last = self.slots // 2 // CHUNK - 1
        chunk = jnp.minimum(index - part * first, last)
        row = pl.multiple_of(chunk * self.span, self.span)
        return part, row, chunk, index < count

    def limits(self, side, part, chunk, valid):
        own = self.ref[2 * self.slots + 4 + part]
        at = self.slots + side * (self.slots // 2) + chunk * CHUNK
        return [jnp.where(valid, (own - self.ref[at + group]) * self.stretch, -2 * self.stretch)
                for group in range(CHUNK)]


def attend(stretch, side, plan_ref, qs_ref, pieces, p_ref, kv_ref, top_ref, sum_ref, acc_ref, s_buf, diff_ref):
    steps, span, cols = p_ref.shape
    rows = kv_ref.shape[0]
    plan = Plan(plan_ref, 2 * rows // stretch, stretch)
    for x_step in range(NX):
        for z_step in range(NZ):
            slot = place_of(side, x_step, z_step)
            for half in range(2):
                at = (z_step * 2 + half) * stretch
                kv_ref[pl.ds(plan.row(slot + half) - side * rows, stretch), :] = pieces[x_step][at:at + stretch, :]
    k_at = lax.broadcasted_iota(jnp.int32, (stretch, cols), 0)
    q_at = lax.broadcasted_iota(jnp.int32, (stretch, cols), 1) % stretch
    diff_ref[...] = k_at - q_at
    top_ref[...] = jnp.full_like(top_ref, NEG)
    sum_ref[...] = jnp.zeros_like(sum_ref)
    acc_ref[...] = jnp.zeros_like(acc_ref)

    for index in range(steps):
        part, row, chunk, valid = plan.step(side, index)
        scores = dot(kv_ref[pl.ds(row, span), :HD], qs_ref[part], NT)
        top = top_ref[part]
        for group, limit in enumerate(plan.limits(side, part, chunk, valid)):
            at = slice(group * stretch, (group + 1) * stretch)
            block = jnp.where(diff_ref[...] <= limit, scores[at], NEG)
            s_buf[index, at] = block
            top = jnp.maximum(top, jnp.max(block.reshape(stretch // 8, 8, cols), axis=0))
        top_ref[part] = top
    for part in range(2):
        top_ref[part] = jnp.broadcast_to(jnp.max(top_ref[part], axis=0, keepdims=True), (8, cols))

    for index in range(steps):
        part, row, chunk, valid = plan.step(side, index)
        shifted = jnp.exp((s_buf[index].reshape(span // 8, 8, cols) - top_ref[part][None]) * SCALE)
        sum_ref[part] += jnp.sum(shifted, axis=0)
        weights = shifted.reshape(span, cols).astype(jnp.bfloat16)
        p_ref[index] = weights
        acc_ref[part] += dot(kv_ref[pl.ds(row, span), HD:], weights, TN)


def near_kernel(stretch, plan_ref, qs_ref, *rest):
    attend(stretch, 0, plan_ref, qs_ref, rest[:NX], *rest[NX:])


def far_kernel(stretch, plan_ref, qs_ref, *rest):
    pieces, rest = rest[:NX], rest[NX:]
    (ds_ref, w_ref, near_top, near_sum, near_acc,
     own_ref, front_ref, back_ref, ahead_ref, behind_ref, p_ref, kv_ref, delta_ref, near_inv, far_inv,
     top_ref, sum_ref, acc_ref, s_buf, diff_ref, attn_ref, turned_ref) = rest
    attend(stretch, 1, plan_ref, qs_ref, pieces, p_ref, kv_ref, top_ref, sum_ref, acc_ref, s_buf, diff_ref)
    cols = qs_ref.shape[1]
    for part in range(2):
        top = jnp.maximum(near_top[part][:1], top_ref[part][:1])
        near = jnp.exp((near_top[part][:1] - top) * SCALE)
        far = jnp.exp((top_ref[part][:1] - top) * SCALE)
        total = (jnp.sum(near_sum[part], axis=0, keepdims=True) * near
                 + jnp.sum(sum_ref[part], axis=0, keepdims=True) * far)
        near, far = near / total, far / total
        near_inv[part] = jnp.broadcast_to(near, (8, cols))
        far_inv[part] = jnp.broadcast_to(far, (8, cols))
        out = (near_acc[part] * near + acc_ref[part] * far).T.astype(jnp.bfloat16)
        prod = ds_ref[part].astype(jnp.float32) * out.astype(jnp.float32)
        delta_ref[part] = jnp.broadcast_to(jnp.sum(prod.T, axis=0, keepdims=True), (8, cols))
        for head in range(QPG):
            attn_ref[part * stretch:(part + 1) * stretch, head * HD:(head + 1) * HD] = (
                out[head * stretch:(head + 1) * stretch])
    rows = attn_ref.shape[0] // (NH * NY)
    zh, y = lax.axis_index("zh"), lax.axis_index("y")
    for y_step in range(NY):
        for h_step in range(NH):
            block = jnp.bitwise_xor(zh, h_step) * NY + lax.rem(y + y_step, NY)
            to = (y_step * NH + h_step) * rows
            turned_ref[to:to + rows, :] = attn_ref[pl.ds(pl.multiple_of(block * rows, rows), rows), :]
    piece = NH * rows
    half = w_ref.shape[1] // 2
    for index in range(w_ref.shape[1] // MIX_SPAN):
        at = slice(index * MIX_SPAN, (index + 1) * MIX_SPAN)
        mixed = dot(turned_ref[...], w_ref[:, at], NN).astype(jnp.bfloat16)
        own_ref[:, at] = mixed[:piece]
        if at.start < half:
            ahead_ref[:, at] = mixed[2 * piece:3 * piece]
            behind_ref[:, at] = mixed[3 * piece:]
            front_ref[:, at] = mixed[piece:2 * piece]
        else:
            ahead_ref[:, at] = mixed[piece:2 * piece]
            behind_ref[:, at] = mixed[2 * piece:3 * piece]
            back_ref[:, at.start - half:at.stop - half] = mixed[3 * piece:]


def bwd_kernel(stretch, side, plan_ref, p_ref, kv_ref, qs_ref, ds_ref, delta_ref, inv_ref, *rest):
    steps, span, cols = p_ref.shape
    total = 2 * kv_ref.shape[0]
    plan = Plan(plan_ref, total // stretch, stretch)
    if side == 0:
        acc_in, dq_ref, out_ref, acc_ref, dk_ref, dv_ref, dn_ref = rest
        acc_ref[...] = acc_in[...]
    else:
        acc_ref, out_ref, dk_ref, dv_ref, dn_ref = rest
        acc_ref[...] = jnp.zeros_like(acc_ref)
    dk_ref[...] = jnp.zeros_like(dk_ref)
    dv_ref[...] = jnp.zeros_like(dv_ref)
    for part in range(2):
        column = jnp.broadcast_to(inv_ref[part][:1], (HD, cols)).T
        dn_ref[part] = (ds_ref[part].astype(jnp.float32) * column).astype(jnp.bfloat16)

    for index in range(steps):
        part, row, chunk, valid = plan.step(side, index)
        here = pl.ds(row, span)
        weights = p_ref[index]
        grad_probs = dot(kv_ref[here, HD:], ds_ref[part], NT)
        moved = (grad_probs.reshape(span // 8, 8, cols) - delta_ref[part][None]) * inv_ref[part][None]
        grad_scores = (weights.astype(jnp.float32) * moved.reshape(span, cols)).astype(jnp.bfloat16)
        dv_ref[here, :] += dot(weights, dn_ref[part], NN)
        dk_ref[here, :] += dot(grad_scores, qs_ref[part], NN)
        acc_ref[part] += dot(kv_ref[here, :HD], grad_scores, TN)

    to = 0
    for x_step in range(NX):
        for z_step in range(NZ):
            slot = place_of(side, x_step, z_step)
            for half in range(2):
                here = pl.ds(plan.row(slot + half) - side * (total // 2), stretch)
                out_ref[to:to + stretch, :HD] = (dk_ref[here, :] * SCALE).astype(jnp.bfloat16)
                out_ref[to:to + stretch, HD:] = dv_ref[here, :].astype(jnp.bfloat16)
                to += stretch
    if side == 0:
        for part in range(2):
            out = (acc_ref[part].T * SCALE).astype(jnp.bfloat16)
            for head in range(QPG):
                dq_ref[part * stretch:(part + 1) * stretch, head * HD:(head + 1) * HD] = (
                    out[head * stretch:(head + 1) * stretch])


def pair(keys, values):
    return pl.pallas_call(
        pair_kernel,
        out_shape=jax.ShapeDtypeStruct((keys.shape[0], 2 * HD), jnp.bfloat16),
        in_specs=[HBM] * 2,
        out_specs=VMEM,
        scratch_shapes=[pltpu.SemaphoreType.DMA((2,))],
        compiler_params=pltpu.CompilerParams(vmem_limit_bytes=60 * MIB),
        name="pair",
    )(keys, values)


def by_heads(queries, grad_heads, kv):
    shape = jax.ShapeDtypeStruct((2, QPG * queries.shape[0] // 2, HD), jnp.bfloat16)
    return pl.pallas_call(
        heads_kernel,
        out_shape=(shape, shape, jax.ShapeDtypeStruct(kv.shape, kv.dtype)),
        in_specs=[HBM] * 2 + [VMEM],
        out_specs=[VMEM] * 3,
        scratch_shapes=[pltpu.SemaphoreType.DMA((2, 2, QPG))],
        compiler_params=pltpu.CompilerParams(vmem_limit_bytes=4 * MIB),
        name="by_heads",
    )(queries, grad_heads, kv)


def stage(ids, piece):
    slots = ids.shape[0]
    shape = jax.ShapeDtypeStruct
    return pl.pallas_call(
        stage_kernel,
        out_shape=(shape((2 * slots + 8,), jnp.int32), shape(piece.shape, piece.dtype)),
        in_specs=[SMEM, VMEM],
        out_specs=[SMEM, VMEM],
        scratch_shapes=[pltpu.SMEM((slots,), jnp.int32)],
        compiler_params=pltpu.CompilerParams(vmem_limit_bytes=4 * MIB),
        name="stage",
    )(ids, piece)


def added(*parts):
    total = parts[0].astype(jnp.float32)
    for part in parts[1:]:
        total = total + part.astype(jnp.float32)
    return total.astype(jnp.bfloat16)


def relay_kernel(front_in, back_in, ahead_in, behind_in, token_ref, front_ref, back_ref):
    half = front_in.shape[1]
    for index in range(half // MIX_SPAN):
        at = slice(index * MIX_SPAN, (index + 1) * MIX_SPAN)
        front_ref[:, at] = added(front_in[:, at], ahead_in[:, at])
        back_ref[:, at] = added(back_in[:, at], behind_in[:, half + at.start:half + at.stop])


def relay(front, back, from_behind, from_ahead, token):
    shape = jax.ShapeDtypeStruct(front.shape, front.dtype)
    return pl.pallas_call(
        relay_kernel,
        out_shape=(shape, shape),
        in_specs=[VMEM] * 4 + [ANY],
        out_specs=[VMEM] * 2,
        compiler_params=pltpu.CompilerParams(vmem_limit_bytes=8 * MIB),
        name="relay",
    )(front, back, from_behind, from_ahead, token)


def settle_kernel(own, from_behind, from_ahead, front, back, *refs):
    keep_ref, give_ref = refs[-2:]
    half = front.shape[1]
    rows = keep_ref.shape[0]
    for index in range(half // MIX_SPAN):
        at = slice(index * MIX_SPAN, (index + 1) * MIX_SPAN)
        to = slice(half + at.start, half + at.stop)
        for where, total in ((at, added(own[:, at], front[:, at], from_ahead[:, at])),
                             (to, added(own[:, to], back[:, at], from_behind[:, to]))):
            keep_ref[:, where] = total[:rows]
            give_ref[:, where] = total[rows:]


def settle(own, from_behind, from_ahead, front, back, *tokens):
    shape = jax.ShapeDtypeStruct((own.shape[0] // NH, own.shape[1]), own.dtype)
    return pl.pallas_call(
        settle_kernel,
        out_shape=(shape, shape),
        in_specs=[VMEM] * 5 + [ANY] * len(tokens),
        out_specs=[VMEM] * 2,
        compiler_params=pltpu.CompilerParams(vmem_limit_bytes=8 * MIB),
        name="settle",
    )(own, from_behind, from_ahead, front, back, *tokens)


def share_kernel(token_ref, near, *refs):
    others, terms = refs[:NX - 1], refs[NX - 1:]
    for index, term in enumerate(terms):
        at = slice(index * term.shape[0], (index + 1) * term.shape[0])
        term[...] = added(near[at, :], *[other[at, :] for other in others])


def share(token, near, *others):
    term = jax.ShapeDtypeStruct((near.shape[0] // NZ, near.shape[1]), near.dtype)
    return pl.pallas_call(
        share_kernel,
        out_shape=(term,) * NZ,
        in_specs=[ANY] + [VMEM] * (1 + len(others)),
        out_specs=[VMEM] * NZ,
        compiler_params=pltpu.CompilerParams(vmem_limit_bytes=8 * MIB),
        cost_estimate=pl.CostEstimate(flops=BWD_FLOPS, bytes_accessed=2 * 10**6, transcendentals=0),
        name="share",
    )(token, near, *others)


def finish_kernel(token_ref, *refs):
    *parts, k_ref, v_ref = refs
    total = added(*[part[...] for part in parts])
    k_ref[...] = total[:, :HD]
    v_ref[...] = total[:, HD:]


def finish(token, *parts):
    shape = jax.ShapeDtypeStruct((parts[0].shape[0], HD), parts[0].dtype)
    return pl.pallas_call(
        finish_kernel,
        out_shape=(shape, shape),
        in_specs=[ANY] + [VMEM] * len(parts),
        out_specs=[VMEM] * 2,
        compiler_params=pltpu.CompilerParams(vmem_limit_bytes=4 * MIB),
        name="finish",
    )(token, *parts)


def stack_kernel(token_ref, *refs):
    *parts, out_ref = refs
    rows = parts[0].shape[0]
    for index, part in enumerate(parts):
        out_ref[index * rows:(index + 1) * rows, :] = part[...]


def stack(token, *parts):
    rows, width = parts[0].shape
    return pl.pallas_call(
        stack_kernel,
        out_shape=jax.ShapeDtypeStruct((len(parts) * rows, width), parts[0].dtype),
        in_specs=[ANY] + [VMEM] * len(parts),
        out_specs=VMEM,
        compiler_params=pltpu.CompilerParams(vmem_limit_bytes=4 * MIB),
        name="stack",
    )(token, *parts)


def forward(side, plan, qs, pieces, *more):
    cols = qs.shape[1]
    stretch = cols // QPG
    tokens = 2 * stretch
    total = sum(piece.shape[0] for piece in pieces)
    span = CHUNK * stretch
    steps = total // span + 1
    b16, f32 = jnp.bfloat16, jnp.float32
    shape = jax.ShapeDtypeStruct
    weights, keys = shape((steps, span, cols), b16), shape((total, 2 * HD), b16)
    row, sums = (2, 8, cols), (2, HD, cols)
    scratch = [pltpu.VMEM((steps, span, cols), f32), pltpu.VMEM((stretch, cols), jnp.int32)]
    if side:
        width = more[1].shape[1]
        outs = (shape((tokens // NY, width), b16),) + (shape((tokens // NY, width // 2), b16),) * 2 + (
            shape((tokens // NY, width), b16),) * 2 + (
            weights, keys, shape(row, f32), shape(row, f32), shape(row, f32))
        scratch = [pltpu.VMEM(row, f32), pltpu.VMEM(row, f32), pltpu.VMEM(sums, f32)] + scratch + [
            pltpu.VMEM((tokens, QPG * HD), b16), pltpu.VMEM((tokens, QPG * HD), b16)]
    else:
        outs = (weights, keys, shape(row, f32), shape(row, f32), shape(sums, f32))
    return pl.pallas_call(
        functools.partial(far_kernel if side else near_kernel, stretch),
        out_shape=outs,
        in_specs=[SMEM] + [VMEM] * (1 + len(pieces) + len(more)),
        out_specs=[VMEM] * len(outs),
        scratch_shapes=scratch,
        compiler_params=pltpu.CompilerParams(vmem_limit_bytes=FWD_MIB * MIB),
        cost_estimate=pl.CostEstimate(flops=3 * 10**9, bytes_accessed=8 * 10**6, transcendentals=10**6),
        name="attention_forward_%d" % side,
    )(plan, qs, *pieces, *more)


def backward(side, plan, probs, kv, qs, ds, delta, inverse, *partial):
    total = 2 * kv.shape[0]
    steps, span, cols = probs.shape
    stretch = cols // QPG
    b16, f32 = jnp.bfloat16, jnp.float32
    shape = jax.ShapeDtypeStruct
    terms = shape((total // 2, 2 * HD), b16)
    sums = (2, HD, cols)
    scratch = [
        pltpu.VMEM((total // 2, HD), f32),
        pltpu.VMEM((total // 2, HD), f32),
        pltpu.VMEM((2, cols, HD), b16),
    ]
    return pl.pallas_call(
        functools.partial(bwd_kernel, stretch, side),
        out_shape=(shape(sums, f32) if side else shape((2 * stretch, QPG * HD), b16), terms),
        in_specs=[SMEM] + [VMEM] * (6 + len(partial)),
        out_specs=[VMEM] * 2,
        scratch_shapes=scratch if side else [pltpu.VMEM(sums, f32)] + scratch,
        compiler_params=pltpu.CompilerParams(vmem_limit_bytes=32 * MIB),
        cost_estimate=pl.CostEstimate(flops=BWD_FLOPS, bytes_accessed=8 * 10**6, transcendentals=0),
        name="attention_backward_%d" % side,
    )(plan, probs, kv, qs, ds, delta, inverse, *partial)


def ahead(block, axis, step):
    count = lax.axis_size(axis)
    return lax.ppermute(block, axis, [(i, (i + step) % count) for i in range(count)])


def behind(block, axis, step):
    count = lax.axis_size(axis)
    return lax.ppermute(block, axis, [((i + step) % count, i) for i in range(count)])


def across(block, axis, step):
    count = lax.axis_size(axis)
    return lax.ppermute(block, axis, [(i, i ^ step) for i in range(count)])


def total_of(parts):
    total = parts[0].astype(jnp.float32)
    for part in parts[1:]:
        total = total + part.astype(jnp.float32)
    return total.astype(jnp.bfloat16)


def on_device(queries, keys, values, stretch_of, out_weight, grad_heads):
    kv = pair(keys, values)
    qs, ds, same = by_heads(queries, grad_heads, kv)
    kv = stack(qs, same, *[across(kv, "zl", step) for step in range(1, NZ)])
    plan, same = stage(stretch_of, kv)
    near = [kv] + [behind(kv, "x", step) for step in range(1, NX)]
    far = [across(piece, "core", 1) for piece in [same] + near[1:]]
    near_probs, near_kv, *partial = forward(0, plan, qs, near)
    own, front, back, to_ahead, to_behind, far_probs, far_kv, delta, near_inv, far_inv = forward(
        1, plan, qs, far, ds, out_weight, *partial)
    from_behind, from_ahead = ahead(to_ahead, "y", 1), ahead(to_behind, "y", NY - 1)
    partial, give = backward(1, plan, far_probs, far_kv, qs, ds, delta, far_inv)
    q_grad, keep = backward(0, plan, near_probs, near_kv, qs, ds, delta, near_inv, partial)
    term = total_of([keep, across(give, "core", 1)])
    front, back = relay(front, back, from_behind, from_ahead, term)
    part = term.shape[0] // NX
    near, *others = [term[step * part:(step + 1) * part] for step in range(NX)]
    others = [ahead(other, "x", step + 1) for step, other in enumerate(others)]
    mixed, give = settle(
        own, from_behind, from_ahead, ahead(front, "y", 1), ahead(back, "y", NY - 1), *others)
    terms = share(mixed, near, *others)
    mixed = total_of([mixed, across(give, "zh", 1)])
    k_grad, v_grad = finish(mixed, terms[0], *[across(terms[step], "zl", step) for step in range(1, NZ)])
    return mixed, q_grad, k_grad, v_grad


def solution(mesh):
    fine = Mesh(mesh.devices.reshape(NX, NZ, NC, NH, NY), CTX + TP)
    return jax.shard_map(
        on_device,
        mesh=fine,
        in_specs=(P(CTX, TP), P(CTX, TP), P(CTX, TP), P(), P(TP, None), P(CTX, TP)),
        out_specs=(P(CTX + TP, None), P(CTX, TP), P(CTX, TP), P(CTX, TP)),
        check_vma=False,
    )
```

```python
import functools
import jax
import jax.numpy as jnp
from jax import lax
from jax.experimental import pallas as pl
from jax.experimental.pallas import tpu as pltpu
from jax.sharding import Mesh, PartitionSpec as P

HD = 128
QPG = 4
NEG = -1e30
SCALE = HD ** (-0.5)
NT = (((1,), (1,)), ((), ()))
NN = (((1,), (0,)), ((), ()))
TN = (((0,), (0,)), ((), ()))
MIB = 1024 * 1024
NX, NZ, NC, NH, NY = 4, 4, 2, 2, 4
CTX = ("x", "zl", "core")
TP = ("zh", "y")
MIX_SPAN = 1024
CHUNK = 4
FWD_MIB = 32
BWD_FLOPS = 2 * 10**10
SMEM = pl.BlockSpec(memory_space=pltpu.SMEM)
VMEM = pl.BlockSpec(memory_space=pltpu.VMEM)
HBM = pl.BlockSpec(memory_space=pltpu.HBM)
ANY = pl.BlockSpec(memory_space=pl.ANY)


def dot(a, b, dims):
    return lax.dot_general(a, b, dims, preferred_element_type=jnp.float32)


def slot_of(x, zl, core, half):
    return ((x * NZ + zl) * NC + core) * 2 + half


def place_of(c_step, x_step, z_step):
    x, zl, core = (lax.axis_index(name) for name in CTX)
    return slot_of(lax.rem(x + x_step, NX), jnp.bitwise_xor(zl, z_step), jnp.bitwise_xor(core, c_step), 0)


def pair_kernel(k_hbm, v_hbm, kv_ref, sem):
    copies = [pltpu.make_async_copy(k_hbm, kv_ref.at[:, :HD], sem.at[0]),
              pltpu.make_async_copy(v_hbm, kv_ref.at[:, HD:], sem.at[1])]
    for copy in copies:
        copy.start()
    for copy in copies:
        copy.wait()


def heads_kernel(q_hbm, do_hbm, kv_ref, qs_ref, ds_ref, same_ref, sem):
    stretch = q_hbm.shape[0] // 2
    copies = []
    for which, (source, target) in enumerate(((q_hbm, qs_ref), (do_hbm, ds_ref))):
        for part in range(2):
            for head in range(QPG):
                copies.append(pltpu.make_async_copy(
                    source.at[part * stretch:(part + 1) * stretch, head * HD:(head + 1) * HD],
                    target.at[part, head * stretch:(head + 1) * stretch, :],
                    sem.at[which, part, head]))
    for copy in copies:
        copy.start()
    same_ref[...] = kv_ref[...]
    for copy in copies:
        copy.wait()


def stage_kernel(ids_ref, piece_ref, plan_ref, same_ref, slot_ref):
    same_ref[...] = piece_ref[...]
    slots = ids_ref.shape[0]
    core = lax.axis_index("core")
    mine = place_of(0, 0, 0)
    own = [ids_ref[mine], ids_ref[mine + 1]]
    for slot in range(slots):
        slot_ref[ids_ref[slot]] = jnp.int32(slot)
    near, far, *seen = (jnp.int32(0),) * 6
    for value in range(slots):
        slot = slot_ref[value]
        away = jnp.bitwise_xor(lax.rem(slot // 2, NC), core)
        at = jnp.where(away == 0, near, slots // 2 + far)
        plan_ref[slot] = at
        plan_ref[slots + at] = jnp.int32(value)
        near, far = near + (1 - away), far + away
        seen = [before + jnp.where((own[part] >= value) & (away == side), 1, 0)
                for before, (side, part) in zip(seen, ((0, 0), (0, 1), (1, 0), (1, 1)))]
    for index in range(4):
        plan_ref[2 * slots + index] = (seen[index] + CHUNK - 1) // CHUNK
    for part in range(2):
        plan_ref[2 * slots + 4 + part] = own[part]


class Plan:
    def __init__(self, ref, slots, stretch):
        self.ref, self.slots, self.stretch = ref, slots, stretch
        self.span = CHUNK * stretch

    def row(self, slot):
        return pl.multiple_of(self.ref[slot] * self.stretch, self.stretch)

    def step(self, side, index):
        first = self.ref[2 * self.slots + 2 * side]
        count = first + self.ref[2 * self.slots + 2 * side + 1]
        late = index >= first
        part = jnp.where(late, 1, 0)
        last = self.slots // 2 // CHUNK - 1
        chunk = jnp.minimum(index - part * first, last)
        row = pl.multiple_of(chunk * self.span, self.span)
        return part, row, chunk, index < count

    def limits(self, side, part, chunk, valid):
        own = self.ref[2 * self.slots + 4 + part]
        at = self.slots + side * (self.slots // 2) + chunk * CHUNK
        return [jnp.where(valid, (own - self.ref[at + group]) * self.stretch, -2 * self.stretch)
                for group in range(CHUNK)]


def attend(stretch, side, plan_ref, qs_ref, pieces, p_ref, kv_ref, top_ref, sum_ref, acc_ref, s_buf, diff_ref):
    steps, span, cols = p_ref.shape
    rows = kv_ref.shape[0]
    plan = Plan(plan_ref, 2 * rows // stretch, stretch)
    for x_step in range(NX):
        for z_step in range(NZ):
            slot = place_of(side, x_step, z_step)
            for half in range(2):
                at = (z_step * 2 + half) * stretch
                kv_ref[pl.ds(plan.row(slot + half) - side * rows, stretch), :] = pieces[x_step][at:at + stretch, :]
    k_at = lax.broadcasted_iota(jnp.int32, (stretch, cols), 0)
    q_at = lax.broadcasted_iota(jnp.int32, (stretch, cols), 1) % stretch
    diff_ref[...] = k_at - q_at
    top_ref[...] = jnp.full_like(top_ref, NEG)
    sum_ref[...] = jnp.zeros_like(sum_ref)
    acc_ref[...] = jnp.zeros_like(acc_ref)

    for index in range(steps):
        part, row, chunk, valid = plan.step(side, index)
        scores = dot(kv_ref[pl.ds(row, span), :HD], qs_ref[part], NT)
        top = top_ref[part]
        for group, limit in enumerate(plan.limits(side, part, chunk, valid)):
            at = slice(group * stretch, (group + 1) * stretch)
            block = jnp.where(diff_ref[...] <= limit, scores[at], NEG)
            s_buf[index, at] = block
            top = jnp.maximum(top, jnp.max(block.reshape(stretch // 8, 8, cols), axis=0))
        top_ref[part] = top
    for part in range(2):
        top_ref[part] = jnp.broadcast_to(jnp.max(top_ref[part], axis=0, keepdims=True), (8, cols))

    for index in range(steps):
        part, row, chunk, valid = plan.step(side, index)
        shifted = jnp.exp((s_buf[index].reshape(span // 8, 8, cols) - top_ref[part][None]) * SCALE)
        sum_ref[part] += jnp.sum(shifted, axis=0)
        weights = shifted.reshape(span, cols).astype(jnp.bfloat16)
        p_ref[index] = weights
        acc_ref[part] += dot(kv_ref[pl.ds(row, span), HD:], weights, TN)


def near_kernel(stretch, plan_ref, qs_ref, *rest):
    attend(stretch, 0, plan_ref, qs_ref, rest[:NX], *rest[NX:])


def far_kernel(stretch, plan_ref, qs_ref, *rest):
    pieces, rest = rest[:NX], rest[NX:]
    (ds_ref, w_ref, near_top, near_sum, near_acc,
     own_ref, front_ref, back_ref, ahead_ref, behind_ref, p_ref, kv_ref, delta_ref, near_inv, far_inv,
     top_ref, sum_ref, acc_ref, s_buf, diff_ref, attn_ref, turned_ref) = rest
    attend(stretch, 1, plan_ref, qs_ref, pieces, p_ref, kv_ref, top_ref, sum_ref, acc_ref, s_buf, diff_ref)
    cols = qs_ref.shape[1]
    for part in range(2):
        top = jnp.maximum(near_top[part][:1], top_ref[part][:1])
        near = jnp.exp((near_top[part][:1] - top) * SCALE)
        far = jnp.exp((top_ref[part][:1] - top) * SCALE)
        total = (jnp.sum(near_sum[part], axis=0, keepdims=True) * near
                 + jnp.sum(sum_ref[part], axis=0, keepdims=True) * far)
        near, far = near / total, far / total
        near_inv[part] = jnp.broadcast_to(near, (8, cols))
        far_inv[part] = jnp.broadcast_to(far, (8, cols))
        out = (near_acc[part] * near + acc_ref[part] * far).T.astype(jnp.bfloat16)
        prod = ds_ref[part].astype(jnp.float32) * out.astype(jnp.float32)
        delta_ref[part] = jnp.broadcast_to(jnp.sum(prod.T, axis=0, keepdims=True), (8, cols))
        for head in range(QPG):
            attn_ref[part * stretch:(part + 1) * stretch, head * HD:(head + 1) * HD] = (
                out[head * stretch:(head + 1) * stretch])
    rows = attn_ref.shape[0] // (NH * NY)
    zh, y = lax.axis_index("zh"), lax.axis_index("y")
    for y_step in range(NY):
        for h_step in range(NH):
            block = jnp.bitwise_xor(zh, h_step) * NY + lax.rem(y + y_step, NY)
            to = (y_step * NH + h_step) * rows
            turned_ref[to:to + rows, :] = attn_ref[pl.ds(pl.multiple_of(block * rows, rows), rows), :]
    piece = NH * rows
    half = w_ref.shape[1] // 2
    for index in range(w_ref.shape[1] // MIX_SPAN):
        at = slice(index * MIX_SPAN, (index + 1) * MIX_SPAN)
        mixed = dot(turned_ref[...], w_ref[:, at], NN).astype(jnp.bfloat16)
        own_ref[:, at] = mixed[:piece]
        if at.start < half:
            ahead_ref[:, at] = mixed[2 * piece:3 * piece]
            behind_ref[:, at] = mixed[3 * piece:]
            front_ref[:, at] = mixed[piece:2 * piece]
        else:
            ahead_ref[:, at] = mixed[piece:2 * piece]
            behind_ref[:, at] = mixed[2 * piece:3 * piece]
            back_ref[:, at.start - half:at.stop - half] = mixed[3 * piece:]


def bwd_kernel(stretch, side, plan_ref, p_ref, kv_ref, qs_ref, ds_ref, delta_ref, inv_ref, *rest):
    steps, span, cols = p_ref.shape
    total = 2 * kv_ref.shape[0]
    plan = Plan(plan_ref, total // stretch, stretch)
    if side == 0:
        acc_in, dq_ref, out_ref, acc_ref, dk_ref, dv_ref, dn_ref = rest
        acc_ref[...] = acc_in[...]
    else:
        acc_ref, out_ref, dk_ref, dv_ref, dn_ref = rest
        acc_ref[...] = jnp.zeros_like(acc_ref)
    dk_ref[...] = jnp.zeros_like(dk_ref)
    dv_ref[...] = jnp.zeros_like(dv_ref)
    for part in range(2):
        column = jnp.broadcast_to(inv_ref[part][:1], (HD, cols)).T
        dn_ref[part] = (ds_ref[part].astype(jnp.float32) * column).astype(jnp.bfloat16)

    for index in range(steps):
        part, row, chunk, valid = plan.step(side, index)
        here = pl.ds(row, span)
        weights = p_ref[index]
        grad_probs = dot(kv_ref[here, HD:], ds_ref[part], NT)
        moved = (grad_probs.reshape(span // 8, 8, cols) - delta_ref[part][None]) * inv_ref[part][None]
        grad_scores = (weights.astype(jnp.float32) * moved.reshape(span, cols)).astype(jnp.bfloat16)
        dv_ref[here, :] += dot(weights, dn_ref[part], NN)
        dk_ref[here, :] += dot(grad_scores, qs_ref[part], NN)
        acc_ref[part] += dot(kv_ref[here, :HD], grad_scores, TN)

    to = 0
    for x_step in range(NX):
        for z_step in range(NZ):
            slot = place_of(side, x_step, z_step)
            for half in range(2):
                here = pl.ds(plan.row(slot + half) - side * (total // 2), stretch)
                out_ref[to:to + stretch, :HD] = (dk_ref[here, :] * SCALE).astype(jnp.bfloat16)
                out_ref[to:to + stretch, HD:] = dv_ref[here, :].astype(jnp.bfloat16)
                to += stretch
    if side == 0:
        for part in range(2):
            out = (acc_ref[part].T * SCALE).astype(jnp.bfloat16)
            for head in range(QPG):
                dq_ref[part * stretch:(part + 1) * stretch, head * HD:(head + 1) * HD] = (
                    out[head * stretch:(head + 1) * stretch])


def pair(keys, values):
    return pl.pallas_call(
        pair_kernel,
        out_shape=jax.ShapeDtypeStruct((keys.shape[0], 2 * HD), jnp.bfloat16),
        in_specs=[HBM] * 2,
        out_specs=VMEM,
        scratch_shapes=[pltpu.SemaphoreType.DMA((2,))],
        compiler_params=pltpu.CompilerParams(vmem_limit_bytes=60 * MIB),
        name="pair",
    )(keys, values)


def by_heads(queries, grad_heads, kv):
    shape = jax.ShapeDtypeStruct((2, QPG * queries.shape[0] // 2, HD), jnp.bfloat16)
    return pl.pallas_call(
        heads_kernel,
        out_shape=(shape, shape, jax.ShapeDtypeStruct(kv.shape, kv.dtype)),
        in_specs=[HBM] * 2 + [VMEM],
        out_specs=[VMEM] * 3,
        scratch_shapes=[pltpu.SemaphoreType.DMA((2, 2, QPG))],
        compiler_params=pltpu.CompilerParams(vmem_limit_bytes=4 * MIB),
        name="by_heads",
    )(queries, grad_heads, kv)


def stage(ids, piece):
    slots = ids.shape[0]
    shape = jax.ShapeDtypeStruct
    return pl.pallas_call(
        stage_kernel,
        out_shape=(shape((2 * slots + 8,), jnp.int32), shape(piece.shape, piece.dtype)),
        in_specs=[SMEM, VMEM],
        out_specs=[SMEM, VMEM],
        scratch_shapes=[pltpu.SMEM((slots,), jnp.int32)],
        compiler_params=pltpu.CompilerParams(vmem_limit_bytes=4 * MIB),
        name="stage",
    )(ids, piece)


def added(*parts):
    total = parts[0].astype(jnp.float32)
    for part in parts[1:]:
        total = total + part.astype(jnp.float32)
    return total.astype(jnp.bfloat16)


def relay_kernel(front_in, back_in, ahead_in, behind_in, token_ref, front_ref, back_ref):
    half = front_in.shape[1]
    for index in range(half // MIX_SPAN):
        at = slice(index * MIX_SPAN, (index + 1) * MIX_SPAN)
        front_ref[:, at] = added(front_in[:, at], ahead_in[:, at])
        back_ref[:, at] = added(back_in[:, at], behind_in[:, half + at.start:half + at.stop])


def relay(front, back, from_behind, from_ahead, token):
    shape = jax.ShapeDtypeStruct(front.shape, front.dtype)
    return pl.pallas_call(
        relay_kernel,
        out_shape=(shape, shape),
        in_specs=[VMEM] * 4 + [ANY],
        out_specs=[VMEM] * 2,
        compiler_params=pltpu.CompilerParams(vmem_limit_bytes=8 * MIB),
        name="relay",
    )(front, back, from_behind, from_ahead, token)


def settle_kernel(own, from_behind, from_ahead, front, back, *refs):
    keep_ref, give_ref = refs[-2:]
    half = front.shape[1]
    rows = keep_ref.shape[0]
    for index in range(half // MIX_SPAN):
        at = slice(index * MIX_SPAN, (index + 1) * MIX_SPAN)
        to = slice(half + at.start, half + at.stop)
        for where, total in ((at, added(own[:, at], front[:, at], from_ahead[:, at])),
                             (to, added(own[:, to], back[:, at], from_behind[:, to]))):
            keep_ref[:, where] = total[:rows]
            give_ref[:, where] = total[rows:]


def settle(own, from_behind, from_ahead, front, back, *tokens):
    shape = jax.ShapeDtypeStruct((own.shape[0] // NH, own.shape[1]), own.dtype)
    return pl.pallas_call(
        settle_kernel,
        out_shape=(shape, shape),
        in_specs=[VMEM] * 5 + [ANY] * len(tokens),
        out_specs=[VMEM] * 2,
        compiler_params=pltpu.CompilerParams(vmem_limit_bytes=8 * MIB),
        name="settle",
    )(own, from_behind, from_ahead, front, back, *tokens)


def share_kernel(token_ref, near, *refs):
    others, terms = refs[:NX - 1], refs[NX - 1:]
    for index, term in enumerate(terms):
        at = slice(index * term.shape[0], (index + 1) * term.shape[0])
        term[...] = added(near[at, :], *[other[at, :] for other in others])


def share(token, near, *others):
    term = jax.ShapeDtypeStruct((near.shape[0] // NZ, near.shape[1]), near.dtype)
    return pl.pallas_call(
        share_kernel,
        out_shape=(term,) * NZ,
        in_specs=[ANY] + [VMEM] * (1 + len(others)),
        out_specs=[VMEM] * NZ,
        compiler_params=pltpu.CompilerParams(vmem_limit_bytes=8 * MIB),
        cost_estimate=pl.CostEstimate(flops=BWD_FLOPS, bytes_accessed=2 * 10**6, transcendentals=0),
        name="share",
    )(token, near, *others)


def finish_kernel(token_ref, *refs):
    *parts, k_ref, v_ref = refs
    total = added(*[part[...] for part in parts])
    k_ref[...] = total[:, :HD]
    v_ref[...] = total[:, HD:]


def finish(token, *parts):
    shape = jax.ShapeDtypeStruct((parts[0].shape[0], HD), parts[0].dtype)
    return pl.pallas_call(
        finish_kernel,
        out_shape=(shape, shape),
        in_specs=[ANY] + [VMEM] * len(parts),
        out_specs=[VMEM] * 2,
        compiler_params=pltpu.CompilerParams(vmem_limit_bytes=4 * MIB),
        name="finish",
    )(token, *parts)


def stack_kernel(token_ref, *refs):
    *parts, out_ref = refs
    rows = parts[0].shape[0]
    for index, part in enumerate(parts):
        out_ref[index * rows:(index + 1) * rows, :] = part[...]


def stack(token, *parts):
    rows, width = parts[0].shape
    return pl.pallas_call(
        stack_kernel,
        out_shape=jax.ShapeDtypeStruct((len(parts) * rows, width), parts[0].dtype),
        in_specs=[ANY] + [VMEM] * len(parts),
        out_specs=VMEM,
        compiler_params=pltpu.CompilerParams(vmem_limit_bytes=4 * MIB),
        name="stack",
    )(token, *parts)


def forward(side, plan, qs, pieces, *more):
    cols = qs.shape[1]
    stretch = cols // QPG
    tokens = 2 * stretch
    total = sum(piece.shape[0] for piece in pieces)
    span = CHUNK * stretch
    steps = total // span + 1
    b16, f32 = jnp.bfloat16, jnp.float32
    shape = jax.ShapeDtypeStruct
    weights, keys = shape((steps, span, cols), b16), shape((total, 2 * HD), b16)
    row, sums = (2, 8, cols), (2, HD, cols)
    scratch = [pltpu.VMEM((steps, span, cols), f32), pltpu.VMEM((stretch, cols), jnp.int32)]
    if side:
        width = more[1].shape[1]
        outs = (shape((tokens // NY, width), b16),) + (shape((tokens // NY, width // 2), b16),) * 2 + (
            shape((tokens // NY, width), b16),) * 2 + (
            weights, keys, shape(row, f32), shape(row, f32), shape(row, f32))
        scratch = [pltpu.VMEM(row, f32), pltpu.VMEM(row, f32), pltpu.VMEM(sums, f32)] + scratch + [
            pltpu.VMEM((tokens, QPG * HD), b16), pltpu.VMEM((tokens, QPG * HD), b16)]
    else:
        outs = (weights, keys, shape(row, f32), shape(row, f32), shape(sums, f32))
    return pl.pallas_call(
        functools.partial(far_kernel if side else near_kernel, stretch),
        out_shape=outs,
        in_specs=[SMEM] + [VMEM] * (1 + len(pieces) + len(more)),
        out_specs=[VMEM] * len(outs),
        scratch_shapes=scratch,
        compiler_params=pltpu.CompilerParams(vmem_limit_bytes=FWD_MIB * MIB),
        cost_estimate=pl.CostEstimate(flops=3 * 10**9, bytes_accessed=8 * 10**6, transcendentals=10**6),
        name="attention_forward_%d" % side,
    )(plan, qs, *pieces, *more)


def backward(side, plan, probs, kv, qs, ds, delta, inverse, *partial):
    total = 2 * kv.shape[0]
    steps, span, cols = probs.shape
    stretch = cols // QPG
    b16, f32 = jnp.bfloat16, jnp.float32
    shape = jax.ShapeDtypeStruct
    terms = shape((total // 2, 2 * HD), b16)
    sums = (2, HD, cols)
    scratch = [
        pltpu.VMEM((total // 2, HD), f32),
        pltpu.VMEM((total // 2, HD), f32),
        pltpu.VMEM((2, cols, HD), b16),
    ]
    return pl.pallas_call(
        functools.partial(bwd_kernel, stretch, side),
        out_shape=(shape(sums, f32) if side else shape((2 * stretch, QPG * HD), b16), terms),
        in_specs=[SMEM] + [VMEM] * (6 + len(partial)),
        out_specs=[VMEM] * 2,
        scratch_shapes=scratch if side else [pltpu.VMEM(sums, f32)] + scratch,
        compiler_params=pltpu.CompilerParams(vmem_limit_bytes=32 * MIB),
        cost_estimate=pl.CostEstimate(flops=BWD_FLOPS, bytes_accessed=8 * 10**6, transcendentals=0),
        name="attention_backward_%d" % side,
    )(plan, probs, kv, qs, ds, delta, inverse, *partial)


def ahead(block, axis, step):
    count = lax.axis_size(axis)
    return lax.ppermute(block, axis, [(i, (i + step) % count) for i in range(count)])


def behind(block, axis, step):
    count = lax.axis_size(axis)
    return lax.ppermute(block, axis, [((i + step) % count, i) for i in range(count)])


def across(block, axis, step):
    count = lax.axis_size(axis)
    return lax.ppermute(block, axis, [(i, i ^ step) for i in range(count)])


def total_of(parts):
    total = parts[0].astype(jnp.float32)
    for part in parts[1:]:
        total = total + part.astype(jnp.float32)
    return total.astype(jnp.bfloat16)


def on_device(queries, keys, values, stretch_of, out_weight, grad_heads):
    kv = pair(keys, values)
    qs, ds, same = by_heads(queries, grad_heads, kv)
    kv = stack(qs, same, *[across(kv, "zl", step) for step in range(1, NZ)])
    plan, same = stage(stretch_of, kv)
    near = [kv] + [behind(kv, "x", step) for step in range(1, NX)]
    far = [across(piece, "core", 1) for piece in [same] + near[1:]]
    near_probs, near_kv, *partial = forward(0, plan, qs, near)
    own, front, back, to_ahead, to_behind, far_probs, far_kv, delta, near_inv, far_inv = forward(
        1, plan, qs, far, ds, out_weight, *partial)
    from_behind, from_ahead = ahead(to_ahead, "y", 1), ahead(to_behind, "y", NY - 1)
    partial, give = backward(1, plan, far_probs, far_kv, qs, ds, delta, far_inv)
    q_grad, keep = backward(0, plan, near_probs, near_kv, qs, ds, delta, near_inv, partial)
    term = total_of([keep, across(give, "core", 1)])
    front, back = relay(front, back, from_behind, from_ahead, term)
    part = term.shape[0] // NX
    near, *others = [term[step * part:(step + 1) * part] for step in range(NX)]
    others = [ahead(other, "x", step + 1) for step, other in enumerate(others)]
    mixed, give = settle(
        own, from_behind, from_ahead, ahead(front, "y", 1), ahead(back, "y", NY - 1))
    terms = share(mixed, near, *others)
    mixed = total_of([mixed, across(give, "zh", 1)])
    k_grad, v_grad = finish(mixed, terms[0], *[across(terms[step], "zl", step) for step in range(1, NZ)])
    return mixed, q_grad, k_grad, v_grad


def solution(mesh):
    fine = Mesh(mesh.devices.reshape(NX, NZ, NC, NH, NY), CTX + TP)
    return jax.shard_map(
        on_device,
        mesh=fine,
        in_specs=(P(CTX, TP), P(CTX, TP), P(CTX, TP), P(), P(TP, None), P(CTX, TP)),
        out_specs=(P(CTX + TP, None), P(CTX, TP), P(CTX, TP), P(CTX, TP)),
        check_vma=False,
    )
```

```python
import functools
import jax
import jax.numpy as jnp
from jax import lax
from jax.experimental import pallas as pl
from jax.experimental.pallas import tpu as pltpu
from jax.sharding import Mesh, PartitionSpec as P

HD = 128
QPG = 4
NEG = -1e30
SCALE = HD ** (-0.5)
NT = (((1,), (1,)), ((), ()))
NN = (((1,), (0,)), ((), ()))
TN = (((0,), (0,)), ((), ()))
MIB = 1024 * 1024
NX, NZ, NC, NH, NY = 4, 4, 2, 2, 4
CTX = ("x", "zl", "core")
TP = ("zh", "y")
MIX_SPAN = 1024
CHUNK = 8
FWD_MIB = 32
BWD_FLOPS = 2 * 10**10
SMEM = pl.BlockSpec(memory_space=pltpu.SMEM)
VMEM = pl.BlockSpec(memory_space=pltpu.VMEM)
HBM = pl.BlockSpec(memory_space=pltpu.HBM)
ANY = pl.BlockSpec(memory_space=pl.ANY)


def dot(a, b, dims):
    return lax.dot_general(a, b, dims, preferred_element_type=jnp.float32)


def slot_of(x, zl, core, half):
    return ((x * NZ + zl) * NC + core) * 2 + half


def place_of(c_step, x_step, z_step):
    x, zl, core = (lax.axis_index(name) for name in CTX)
    return slot_of(lax.rem(x + x_step, NX), jnp.bitwise_xor(zl, z_step), jnp.bitwise_xor(core, c_step), 0)


def pair_kernel(k_hbm, v_hbm, kv_ref, sem):
    copies = [pltpu.make_async_copy(k_hbm, kv_ref.at[:, :HD], sem.at[0]),
              pltpu.make_async_copy(v_hbm, kv_ref.at[:, HD:], sem.at[1])]
    for copy in copies:
        copy.start()
    for copy in copies:
        copy.wait()


def heads_kernel(q_hbm, do_hbm, kv_ref, qs_ref, ds_ref, same_ref, sem):
    stretch = q_hbm.shape[0] // 2
    copies = []
    for which, (source, target) in enumerate(((q_hbm, qs_ref), (do_hbm, ds_ref))):
        for part in range(2):
            for head in range(QPG):
                copies.append(pltpu.make_async_copy(
                    source.at[part * stretch:(part + 1) * stretch, head * HD:(head + 1) * HD],
                    target.at[part, head * stretch:(head + 1) * stretch, :],
                    sem.at[which, part, head]))
    for copy in copies:
        copy.start()
    same_ref[...] = kv_ref[...]
    for copy in copies:
        copy.wait()


def stage_kernel(ids_ref, piece_ref, plan_ref, same_ref, slot_ref):
    same_ref[...] = piece_ref[...]
    slots = ids_ref.shape[0]
    core = lax.axis_index("core")
    mine = place_of(0, 0, 0)
    own = [ids_ref[mine], ids_ref[mine + 1]]
    for slot in range(slots):
        slot_ref[ids_ref[slot]] = jnp.int32(slot)
    near, far, *seen = (jnp.int32(0),) * 6
    for value in range(slots):
        slot = slot_ref[value]
        away = jnp.bitwise_xor(lax.rem(slot // 2, NC), core)
        at = jnp.where(away == 0, near, slots // 2 + far)
        plan_ref[slot] = at
        plan_ref[slots + at] = jnp.int32(value)
        near, far = near + (1 - away), far + away
        seen = [before + jnp.where((own[part] >= value) & (away == side), 1, 0)
                for before, (side, part) in zip(seen, ((0, 0), (0, 1), (1, 0), (1, 1)))]
    for index in range(4):
        plan_ref[2 * slots + index] = (seen[index] + CHUNK - 1) // CHUNK
    for part in range(2):
        plan_ref[2 * slots + 4 + part] = own[part]


class Plan:
    def __init__(self, ref, slots, stretch):
        self.ref, self.slots, self.stretch = ref, slots, stretch
        self.span = CHUNK * stretch

    def row(self, slot):
        return pl.multiple_of(self.ref[slot] * self.stretch, self.stretch)

    def step(self, side, index):
        first = self.ref[2 * self.slots + 2 * side]
        count = first + self.ref[2 * self.slots + 2 * side + 1]
        late = index >= first
        part = jnp.where(late, 1, 0)
        last = self.slots // 2 // CHUNK - 1
        chunk = jnp.minimum(index - part * first, last)
        row = pl.multiple_of(chunk * self.span, self.span)
        return part, row, chunk, index < count

    def limits(self, side, part, chunk, valid):
        own = self.ref[2 * self.slots + 4 + part]
        at = self.slots + side * (self.slots // 2) + chunk * CHUNK
        return [jnp.where(valid, (own - self.ref[at + group]) * self.stretch, -2 * self.stretch)
                for group in range(CHUNK)]


def attend(stretch, side, plan_ref, qs_ref, pieces, p_ref, kv_ref, top_ref, sum_ref, acc_ref, s_buf, diff_ref):
    steps, span, cols = p_ref.shape
    rows = kv_ref.shape[0]
    plan = Plan(plan_ref, 2 * rows // stretch, stretch)
    for x_step in range(NX):
        for z_step in range(NZ):
            slot = place_of(side, x_step, z_step)
            for half in range(2):
                at = (z_step * 2 + half) * stretch
                kv_ref[pl.ds(plan.row(slot + half) - side * rows, stretch), :] = pieces[x_step][at:at + stretch, :]
    k_at = lax.broadcasted_iota(jnp.int32, (stretch, cols), 0)
    q_at = lax.broadcasted_iota(jnp.int32, (stretch, cols), 1) % stretch
    diff_ref[...] = k_at - q_at
    top_ref[...] = jnp.full_like(top_ref, NEG)
    sum_ref[...] = jnp.zeros_like(sum_ref)
    acc_ref[...] = jnp.zeros_like(acc_ref)

    for index in range(steps):
        part, row, chunk, valid = plan.step(side, index)
        scores = dot(kv_ref[pl.ds(row, span), :HD], qs_ref[part], NT)
        top = top_ref[part]
        for group, limit in enumerate(plan.limits(side, part, chunk, valid)):
            at = slice(group * stretch, (group + 1) * stretch)
            block = jnp.where(diff_ref[...] <= limit, scores[at], NEG)
            s_buf[index, at] = block
            top = jnp.maximum(top, jnp.max(block.reshape(stretch // 8, 8, cols), axis=0))
        top_ref[part] = top
    for part in range(2):
        top_ref[part] = jnp.broadcast_to(jnp.max(top_ref[part], axis=0, keepdims=True), (8, cols))

    for index in range(steps):
        part, row, chunk, valid = plan.step(side, index)
        shifted = jnp.exp((s_buf[index].reshape(span // 8, 8, cols) - top_ref[part][None]) * SCALE)
        sum_ref[part] += jnp.sum(shifted, axis=0)
        weights = shifted.reshape(span, cols).astype(jnp.bfloat16)
        p_ref[index] = weights
        acc_ref[part] += dot(kv_ref[pl.ds(row, span), HD:], weights, TN)


def near_kernel(stretch, plan_ref, qs_ref, *rest):
    attend(stretch, 0, plan_ref, qs_ref, rest[:NX], *rest[NX:])


def far_kernel(stretch, plan_ref, qs_ref, *rest):
    pieces, rest = rest[:NX], rest[NX:]
    (ds_ref, w_ref, near_top, near_sum, near_acc,
     own_ref, front_ref, back_ref, ahead_ref, behind_ref, p_ref, kv_ref, delta_ref, near_inv, far_inv,
     top_ref, sum_ref, acc_ref, s_buf, diff_ref, attn_ref, turned_ref) = rest
    attend(stretch, 1, plan_ref, qs_ref, pieces, p_ref, kv_ref, top_ref, sum_ref, acc_ref, s_buf, diff_ref)
    cols = qs_ref.shape[1]
    for part in range(2):
        top = jnp.maximum(near_top[part][:1], top_ref[part][:1])
        near = jnp.exp((near_top[part][:1] - top) * SCALE)
        far = jnp.exp((top_ref[part][:1] - top) * SCALE)
        total = (jnp.sum(near_sum[part], axis=0, keepdims=True) * near
                 + jnp.sum(sum_ref[part], axis=0, keepdims=True) * far)
        near, far = near / total, far / total
        near_inv[part] = jnp.broadcast_to(near, (8, cols))
        far_inv[part] = jnp.broadcast_to(far, (8, cols))
        out = (near_acc[part] * near + acc_ref[part] * far).T.astype(jnp.bfloat16)
        prod = ds_ref[part].astype(jnp.float32) * out.astype(jnp.float32)
        delta_ref[part] = jnp.broadcast_to(jnp.sum(prod.T, axis=0, keepdims=True), (8, cols))
        for head in range(QPG):
            attn_ref[part * stretch:(part + 1) * stretch, head * HD:(head + 1) * HD] = (
                out[head * stretch:(head + 1) * stretch])
    rows = attn_ref.shape[0] // (NH * NY)
    zh, y = lax.axis_index("zh"), lax.axis_index("y")
    for y_step in range(NY):
        for h_step in range(NH):
            block = jnp.bitwise_xor(zh, h_step) * NY + lax.rem(y + y_step, NY)
            to = (y_step * NH + h_step) * rows
            turned_ref[to:to + rows, :] = attn_ref[pl.ds(pl.multiple_of(block * rows, rows), rows), :]
    piece = NH * rows
    half = w_ref.shape[1] // 2
    for index in range(w_ref.shape[1] // MIX_SPAN):
        at = slice(index * MIX_SPAN, (index + 1) * MIX_SPAN)
        mixed = dot(turned_ref[...], w_ref[:, at], NN).astype(jnp.bfloat16)
        own_ref[:, at] = mixed[:piece]
        far, near, last = mixed[2 * piece:3 * piece], mixed[piece:2 * piece], mixed[3 * piece:]
        quarter = half // 2
        if at.start < half:
            ahead_ref[:, at] = far
            front_ref[:, at] = near
        else:
            behind_ref[:, at.start - quarter:at.stop - quarter] = far
            if at.start < half + quarter:
                ahead_ref[:, at] = near
            else:
                front_ref[:, at.start - quarter:at.stop - quarter] = near
        if at.start < quarter:
            behind_ref[:, at] = last
        else:
            back_ref[:, at.start - quarter:at.stop - quarter] = last


def bwd_kernel(stretch, side, plan_ref, p_ref, kv_ref, qs_ref, ds_ref, delta_ref, inv_ref, *rest):
    steps, span, cols = p_ref.shape
    total = 2 * kv_ref.shape[0]
    plan = Plan(plan_ref, total // stretch, stretch)
    if side == 0:
        acc_in, dq_ref, out_ref, acc_ref, dk_ref, dv_ref, dn_ref = rest
        acc_ref[...] = acc_in[...]
    else:
        acc_ref, out_ref, dk_ref, dv_ref, dn_ref = rest
        acc_ref[...] = jnp.zeros_like(acc_ref)
    dk_ref[...] = jnp.zeros_like(dk_ref)
    dv_ref[...] = jnp.zeros_like(dv_ref)
    for part in range(2):
        column = jnp.broadcast_to(inv_ref[part][:1], (HD, cols)).T
        dn_ref[part] = (ds_ref[part].astype(jnp.float32) * column).astype(jnp.bfloat16)

    for index in range(steps):
        part, row, chunk, valid = plan.step(side, index)
        here = pl.ds(row, span)
        weights = p_ref[index]
        grad_probs = dot(kv_ref[here, HD:], ds_ref[part], NT)
        moved = (grad_probs.reshape(span // 8, 8, cols) - delta_ref[part][None]) * inv_ref[part][None]
        grad_scores = (weights.astype(jnp.float32) * moved.reshape(span, cols)).astype(jnp.bfloat16)
        dv_ref[here, :] += dot(weights, dn_ref[part], NN)
        dk_ref[here, :] += dot(grad_scores, qs_ref[part], NN)
        acc_ref[part] += dot(kv_ref[here, :HD], grad_scores, TN)

    to = 0
    for x_step in range(NX):
        for z_step in range(NZ):
            slot = place_of(side, x_step, z_step)
            for half in range(2):
                here = pl.ds(plan.row(slot + half) - side * (total // 2), stretch)
                out_ref[to:to + stretch, :HD] = (dk_ref[here, :] * SCALE).astype(jnp.bfloat16)
                out_ref[to:to + stretch, HD:] = dv_ref[here, :].astype(jnp.bfloat16)
                to += stretch
    if side == 0:
        for part in range(2):
            out = (acc_ref[part].T * SCALE).astype(jnp.bfloat16)
            for head in range(QPG):
                dq_ref[part * stretch:(part + 1) * stretch, head * HD:(head + 1) * HD] = (
                    out[head * stretch:(head + 1) * stretch])


def pair(keys, values):
    return pl.pallas_call(
        pair_kernel,
        out_shape=jax.ShapeDtypeStruct((keys.shape[0], 2 * HD), jnp.bfloat16),
        in_specs=[HBM] * 2,
        out_specs=HBM,
        scratch_shapes=[pltpu.SemaphoreType.DMA((2,))],
        compiler_params=pltpu.CompilerParams(vmem_limit_bytes=60 * MIB),
        name="pair",
    )(keys, values)


def by_heads(queries, grad_heads, kv):
    shape = jax.ShapeDtypeStruct((2, QPG * queries.shape[0] // 2, HD), jnp.bfloat16)
    return pl.pallas_call(
        heads_kernel,
        out_shape=(shape, shape, jax.ShapeDtypeStruct(kv.shape, kv.dtype)),
        in_specs=[HBM] * 2 + [VMEM],
        out_specs=[VMEM] * 3,
        scratch_shapes=[pltpu.SemaphoreType.DMA((2, 2, QPG))],
        compiler_params=pltpu.CompilerParams(vmem_limit_bytes=4 * MIB),
        name="by_heads",
    )(queries, grad_heads, kv)


def stage(ids, piece):
    slots = ids.shape[0]
    shape = jax.ShapeDtypeStruct
    return pl.pallas_call(
        stage_kernel,
        out_shape=(shape((2 * slots + 8,), jnp.int32), shape(piece.shape, piece.dtype)),
        in_specs=[SMEM, VMEM],
        out_specs=[SMEM, VMEM],
        scratch_shapes=[pltpu.SMEM((slots,), jnp.int32)],
        compiler_params=pltpu.CompilerParams(vmem_limit_bytes=4 * MIB),
        name="stage",
    )(ids, piece)


def added(*parts):
    total = parts[0].astype(jnp.float32)
    for part in parts[1:]:
        total = total + part.astype(jnp.float32)
    return total.astype(jnp.bfloat16)


def relay_kernel(front_in, back_in, ahead_in, behind_in, token_ref, front_ref, back_ref):
    quarter = front_in.shape[1] // 3
    for index in range(2 * quarter // MIX_SPAN):
        at = slice(index * MIX_SPAN, (index + 1) * MIX_SPAN)
        front_ref[:, at] = added(front_in[:, at], ahead_in[:, at])
        to = slice(quarter + at.start, quarter + at.stop)
        back_ref[:, to] = added(back_in[:, to], behind_in[:, to])


def relay(front, back, from_behind, from_ahead, token):
    shape = jax.ShapeDtypeStruct(front.shape, front.dtype)
    return pl.pallas_call(
        relay_kernel,
        out_shape=(shape, shape),
        in_specs=[VMEM] * 4 + [ANY],
        out_specs=[VMEM] * 2,
        input_output_aliases={0: 0, 1: 1},
        compiler_params=pltpu.CompilerParams(vmem_limit_bytes=8 * MIB),
        name="relay",
    )(front, back, from_behind, from_ahead, token)


def settle_kernel(own, from_behind, from_ahead, front, back, keep_ref, give_ref):
    quarter = front.shape[1] // 3
    rows = keep_ref.shape[0]
    for index in range(own.shape[1] // MIX_SPAN):
        at = slice(index * MIX_SPAN, (index + 1) * MIX_SPAN)
        less = slice(at.start - quarter, at.stop - quarter)
        which = at.start // quarter
        behind = from_behind[:, at] if which == 2 else front[:, at if which < 2 else less]
        before = from_ahead[:, at] if which == 0 else back[:, less]
        total = added(own[:, at], behind, before)
        keep_ref[:, at] = total[:rows]
        give_ref[:, at] = total[rows:]


def settle(own, from_behind, from_ahead, front, back):
    shape = jax.ShapeDtypeStruct((own.shape[0] // NH, own.shape[1]), own.dtype)
    return pl.pallas_call(
        settle_kernel,
        out_shape=(shape, shape),
        in_specs=[VMEM] * 5,
        out_specs=[VMEM] * 2,
        compiler_params=pltpu.CompilerParams(vmem_limit_bytes=8 * MIB),
        name="settle",
    )(own, from_behind, from_ahead, front, back)


def share_kernel(token_ref, near, *refs):
    others, terms = refs[:NX - 1], refs[NX - 1:]
    for index, term in enumerate(terms):
        at = slice(index * term.shape[0], (index + 1) * term.shape[0])
        term[...] = added(near[at, :], *[other[at, :] for other in others])


def share(token, near, *others):
    term = jax.ShapeDtypeStruct((near.shape[0] // NZ, near.shape[1]), near.dtype)
    return pl.pallas_call(
        share_kernel,
        out_shape=(term,) * NZ,
        in_specs=[ANY] + [VMEM] * (1 + len(others)),
        out_specs=[VMEM] * NZ,
        compiler_params=pltpu.CompilerParams(vmem_limit_bytes=8 * MIB),
        cost_estimate=pl.CostEstimate(flops=BWD_FLOPS, bytes_accessed=2 * 10**6, transcendentals=0),
        name="share",
    )(token, near, *others)


def finish_kernel(token_ref, *refs):
    *parts, k_ref, v_ref = refs
    total = added(*[part[...] for part in parts])
    k_ref[...] = total[:, :HD]
    v_ref[...] = total[:, HD:]


def finish(token, *parts):
    shape = jax.ShapeDtypeStruct((parts[0].shape[0], HD), parts[0].dtype)
    return pl.pallas_call(
        finish_kernel,
        out_shape=(shape, shape),
        in_specs=[ANY] + [VMEM] * len(parts),
        out_specs=[VMEM] * 2,
        compiler_params=pltpu.CompilerParams(vmem_limit_bytes=4 * MIB),
        name="finish",
    )(token, *parts)


def stack_kernel(token_ref, *refs):
    *parts, out_ref = refs
    rows = parts[0].shape[0]
    for index, part in enumerate(parts):
        out_ref[index * rows:(index + 1) * rows, :] = part[...]


def stack(token, *parts):
    rows, width = parts[0].shape
    return pl.pallas_call(
        stack_kernel,
        out_shape=jax.ShapeDtypeStruct((len(parts) * rows, width), parts[0].dtype),
        in_specs=[ANY] + [VMEM] * len(parts),
        out_specs=VMEM,
        compiler_params=pltpu.CompilerParams(vmem_limit_bytes=4 * MIB),
        name="stack",
    )(token, *parts)


def forward(side, plan, qs, pieces, *more):
    cols = qs.shape[1]
    stretch = cols // QPG
    tokens = 2 * stretch
    total = sum(piece.shape[0] for piece in pieces)
    span = CHUNK * stretch
    steps = total // span + 1
    b16, f32 = jnp.bfloat16, jnp.float32
    shape = jax.ShapeDtypeStruct
    weights, keys = shape((steps, span, cols), b16), shape((total, 2 * HD), b16)
    row, sums = (2, 8, cols), (2, HD, cols)
    scratch = [pltpu.VMEM((steps, span, cols), f32), pltpu.VMEM((stretch, cols), jnp.int32)]
    if side:
        width = more[1].shape[1]
        outs = (shape((tokens // NY, width), b16),) + (shape((tokens // NY, 3 * width // 4), b16),) * 4 + (
            weights, keys, shape(row, f32), shape(row, f32), shape(row, f32))
        scratch = [pltpu.VMEM(row, f32), pltpu.VMEM(row, f32), pltpu.VMEM(sums, f32)] + scratch + [
            pltpu.VMEM((tokens, QPG * HD), b16), pltpu.VMEM((tokens, QPG * HD), b16)]
    else:
        outs = (weights, keys, shape(row, f32), shape(row, f32), shape(sums, f32))
    return pl.pallas_call(
        functools.partial(far_kernel if side else near_kernel, stretch),
        out_shape=outs,
        in_specs=[SMEM] + [VMEM] * (1 + len(pieces) + len(more)),
        out_specs=[VMEM] * len(outs),
        scratch_shapes=scratch,
        compiler_params=pltpu.CompilerParams(vmem_limit_bytes=FWD_MIB * MIB),
        cost_estimate=pl.CostEstimate(flops=3 * 10**9, bytes_accessed=8 * 10**6, transcendentals=10**6),
        name="attention_forward_%d" % side,
    )(plan, qs, *pieces, *more)


def backward(side, plan, probs, kv, qs, ds, delta, inverse, *partial):
    total = 2 * kv.shape[0]
    steps, span, cols = probs.shape
    stretch = cols // QPG
    b16, f32 = jnp.bfloat16, jnp.float32
    shape = jax.ShapeDtypeStruct
    terms = shape((total // 2, 2 * HD), b16)
    sums = (2, HD, cols)
    scratch = [
        pltpu.VMEM((total // 2, HD), f32),
        pltpu.VMEM((total // 2, HD), f32),
        pltpu.VMEM((2, cols, HD), b16),
    ]
    return pl.pallas_call(
        functools.partial(bwd_kernel, stretch, side),
        out_shape=(shape(sums, f32) if side else shape((2 * stretch, QPG * HD), b16), terms),
        in_specs=[SMEM] + [VMEM] * (6 + len(partial)),
        out_specs=[VMEM] * 2,
        scratch_shapes=scratch if side else [pltpu.VMEM(sums, f32)] + scratch,
        compiler_params=pltpu.CompilerParams(vmem_limit_bytes=32 * MIB),
        cost_estimate=pl.CostEstimate(flops=BWD_FLOPS, bytes_accessed=8 * 10**6, transcendentals=0),
        name="attention_backward_%d" % side,
    )(plan, probs, kv, qs, ds, delta, inverse, *partial)


def ahead(block, axis, step):
    count = lax.axis_size(axis)
    return lax.ppermute(block, axis, [(i, (i + step) % count) for i in range(count)])


def behind(block, axis, step):
    count = lax.axis_size(axis)
    return lax.ppermute(block, axis, [((i + step) % count, i) for i in range(count)])


def across(block, axis, step):
    count = lax.axis_size(axis)
    return lax.ppermute(block, axis, [(i, i ^ step) for i in range(count)])


def total_of(parts):
    total = parts[0].astype(jnp.float32)
    for part in parts[1:]:
        total = total + part.astype(jnp.float32)
    return total.astype(jnp.bfloat16)


def on_device(queries, keys, values, stretch_of, out_weight, grad_heads):
    kv = pair(keys, values)
    qs, ds, same = by_heads(queries, grad_heads, kv)
    kv = stack(qs, same, *[across(kv, "zl", step) for step in range(1, NZ)])
    plan, same = stage(stretch_of, kv)
    near = [kv] + [behind(kv, "x", step) for step in range(1, NX)]
    far = [across(piece, "core", 1) for piece in [same] + near[1:]]
    near_probs, near_kv, *partial = forward(0, plan, qs, near)
    own, front, back, to_ahead, to_behind, far_probs, far_kv, delta, near_inv, far_inv = forward(
        1, plan, qs, far, ds, out_weight, *partial)
    from_behind, from_ahead = ahead(to_ahead, "y", 1), ahead(to_behind, "y", NY - 1)
    partial, give = backward(1, plan, far_probs, far_kv, qs, ds, delta, far_inv)
    q_grad, keep = backward(0, plan, near_probs, near_kv, qs, ds, delta, near_inv, partial)
    term = total_of([keep, across(give, "core", 1)])
    front, back = relay(front, back, from_behind, from_ahead, term)
    part = term.shape[0] // NX
    near, *others = [term[step * part:(step + 1) * part] for step in range(NX)]
    others = [ahead(other, "x", step + 1) for step, other in enumerate(others)]
    mixed, give = settle(
        own, from_behind, from_ahead, ahead(front, "y", 1), ahead(back, "y", NY - 1))
    terms = share(mixed, near, *others)
    mixed = total_of([mixed, across(give, "zh", 1)])
    k_grad, v_grad = finish(mixed, terms[0], *[across(terms[step], "zl", step) for step in (2, 3, 1)])
    return mixed, q_grad, k_grad, v_grad


def solution(mesh):
    fine = Mesh(mesh.devices.reshape(NX, NZ, NC, NH, NY), CTX + TP)
    return jax.shard_map(
        on_device,
        mesh=fine,
        in_specs=(P(CTX, TP), P(CTX, TP), P(CTX, TP), P(), P(TP, None), P(CTX, TP)),
        out_specs=(P(CTX + TP, None), P(CTX, TP), P(CTX, TP), P(CTX, TP)),
        check_vma=False,
    )
```

```python
import functools
import jax
import jax.numpy as jnp
from jax import lax
from jax.experimental import pallas as pl
from jax.experimental.pallas import tpu as pltpu
from jax.sharding import Mesh, PartitionSpec as P

HD = 128
QPG = 4
NEG = -1e30
SCALE = HD ** (-0.5)
NT = (((1,), (1,)), ((), ()))
NN = (((1,), (0,)), ((), ()))
TN = (((0,), (0,)), ((), ()))
MIB = 1024 * 1024
NX, NZ, NC, NH, NY = 4, 4, 2, 2, 4
CTX = ("x", "zl", "core")
TP = ("zh", "y")
MIX_SPAN = 1024
CHUNK = 8
FWD_MIB = 32
BWD_FLOPS = 2 * 10**10
SMEM = pl.BlockSpec(memory_space=pltpu.SMEM)
VMEM = pl.BlockSpec(memory_space=pltpu.VMEM)
HBM = pl.BlockSpec(memory_space=pltpu.HBM)
ANY = pl.BlockSpec(memory_space=pl.ANY)


def dot(a, b, dims):
    return lax.dot_general(a, b, dims, preferred_element_type=jnp.float32)


def slot_of(x, zl, core, half):
    return ((x * NZ + zl) * NC + core) * 2 + half


def place_of(c_step, x_step, z_step):
    x, zl, core = (lax.axis_index(name) for name in CTX)
    return slot_of(lax.rem(x + x_step, NX), jnp.bitwise_xor(zl, z_step), jnp.bitwise_xor(core, c_step), 0)


def pair_kernel(k_hbm, v_hbm, kv_ref, sem):
    copies = [pltpu.make_async_copy(k_hbm, kv_ref.at[:, :HD], sem.at[0]),
              pltpu.make_async_copy(v_hbm, kv_ref.at[:, HD:], sem.at[1])]
    for copy in copies:
        copy.start()
    for copy in copies:
        copy.wait()


def heads_kernel(q_hbm, do_hbm, kv_ref, qs_ref, ds_ref, same_ref, sem):
    stretch = q_hbm.shape[0] // 2
    copies = []
    for which, (source, target) in enumerate(((q_hbm, qs_ref), (do_hbm, ds_ref))):
        for part in range(2):
            for head in range(QPG):
                copies.append(pltpu.make_async_copy(
                    source.at[part * stretch:(part + 1) * stretch, head * HD:(head + 1) * HD],
                    target.at[part, head * stretch:(head + 1) * stretch, :],
                    sem.at[which, part, head]))
    for copy in copies:
        copy.start()
    same_ref[...] = kv_ref[...]
    for copy in copies:
        copy.wait()


def stage_kernel(ids_ref, piece_ref, plan_ref, same_ref, slot_ref):
    same_ref[...] = piece_ref[...]
    slots = ids_ref.shape[0]
    core = lax.axis_index("core")
    mine = place_of(0, 0, 0)
    own = [ids_ref[mine], ids_ref[mine + 1]]
    for slot in range(slots):
        slot_ref[ids_ref[slot]] = jnp.int32(slot)
    near, far, *seen = (jnp.int32(0),) * 6
    for value in range(slots):
        slot = slot_ref[value]
        away = jnp.bitwise_xor(lax.rem(slot // 2, NC), core)
        at = jnp.where(away == 0, near, slots // 2 + far)
        plan_ref[slot] = at
        plan_ref[slots + at] = jnp.int32(value)
        near, far = near + (1 - away), far + away
        seen = [before + jnp.where((own[part] >= value) & (away == side), 1, 0)
                for before, (side, part) in zip(seen, ((0, 0), (0, 1), (1, 0), (1, 1)))]
    for index in range(4):
        plan_ref[2 * slots + index] = (seen[index] + CHUNK - 1) // CHUNK
    for part in range(2):
        plan_ref[2 * slots + 4 + part] = own[part]


class Plan:
    def __init__(self, ref, slots, stretch):
        self.ref, self.slots, self.stretch = ref, slots, stretch
        self.span = CHUNK * stretch

    def row(self, slot):
        return pl.multiple_of(self.ref[slot] * self.stretch, self.stretch)

    def step(self, side, index):
        first = self.ref[2 * self.slots + 2 * side]
        count = first + self.ref[2 * self.slots + 2 * side + 1]
        late = index >= first
        part = jnp.where(late, 1, 0)
        last = self.slots // 2 // CHUNK - 1
        chunk = jnp.minimum(index - part * first, last)
        row = pl.multiple_of(chunk * self.span, self.span)
        return part, row, chunk, index < count

    def limits(self, side, part, chunk, valid):
        own = self.ref[2 * self.slots + 4 + part]
        at = self.slots + side * (self.slots // 2) + chunk * CHUNK
        return [jnp.where(valid, (own - self.ref[at + group]) * self.stretch, -2 * self.stretch)
                for group in range(CHUNK)]


def attend(stretch, side, plan_ref, qs_ref, pieces, p_ref, kv_ref, top_ref, sum_ref, acc_ref, s_buf, diff_ref):
    steps, span, cols = p_ref.shape
    rows = kv_ref.shape[0]
    plan = Plan(plan_ref, 2 * rows // stretch, stretch)
    for x_step in range(NX):
        for z_step in range(NZ):
            slot = place_of(side, x_step, z_step)
            for half in range(2):
                at = (z_step * 2 + half) * stretch
                kv_ref[pl.ds(plan.row(slot + half) - side * rows, stretch), :] = pieces[x_step][at:at + stretch, :]
    k_at = lax.broadcasted_iota(jnp.int32, (stretch, cols), 0)
    q_at = lax.broadcasted_iota(jnp.int32, (stretch, cols), 1) % stretch
    diff_ref[...] = k_at - q_at
    top_ref[...] = jnp.full_like(top_ref, NEG)
    sum_ref[...] = jnp.zeros_like(sum_ref)
    acc_ref[...] = jnp.zeros_like(acc_ref)

    for index in range(steps):
        part, row, chunk, valid = plan.step(side, index)
        scores = dot(kv_ref[pl.ds(row, span), :HD], qs_ref[part], NT)
        top = top_ref[part]
        for group, limit in enumerate(plan.limits(side, part, chunk, valid)):
            at = slice(group * stretch, (group + 1) * stretch)
            block = jnp.where(diff_ref[...] <= limit, scores[at], NEG)
            s_buf[index, at] = block
            top = jnp.maximum(top, jnp.max(block.reshape(stretch // 8, 8, cols), axis=0))
        top_ref[part] = top
    for part in range(2):
        top_ref[part] = jnp.broadcast_to(jnp.max(top_ref[part], axis=0, keepdims=True), (8, cols))

    for index in range(steps):
        part, row, chunk, valid = plan.step(side, index)
        shifted = jnp.exp((s_buf[index].reshape(span // 8, 8, cols) - top_ref[part][None]) * SCALE)
        sum_ref[part] += jnp.sum(shifted, axis=0)
        weights = shifted.reshape(span, cols).astype(jnp.bfloat16)
        p_ref[index] = weights
        acc_ref[part] += dot(kv_ref[pl.ds(row, span), HD:], weights, TN)


def near_kernel(stretch, plan_ref, qs_ref, *rest):
    attend(stretch, 0, plan_ref, qs_ref, rest[:NX], *rest[NX:])


def far_kernel(stretch, plan_ref, qs_ref, *rest):
    pieces, rest = rest[:NX], rest[NX:]
    (ds_ref, w_ref, near_top, near_sum, near_acc,
     own_ref, front_ref, back_ref, ahead_ref, behind_ref, p_ref, kv_ref, delta_ref, near_inv, far_inv,
     top_ref, sum_ref, acc_ref, s_buf, diff_ref, attn_ref, turned_ref) = rest
    attend(stretch, 1, plan_ref, qs_ref, pieces, p_ref, kv_ref, top_ref, sum_ref, acc_ref, s_buf, diff_ref)
    cols = qs_ref.shape[1]
    for part in range(2):
        top = jnp.maximum(near_top[part][:1], top_ref[part][:1])
        near = jnp.exp((near_top[part][:1] - top) * SCALE)
        far = jnp.exp((top_ref[part][:1] - top) * SCALE)
        total = (jnp.sum(near_sum[part], axis=0, keepdims=True) * near
                 + jnp.sum(sum_ref[part], axis=0, keepdims=True) * far)
        near, far = near / total, far / total
        near_inv[part] = jnp.broadcast_to(near, (8, cols))
        far_inv[part] = jnp.broadcast_to(far, (8, cols))
        out = (near_acc[part] * near + acc_ref[part] * far).T.astype(jnp.bfloat16)
        prod = ds_ref[part].astype(jnp.float32) * out.astype(jnp.float32)
        delta_ref[part] = jnp.broadcast_to(jnp.sum(prod.T, axis=0, keepdims=True), (8, cols))
        for head in range(QPG):
            attn_ref[part * stretch:(part + 1) * stretch, head * HD:(head + 1) * HD] = (
                out[head * stretch:(head + 1) * stretch])
    rows = attn_ref.shape[0] // (NH * NY)
    zh, y = lax.axis_index("zh"), lax.axis_index("y")
    for y_step in range(NY):
        for h_step in range(NH):
            block = jnp.bitwise_xor(zh, h_step) * NY + lax.rem(y + y_step, NY)
            to = (y_step * NH + h_step) * rows
            turned_ref[to:to + rows, :] = attn_ref[pl.ds(pl.multiple_of(block * rows, rows), rows), :]
    piece = NH * rows
    half = w_ref.shape[1] // 2
    for index in range(w_ref.shape[1] // MIX_SPAN):
        at = slice(index * MIX_SPAN, (index + 1) * MIX_SPAN)
        mixed = dot(turned_ref[...], w_ref[:, at], NN).astype(jnp.bfloat16)
        own_ref[:, at] = mixed[:piece]
        far, near, last = mixed[2 * piece:3 * piece], mixed[piece:2 * piece], mixed[3 * piece:]
        quarter = half // 2
        if at.start < half:
            ahead_ref[:, at] = far
            front_ref[:, at] = near
        else:
            behind_ref[:, at.start - quarter:at.stop - quarter] = far
            if at.start < half + quarter:
                ahead_ref[:, at] = near
            else:
                front_ref[:, at.start - quarter:at.stop - quarter] = near
        if at.start < quarter:
            behind_ref[:, at] = last
        else:
            back_ref[:, at.start - quarter:at.stop - quarter] = last


def bwd_kernel(stretch, side, plan_ref, p_ref, kv_ref, qs_ref, ds_ref, delta_ref, inv_ref, *rest):
    steps, span, cols = p_ref.shape
    total = 2 * kv_ref.shape[0]
    plan = Plan(plan_ref, total // stretch, stretch)
    if side == 0:
        acc_in, dq_ref, out_ref, acc_ref, dk_ref, dv_ref, dn_ref = rest
        acc_ref[...] = acc_in[...]
    else:
        acc_ref, out_ref, dk_ref, dv_ref, dn_ref = rest
        acc_ref[...] = jnp.zeros_like(acc_ref)
    dk_ref[...] = jnp.zeros_like(dk_ref)
    dv_ref[...] = jnp.zeros_like(dv_ref)
    for part in range(2):
        column = jnp.broadcast_to(inv_ref[part][:1], (HD, cols)).T
        dn_ref[part] = (ds_ref[part].astype(jnp.float32) * column).astype(jnp.bfloat16)

    for index in range(steps):
        part, row, chunk, valid = plan.step(side, index)
        here = pl.ds(row, span)
        weights = p_ref[index]
        grad_probs = dot(kv_ref[here, HD:], ds_ref[part], NT)
        moved = (grad_probs.reshape(span // 8, 8, cols) - delta_ref[part][None]) * inv_ref[part][None]
        grad_scores = (weights.astype(jnp.float32) * moved.reshape(span, cols)).astype(jnp.bfloat16)
        dv_ref[here, :] += dot(weights, dn_ref[part], NN)
        dk_ref[here, :] += dot(grad_scores, qs_ref[part], NN)
        acc_ref[part] += dot(kv_ref[here, :HD], grad_scores, TN)

    to = 0
    for x_step in range(NX):
        for z_step in range(NZ):
            slot = place_of(side, x_step, z_step)
            for half in range(2):
                here = pl.ds(plan.row(slot + half) - side * (total // 2), stretch)
                out_ref[to:to + stretch, :HD] = (dk_ref[here, :] * SCALE).astype(jnp.bfloat16)
                out_ref[to:to + stretch, HD:] = dv_ref[here, :].astype(jnp.bfloat16)
                to += stretch
    if side == 0:
        for part in range(2):
            out = (acc_ref[part].T * SCALE).astype(jnp.bfloat16)
            for head in range(QPG):
                dq_ref[part * stretch:(part + 1) * stretch, head * HD:(head + 1) * HD] = (
                    out[head * stretch:(head + 1) * stretch])


def pair(keys, values):
    return pl.pallas_call(
        pair_kernel,
        out_shape=jax.ShapeDtypeStruct((keys.shape[0], 2 * HD), jnp.bfloat16),
        in_specs=[HBM] * 2,
        out_specs=VMEM,
        scratch_shapes=[pltpu.SemaphoreType.DMA((2,))],
        compiler_params=pltpu.CompilerParams(vmem_limit_bytes=60 * MIB),
        name="pair",
    )(keys, values)


def by_heads(queries, grad_heads, kv):
    shape = jax.ShapeDtypeStruct((2, QPG * queries.shape[0] // 2, HD), jnp.bfloat16)
    return pl.pallas_call(
        heads_kernel,
        out_shape=(shape, shape, jax.ShapeDtypeStruct(kv.shape, kv.dtype)),
        in_specs=[HBM] * 2 + [VMEM],
        out_specs=[VMEM] * 3,
        scratch_shapes=[pltpu.SemaphoreType.DMA((2, 2, QPG))],
        compiler_params=pltpu.CompilerParams(vmem_limit_bytes=4 * MIB),
        name="by_heads",
    )(queries, grad_heads, kv)


def stage(ids, piece):
    slots = ids.shape[0]
    shape = jax.ShapeDtypeStruct
    return pl.pallas_call(
        stage_kernel,
        out_shape=(shape((2 * slots + 8,), jnp.int32), shape(piece.shape, piece.dtype)),
        in_specs=[SMEM, VMEM],
        out_specs=[SMEM, VMEM],
        scratch_shapes=[pltpu.SMEM((slots,), jnp.int32)],
        compiler_params=pltpu.CompilerParams(vmem_limit_bytes=4 * MIB),
        name="stage",
    )(ids, piece)


def added(*parts):
    total = parts[0].astype(jnp.float32)
    for part in parts[1:]:
        total = total + part.astype(jnp.float32)
    return total.astype(jnp.bfloat16)


def relay_kernel(front_in, back_in, ahead_in, behind_in, token_ref, front_ref, back_ref):
    quarter = front_in.shape[1] // 3
    for index in range(2 * quarter // MIX_SPAN):
        at = slice(index * MIX_SPAN, (index + 1) * MIX_SPAN)
        front_ref[:, at] = added(front_in[:, at], ahead_in[:, at])
        to = slice(quarter + at.start, quarter + at.stop)
        back_ref[:, to] = added(back_in[:, to], behind_in[:, to])


def relay(front, back, from_behind, from_ahead, token):
    shape = jax.ShapeDtypeStruct(front.shape, front.dtype)
    return pl.pallas_call(
        relay_kernel,
        out_shape=(shape, shape),
        in_specs=[VMEM] * 4 + [ANY],
        out_specs=[VMEM] * 2,
        input_output_aliases={0: 0, 1: 1},
        compiler_params=pltpu.CompilerParams(vmem_limit_bytes=8 * MIB),
        name="relay",
    )(front, back, from_behind, from_ahead, token)


def settle_kernel(own, from_behind, from_ahead, front, back, keep_ref, give_ref):
    quarter = front.shape[1] // 3
    rows = keep_ref.shape[0]
    for index in range(own.shape[1] // MIX_SPAN):
        at = slice(index * MIX_SPAN, (index + 1) * MIX_SPAN)
        less = slice(at.start - quarter, at.stop - quarter)
        which = at.start // quarter
        behind = from_behind[:, at] if which == 2 else front[:, at if which < 2 else less]
        before = from_ahead[:, at] if which == 0 else back[:, less]
        total = added(own[:, at], behind, before)
        keep_ref[:, at] = total[:rows]
        give_ref[:, at] = total[rows:]


def settle(own, from_behind, from_ahead, front, back):
    shape = jax.ShapeDtypeStruct((own.shape[0] // NH, own.shape[1]), own.dtype)
    return pl.pallas_call(
        settle_kernel,
        out_shape=(shape, shape),
        in_specs=[VMEM] * 5,
        out_specs=[VMEM] * 2,
        compiler_params=pltpu.CompilerParams(vmem_limit_bytes=8 * MIB),
        name="settle",
    )(own, from_behind, from_ahead, front, back)


def share_kernel(token_ref, near, *refs):
    others, terms = refs[:NX - 1], refs[NX - 1:]
    for index, term in enumerate(terms):
        at = slice(index * term.shape[0], (index + 1) * term.shape[0])
        term[...] = added(near[at, :], *[other[at, :] for other in others])


def share(token, near, *others):
    term = jax.ShapeDtypeStruct((near.shape[0] // NZ, near.shape[1]), near.dtype)
    return pl.pallas_call(
        share_kernel,
        out_shape=(term,) * NZ,
        in_specs=[ANY] + [VMEM] * (1 + len(others)),
        out_specs=[VMEM] * NZ,
        compiler_params=pltpu.CompilerParams(vmem_limit_bytes=8 * MIB),
        cost_estimate=pl.CostEstimate(flops=BWD_FLOPS, bytes_accessed=2 * 10**6, transcendentals=0),
        name="share",
    )(token, near, *others)


def finish_kernel(token_ref, *refs):
    *parts, k_ref, v_ref = refs
    total = added(*[part[...] for part in parts])
    k_ref[...] = total[:, :HD]
    v_ref[...] = total[:, HD:]


def finish(token, *parts):
    shape = jax.ShapeDtypeStruct((parts[0].shape[0], HD), parts[0].dtype)
    return pl.pallas_call(
        finish_kernel,
        out_shape=(shape, shape),
        in_specs=[ANY] + [VMEM] * len(parts),
        out_specs=[VMEM] * 2,
        compiler_params=pltpu.CompilerParams(vmem_limit_bytes=4 * MIB),
        name="finish",
    )(token, *parts)


def stack_kernel(token_ref, *refs):
    *parts, out_ref = refs
    rows = parts[0].shape[0]
    for index, part in enumerate(parts):
        out_ref[index * rows:(index + 1) * rows, :] = part[...]


def stack(token, *parts):
    rows, width = parts[0].shape
    return pl.pallas_call(
        stack_kernel,
        out_shape=jax.ShapeDtypeStruct((len(parts) * rows, width), parts[0].dtype),
        in_specs=[ANY] + [VMEM] * len(parts),
        out_specs=VMEM,
        compiler_params=pltpu.CompilerParams(vmem_limit_bytes=4 * MIB),
        name="stack",
    )(token, *parts)


def forward(side, plan, qs, pieces, *more):
    cols = qs.shape[1]
    stretch = cols // QPG
    tokens = 2 * stretch
    total = sum(piece.shape[0] for piece in pieces)
    span = CHUNK * stretch
    steps = total // span + 1
    b16, f32 = jnp.bfloat16, jnp.float32
    shape = jax.ShapeDtypeStruct
    weights, keys = shape((steps, span, cols), b16), shape((total, 2 * HD), b16)
    row, sums = (2, 8, cols), (2, HD, cols)
    scratch = [pltpu.VMEM((steps, span, cols), f32), pltpu.VMEM((stretch, cols), jnp.int32)]
    if side:
        width = more[1].shape[1]
        outs = (shape((tokens // NY, width), b16),) + (shape((tokens // NY, 3 * width // 4), b16),) * 4 + (
            weights, keys, shape(row, f32), shape(row, f32), shape(row, f32))
        scratch = [pltpu.VMEM(row, f32), pltpu.VMEM(row, f32), pltpu.VMEM(sums, f32)] + scratch + [
            pltpu.VMEM((tokens, QPG * HD), b16), pltpu.VMEM((tokens, QPG * HD), b16)]
    else:
        outs = (weights, keys, shape(row, f32), shape(row, f32), shape(sums, f32))
    return pl.pallas_call(
        functools.partial(far_kernel if side else near_kernel, stretch),
        out_shape=outs,
        in_specs=[SMEM] + [VMEM] * (1 + len(pieces) + len(more)),
        out_specs=[VMEM] * len(outs),
        scratch_shapes=scratch,
        compiler_params=pltpu.CompilerParams(vmem_limit_bytes=FWD_MIB * MIB),
        cost_estimate=pl.CostEstimate(flops=3 * 10**9, bytes_accessed=8 * 10**6, transcendentals=10**6),
        name="attention_forward_%d" % side,
    )(plan, qs, *pieces, *more)


def backward(side, plan, probs, kv, qs, ds, delta, inverse, *partial):
    total = 2 * kv.shape[0]
    steps, span, cols = probs.shape
    stretch = cols // QPG
    b16, f32 = jnp.bfloat16, jnp.float32
    shape = jax.ShapeDtypeStruct
    terms = shape((total // 2, 2 * HD), b16)
    sums = (2, HD, cols)
    scratch = [
        pltpu.VMEM((total // 2, HD), f32),
        pltpu.VMEM((total // 2, HD), f32),
        pltpu.VMEM((2, cols, HD), b16),
    ]
    return pl.pallas_call(
        functools.partial(bwd_kernel, stretch, side),
        out_shape=(shape(sums, f32) if side else shape((2 * stretch, QPG * HD), b16), terms),
        in_specs=[SMEM] + [VMEM] * (6 + len(partial)),
        out_specs=[VMEM] * 2,
        scratch_shapes=scratch if side else [pltpu.VMEM(sums, f32)] + scratch,
        compiler_params=pltpu.CompilerParams(vmem_limit_bytes=32 * MIB),
        cost_estimate=pl.CostEstimate(flops=BWD_FLOPS, bytes_accessed=8 * 10**6, transcendentals=0),
        name="attention_backward_%d" % side,
    )(plan, probs, kv, qs, ds, delta, inverse, *partial)


def ahead(block, axis, step):
    count = lax.axis_size(axis)
    return lax.ppermute(block, axis, [(i, (i + step) % count) for i in range(count)])


def behind(block, axis, step):
    count = lax.axis_size(axis)
    return lax.ppermute(block, axis, [((i + step) % count, i) for i in range(count)])


def across(block, axis, step):
    count = lax.axis_size(axis)
    return lax.ppermute(block, axis, [(i, i ^ step) for i in range(count)])


def total_of(parts):
    total = parts[0].astype(jnp.float32)
    for part in parts[1:]:
        total = total + part.astype(jnp.float32)
    return total.astype(jnp.bfloat16)


def on_device(queries, keys, values, stretch_of, out_weight, grad_heads):
    kv = pair(keys, values)
    qs, ds, same = by_heads(queries, grad_heads, kv)
    kv = stack(qs, same, *[across(kv, "zl", step) for step in range(1, NZ)])
    plan, same = stage(stretch_of, kv)
    near = [kv] + [behind(kv, "x", step) for step in range(1, NX)]
    far = [across(piece, "core", 1) for piece in [same] + near[1:]]
    near_probs, near_kv, *partial = forward(0, plan, qs, near)
    own, front, back, to_ahead, to_behind, far_probs, far_kv, delta, near_inv, far_inv = forward(
        1, plan, qs, far, ds, out_weight, *partial)
    from_behind, from_ahead = ahead(to_ahead, "y", 1), ahead(to_behind, "y", NY - 1)
    partial, give = backward(1, plan, far_probs, far_kv, qs, ds, delta, far_inv)
    q_grad, keep = backward(0, plan, near_probs, near_kv, qs, ds, delta, near_inv, partial)
    term = total_of([keep, across(give, "core", 1)])
    front, back = relay(front, back, from_behind, from_ahead, term)
    part = term.shape[0] // NX
    near, *others = [term[step * part:(step + 1) * part] for step in range(NX)]
    others = [ahead(other, "x", step + 1) for step, other in enumerate(others)]
    mixed, give = settle(
        own, from_behind, from_ahead, ahead(front, "y", 1), ahead(back, "y", NY - 1))
    terms = share(mixed, near, *others)
    mixed = total_of([mixed, across(give, "zh", 1)])
    k_grad, v_grad = finish(mixed, terms[0], *[across(terms[step], "zl", step) for step in range(1, NZ)])
    return mixed, q_grad, k_grad, v_grad


def solution(mesh):
    fine = Mesh(mesh.devices.reshape(NX, NZ, NC, NH, NY), CTX + TP)
    return jax.shard_map(
        on_device,
        mesh=fine,
        in_specs=(P(CTX, TP), P(CTX, TP), P(CTX, TP), P(), P(TP, None), P(CTX, TP)),
        out_specs=(P(CTX + TP, None), P(CTX, TP), P(CTX, TP), P(CTX, TP)),
        check_vma=False,
    )
```
